128 devices in a mesh: frame: 4 (over z_hi, core), row: 8 (over z_lo, x), col: 4 (over y).
Axes of the slice: x: 4, y: 4, z: 4 (z_hi: 2, z_lo: 2; z = z_hi * 2 + z_lo), core: 2. Of those that a mesh axis runs over, the one named last changes fastest.
Arguments:
- tokens_in: bfloat16 [16, 128, 64, 3072], P('frame', 'row', 'col'), may hold values from -4 to 4
- queries: bfloat16 [16, 128, 64, 1536], P('frame', 'row', 'col'), may hold values from -100 to 100
- key_rows: bfloat16 [16, 128, 64, 1536], P('frame', 'row', 'col'), may hold values from -6 to 6
- value_rows: bfloat16 [16, 128, 64, 1536], P('frame', 'row', 'col'), may hold values from -6 to 6
- out_weight: bfloat16 [1536, 3072], P(None, ('frame', 'row', 'col')), may hold values from -2.5 to 2.5
- row_valid: int32 [128], replicated, may hold values from 0 to 1, as said below
Outputs:
- layer_out: bfloat16 [16, 128, 64, 3072], P('frame', 'row', 'col')
The draws below stay inside these ranges and needn't reach their ends.
Inputs may be any that keep to these rules, and one draw needn't show every extreme that they name: row_valid is 1 on a leading run of rows and 0 on the rest; at least one row is 0 and at most 24 are.
All inputs are finite; a program needn't handle non-finite values.
Results may differ from the reference program's by a relative error of at most 0.014.
Values may be sent and summed in bfloat16 or wider, within the bound.
No kernel may reach another device: no remote copies, remote signals or barrier semaphores. Data moves between devices by JAX's collectives and lax.ppermute only.
A program may use at most 192 MiB of HBM per device.

```python
import jax
import jax.numpy as jnp
from jax import lax

D = 3072
H = 12
HS = 128
WF = 4
WR = 16
WC = 16
HD = 1536
NF = 16
NY = 128
NX = 64


def shared_field(key):
    field = jax.random.normal(key, (NF, NY, NX, H * HS), jnp.float32)
    return jnp.clip(field, -5.0, 5.0)


def draw_queries(key, part):
    key = jax.random.fold_in(key, 5)
    fresh = jax.random.normal(key, (NF, NY, NX, H * HS), jnp.float32)
    fresh = jnp.clip(fresh, -5.0, 5.0)
    return fresh.astype(jnp.bfloat16)


def draw_key_rows(key, part):
    shared = shared_field(key)
    return shared.astype(jnp.bfloat16)


def draw_row_valid(key, part):
    key = jax.random.fold_in(key, 7)
    padded = jax.random.randint(key, (), 1, 3 * WR // 2 + 1)
    row_order = jnp.arange(NY, dtype=jnp.int32)
    return (row_order < NY - padded).astype(jnp.int32)


def shard_levels(rng, shape, shards, low, largest):
    gain, own = 1.0, jax.random.fold_in(rng, 6)
    for axis_at, blocks in shards:
        draws = jnp.exp(jax.random.uniform(jax.random.fold_in(own, axis_at), (blocks,), jnp.float32, low / len(shards), largest / len(shards)))
        gain = gain * jnp.repeat(draws, shape[axis_at] // blocks).reshape([-1 if axis == axis_at else 1 for axis in range(len(shape))])
    return gain


def centred(rng, dims, deviation, limit, cuts=(), held_as=jnp.bfloat16):
    result = jax.random.normal(rng, dims, jnp.float32) * deviation
    if len(cuts) > 0:
        result = shard_levels(rng, dims, cuts, -0.22, 0.18) * result
    return jnp.clip(result, min=-limit, max=limit).astype(held_as)


def setup_inputs(seed: int = 0) -> dict:
    streams_of = jax.random.split(jax.random.key(seed), 7)
    return {
        "tokens_in": centred(streams_of[0], (NF, NY, NX, D), 0.3, 4.0, ((0, 4), (1, 8), (2, 4))),
        "queries": draw_queries(jax.random.fold_in(streams_of[6], 71), 0),
        "key_rows": draw_key_rows(jax.random.fold_in(streams_of[6], 71), 0),
        "value_rows": centred(streams_of[3], (NF, NY, NX, HD), 1.0, 6.0, ((0, 4), (1, 8), (2, 4))),
        "out_weight": centred(streams_of[4], (HD, D), (max(HD // 256, 1)) ** -0.5, 2.5, ((1, 128),)),
        "row_valid": draw_row_valid(jax.random.fold_in(streams_of[6], 71), 0),
    }


def attend_window(query_win, key_win, value_win, frame_ids, row_ids, col_ids, alive_mask):
    tokens_win = query_win.shape[0]
    head_count = query_win.shape[1] // HS
    query_heads = query_win.reshape(tokens_win, head_count, HS).astype(jnp.float32)
    key_heads = key_win.reshape(tokens_win, head_count, HS).astype(jnp.float32)
    value_heads = value_win.reshape(tokens_win, head_count, HS).astype(jnp.float32)
    scores = jnp.einsum("qhd,khd->hqk", query_heads, key_heads) * (HS ** -0.5)
    allowed = (frame_ids[:, None] == frame_ids[None, :]) & (row_ids[:, None] == row_ids[None, :])
    allowed = allowed & (col_ids[:, None] == col_ids[None, :])
    allowed = allowed & (alive_mask[:, None] > 0) & (alive_mask[None, :] > 0)
    scores = jnp.where(allowed[None], scores, -1e30)
    row_max = jnp.max(scores, axis=2, keepdims=True)
    exponent = jnp.exp(scores - row_max)
    row_total = jnp.sum(exponent, axis=2, keepdims=True)
    weights = (exponent / row_total).astype(jnp.bfloat16)
    mixed_heads = jnp.einsum("hqk,khd->qhd", weights.astype(jnp.float32), value_heads)
    mixed_heads = mixed_heads * alive_mask[:, None, None].astype(jnp.float32)
    return mixed_heads.reshape(tokens_win, head_count * HS).astype(jnp.bfloat16)


def to_windows(array):
    frames, rows_all, cols_all, channels = array.shape
    split = array.reshape(frames // WF, WF, rows_all // WR, WR, cols_all // WC, WC, channels)
    split = split.transpose(0, 2, 4, 1, 3, 5, 6)
    return split.reshape(-1, WF * WR * WC, channels)


def reference(tokens_in, queries, key_rows, value_rows, out_weight, row_valid):
    frames, rows_all, cols_all, feature_width = queries.shape
    shifts = (WF // 2, WR // 2, WC // 2)
    frame_place = (jnp.arange(frames) - WF // 2) % frames
    row_place = (jnp.arange(rows_all) - WR // 2) % rows_all
    col_place = (jnp.arange(cols_all) - WC // 2) % cols_all
    frame_ids = (frame_place + WF // 2) // WF
    row_ids = (row_place + WR // 2) // WR
    col_ids = (col_place + WC // 2) // WC
    alive_rows = row_valid[row_place]
    grid_shape = (frames, rows_all, cols_all)
    frame_grid = jnp.broadcast_to(frame_ids[:, None, None], grid_shape)[..., None]
    row_grid = jnp.broadcast_to(row_ids[None, :, None], grid_shape)[..., None]
    col_grid = jnp.broadcast_to(col_ids[None, None, :], grid_shape)[..., None]
    alive_grid = jnp.broadcast_to(alive_rows[None, :, None], grid_shape)[..., None]
    query_wins = to_windows(jnp.roll(queries, shifts, axis=(0, 1, 2)))
    key_wins = to_windows(jnp.roll(key_rows, shifts, axis=(0, 1, 2)))
    value_wins = to_windows(jnp.roll(value_rows, shifts, axis=(0, 1, 2)))
    bundle = (query_wins, key_wins, value_wins, to_windows(frame_grid)[..., 0], to_windows(row_grid)[..., 0],
              to_windows(col_grid)[..., 0], to_windows(alive_grid)[..., 0])
    attended = lax.map(lambda items: attend_window(*items), bundle)
    attended = attended.reshape(frames // WF, rows_all // WR, cols_all // WC, WF, WR, WC, feature_width)
    attended = attended.transpose(0, 3, 1, 4, 2, 5, 6).reshape(frames, rows_all, cols_all, feature_width)
    attended = jnp.roll(attended, tuple(-value for value in shifts), axis=(0, 1, 2))
    flat_rows = attended.reshape(-1, feature_width)
    projected = jnp.dot(flat_rows, out_weight, preferred_element_type=jnp.float32)
    summed = projected + tokens_in.reshape(-1, D).astype(jnp.float32)
    return summed.astype(jnp.bfloat16).reshape(frames, rows_all, cols_all, D)
```

```python
import functools
import math

import jax
import jax.numpy as jnp
from jax import lax
from jax.experimental import pallas as pl
from jax.experimental.pallas import tpu as pltpu
from jax.sharding import PartitionSpec as P

D = 3072
H = 12
HS = 128
HD = 1536
F, R, C = 4, 8, 4
AXES = ("frame", "row", "col")
GROUPS = ((0, 6), (6, 6))
BIG = 1e30
TILE = 384
VMEM = 56 * 1024 * 1024


def index(f, r, c):
    return ((f % F) * R + (r % R)) * C + (c % C)


def every():
    return [(f, r, c) for f in range(F) for r in range(R) for c in range(C)]


def window_pairs(half, dr, dc, back=False):
    pairs = []
    for f, r, c in every():
        step = 1 if (f + half) % 2 == 0 else -1
        here, there = index(f, r, c), index(f, r + step * dr, c + step * dc)
        pairs.append((there, here) if back else (here, there))
    return pairs


def frame_pairs(step):
    return [(index(f, r, c), index(f + step, r, c)) for f, r, c in every() if 0 <= f + step < F]


def core_pairs():
    return [(index(f, r, c), index(f ^ 1, r, c)) for f, r, c in every()]


def plane_pairs(dx, dy):
    pairs = []
    for f, r, c in every():
        zlo, x = divmod(r, 4)
        pairs.append((index(f, r, c), index(f, zlo * 4 + (x + dx) % 4, c + dy)))
    return pairs


def depth_pairs():
    pairs = []
    for f, r, c in every():
        zhi, core = divmod(f, 2)
        zlo, x = divmod(r, 4)
        z = (zhi * 2 + zlo + (1 if core == 0 else -1)) % 4
        pairs.append((index(f, r, c), index((z // 2) * 2 + core, (z % 2) * 4 + x, c)))
    return pairs


def send(value, pairs):
    return lax.ppermute(value, AXES, pairs)


MOVES = ((0, 0), (1, 0), (0, 1), (1, 1))


def pack_kernel(half, lane, width, sign_ref, q_ref, k_ref, v_ref, *rest):
    outs, sems = rest[:4], rest[4]
    s = sign_ref[0]
    copies = []
    for piece, (a, b) in enumerate(MOVES):
        i = s + a * (1 - 2 * s)
        j = s + b * (1 - 2 * s)
        for n, src in enumerate((q_ref, k_ref, v_ref)):
            for fr in range(2):
                copies.append(
                    pltpu.make_async_copy(
                        src.at[2 * half + fr, i, :, j, :, pl.ds(lane, width)],
                        outs[piece].at[n, fr],
                        sems.at[piece * 6 + n * 2 + fr],
                    )
                )
    for copy in copies:
        copy.start()
    for copy in copies:
        copy.wait()


def pack(half, first, heads, sign, q, k, v):
    width = heads * HS
    any_spec = pl.BlockSpec(memory_space=pl.ANY)
    shape = jax.ShapeDtypeStruct((3, 2, 8, 8, width), jnp.bfloat16)
    outs = pl.pallas_call(
        functools.partial(pack_kernel, half, first * HS, width),
        out_shape=[shape] * 4,
        in_specs=[pl.BlockSpec(memory_space=pltpu.SMEM)] + [any_spec] * 3,
        out_specs=[any_spec] * 4,
        scratch_shapes=[pltpu.SemaphoreType.DMA((24,))],
        cost_estimate=pl.CostEstimate(flops=0, bytes_accessed=24 * 128 * width * 2, transcendentals=0),
        name=f"pack_{half}_{first}",
    )(sign, q, k, v)
    return [o.reshape(3, 128, width) for o in outs]


def halo_kernel(*refs):
    srcs, out, sems = refs[:4], refs[4], refs[5]
    copies = []
    for piece, src in enumerate(srcs):
        for n in range(2):
            copies.append(pltpu.make_async_copy(src.at[1 + n], out.at[n, piece], sems.at[piece * 2 + n]))
    for copy in copies:
        copy.start()
    for copy in copies:
        copy.wait()


def halo_pack(pieces):
    width = pieces[0].shape[2]
    any_spec = pl.BlockSpec(memory_space=pl.ANY)
    return pl.pallas_call(
        halo_kernel,
        out_shape=jax.ShapeDtypeStruct((2, 4, 128, width), jnp.bfloat16),
        in_specs=[any_spec] * 4,
        out_specs=any_spec,
        scratch_shapes=[pltpu.SemaphoreType.DMA((8,))],
        cost_estimate=pl.CostEstimate(flops=0, bytes_accessed=16 * 128 * width * 2, transcendentals=0),
        name="halo_pack",
    )(*pieces)


def attend_kernel(p0, p1, p2, p3, halo, kf, qf, alive, o0, o1, o2, o3, kaug, vaug, qaug):
    pieces, outs = (p0, p1, p2, p3), (o0, o1, o2, o3)

    @pl.when(pl.program_id(0) == 0)
    def _():
        kaug[:, HS:] = kf[...]
        qaug[:, HS:] = qf[...]
        vaug[:, HS:] = jnp.ones((1024, HS), jnp.bfloat16)

    for n, piece in enumerate(pieces):
        rows = pl.ds(n * 128, 128)
        qaug[rows, :HS] = piece[0]
        kaug[rows, :HS] = piece[1]
        vaug[rows, :HS] = piece[2]
        rows = pl.ds(512 + n * 128, 128)
        kaug[rows, :HS] = halo[0, n]
        vaug[rows, :HS] = halo[1, n]
    scale = math.log2(math.e) / math.sqrt(HS)
    for part in range(2):
        rows = pl.ds(part * 256, 256)
        scores = lax.dot_general(
            qaug[rows, :], kaug[...], (((1,), (1,)), ((), ())), preferred_element_type=jnp.float32
        )
        top = jnp.max(scores, axis=1, keepdims=True)
        weights = jnp.exp2((scores - top) * scale).astype(jnp.bfloat16)
        mixed = jnp.dot(weights, vaug[...], preferred_element_type=jnp.float32)
        result = (mixed[:, :HS] / mixed[:, HS:] * alive[rows, :]).astype(jnp.bfloat16)
        outs[2 * part][...] = result[:128]
        outs[2 * part + 1][...] = result[128:]


def attend(pieces, halo, kf, qf, alive):
    width = pieces[0].shape[2]
    heads = width // HS
    out = jax.ShapeDtypeStruct((128, width), jnp.bfloat16)
    return pl.pallas_call(
        attend_kernel,
        grid=(heads,),
        out_shape=[out] * 4,
        in_specs=[pl.BlockSpec((3, 128, HS), lambda h: (0, 0, h))] * 4
        + [
            pl.BlockSpec((2, 4, 128, HS), lambda h: (0, 0, 0, h)),
            pl.BlockSpec((1024, HS), lambda h: (0, 0)),
            pl.BlockSpec((512, HS), lambda h: (0, 0)),
            pl.BlockSpec((512, HS), lambda h: (0, 0)),
        ],
        out_specs=[pl.BlockSpec((128, HS), lambda h: (0, h))] * 4,
        scratch_shapes=[
            pltpu.VMEM((1024, 2 * HS), jnp.bfloat16),
            pltpu.VMEM((1024, 2 * HS), jnp.bfloat16),
            pltpu.VMEM((512, 2 * HS), jnp.bfloat16),
        ],
        compiler_params=pltpu.CompilerParams(vmem_limit_bytes=VMEM),
        cost_estimate=pl.CostEstimate(
            flops=heads * 4 * 512 * 1024 * 256, bytes_accessed=heads * 20 * 128 * 256, transcendentals=heads * 512 * 1024
        ),
        name="attend",
    )(*pieces, halo, kf, qf, alive)


def project_kernel(groups, signs, places, *refs):
    count = 8 * len(groups)
    attended, w_ref, tokens, out, lhs = refs[:count], refs[count], refs[count + 1], refs[count + 2], refs[count + 3]

    @pl.when(pl.program_id(0) == 0)
    def _():
        for half in range(2):
            s = signs[half]
            for piece, (a, b) in enumerate(MOVES):
                i = s + a * (1 - 2 * s)
                j = s + b * (1 - 2 * s)
                for g, (first, heads) in enumerate(groups):
                    lanes = pl.ds(first * HS, heads * HS)
                    lhs[half * 4 + i * 2 + j, :, lanes] = attended[g * 8 + half * 4 + piece][...]

    total = lax.dot_general(
        lhs[...].reshape(1024, HD), w_ref[...], (((1,), (1,)), ((), ())), preferred_element_type=jnp.float32
    ).reshape(2, 2, 2, 2, 8, 8, TILE)
    for half in range(2):
        for i in range(2):
            block = jnp.concatenate([total[half, i, 0], total[half, i, 1]], axis=2)
            at = (slice(2 * half, 2 * half + 2), slice(8 * i, 8 * i + 8))
            out[at] = (block + tokens[at].astype(jnp.float32)).astype(jnp.bfloat16)


def project(groups, attended, signs, places, w, tokens):
    whole = [pl.BlockSpec((128, heads * HS), lambda t, s, p: (0, 0)) for _, heads in groups for _ in range(8)]
    grid_spec = pltpu.PrefetchScalarGridSpec(
        num_scalar_prefetch=2,
        grid=(D // TILE,),
        in_specs=whole
        + [
            pl.BlockSpec((TILE, HD), lambda t, s, p: (t, 0)),
            pl.BlockSpec((4, 16, 16, TILE), lambda t, s, p: (0, 0, 0, p[t])),
        ],
        out_specs=pl.BlockSpec((4, 16, 16, TILE), lambda t, s, p: (0, 0, 0, p[t])),
        scratch_shapes=[pltpu.VMEM((8, 128, HD), jnp.bfloat16)],
    )
    return pl.pallas_call(
        functools.partial(project_kernel, groups),
        grid_spec=grid_spec,
        out_shape=jax.ShapeDtypeStruct((4, 16, 16, D), jnp.bfloat16),
        compiler_params=pltpu.CompilerParams(vmem_limit_bytes=VMEM),
        cost_estimate=pl.CostEstimate(flops=2 * 1024 * HD * D, bytes_accessed=25 * 2**20, transcendentals=0),
        name="project",
    )(signs, places, *attended, w, tokens)


def ring_order(own, first, second, third, place):
    row = jnp.stack([third, second, first, own, third, second, first])
    return lax.dynamic_slice_in_dim(row, 3 - place, 4, axis=0).reshape((-1,) + own.shape[1:])


def gather_weight(out_weight):
    f, r, c = (lax.axis_index(a) for a in AXES)
    core, x, z = f % 2, r % 4, (f // 2) * 2 + r // 4
    mine = out_weight.T
    mine = ring_order(mine, *(send(mine, plane_pairs(0, d)) for d in (1, 2, 3)), c)
    mine = ring_order(mine, *(send(mine, plane_pairs(d, 0)) for d in (1, 2, 3)), x)
    chunks = [mine]
    for _ in range(3):
        chunks.append(send(chunks[-1], depth_pairs()))
    others = [send(chunk, core_pairs()) for chunk in chunks]
    places = []
    for k in (core, 1 - core):
        for n in range(4):
            at = (z + n * (2 * k - 1) + 4) % 4
            places.append(((at // 2) * 2 + k) * 2 + at % 2)
    return jnp.concatenate(chunks + others), jnp.stack(places).astype(jnp.int32)


def masks(half, sign, row_valid):
    f, r, c = (lax.axis_index(a) for a in AXES)
    valid = row_valid.reshape(16, 8)
    stay = 2 * r + sign
    moved = (stay + 2 * sign - 1 + 16) % 16
    pick = lambda at: lax.dynamic_index_in_dim(valid, at, 0, keepdims=False)
    live = jnp.stack([pick(stay), pick(moved)])
    xbit = jnp.array([0, 1, 0, 1], jnp.int32)
    ybit = jnp.array([0, 0, 1, 1], jnp.int32)
    live = jnp.concatenate([live, live])
    live = jnp.broadcast_to(live[:, None, :, None], (4, 2, 8, 8)).reshape(512, 1)
    row_split = jnp.where(sign == 0, r == 0, r == R - 1)
    col_split = jnp.where(sign == 0, c == 0, c == C - 1)
    apart = (row_split & (xbit[:, None] != xbit[None, :])) | (col_split & (ybit[:, None] != ybit[None, :]))
    missing = (f == 0) if half == 0 else (f == F - 1)
    lane = jnp.arange(HS, dtype=jnp.int32)[None, :]
    piece = (jnp.arange(512, dtype=jnp.int32) // 128)[:, None]
    dead = (lane == 4) & (live == 0)
    own = (lane == piece) | dead
    kf = jnp.concatenate([own, own | (lane == 5)]).astype(jnp.bfloat16)
    apart = jnp.pad(apart, ((0, 0), (0, HS - 4)))
    apart = jnp.broadcast_to(apart[:, None, :], (4, 128, HS)).reshape(512, HS)
    qf = jnp.where(apart | (lane == 4) | ((lane == 5) & missing), -BIG, 0.0).astype(jnp.bfloat16)
    alive = jnp.broadcast_to(live, (512, HS)).astype(jnp.float32)
    return kf, qf, alive


def local(tokens_in, queries, key_rows, value_rows, out_weight, row_valid):
    f = lax.axis_index("frame")
    signs = jnp.stack([f % 2, 1 - f % 2]).astype(jnp.int32)
    split = lambda a: a.reshape(4, 2, 8, 2, 8, HD)
    q, k, v = split(queries), split(key_rows), split(value_rows)
    weight, places = gather_weight(out_weight)
    features = [masks(half, signs[half], row_valid) for half in range(2)]
    attended = []
    for first, heads in GROUPS:
        windows = []
        for half in range(2):
            packed = pack(half, first, heads, signs[half : half + 1], q, k, v)
            windows.append(
                [packed[0]] + [send(packed[n], window_pairs(half, *MOVES[n])) for n in (1, 2, 3)]
            )
        kv = [halo_pack(pieces) for pieces in windows]
        halos = [send(kv[1], frame_pairs(1)), send(kv[0], frame_pairs(-1))]
        for half in range(2):
            mixed = attend(windows[half], halos[half], *features[half])
            attended += [mixed[0]] + [send(mixed[n], window_pairs(half, *MOVES[n], back=True)) for n in (1, 2, 3)]
    return project(GROUPS, attended, signs, places, weight, tokens_in)


def solution(mesh):
    return jax.shard_map(
        local,
        mesh=mesh,
        in_specs=(
            P("frame", "row", "col", None),
            P("frame", "row", "col", None),
            P("frame", "row", "col", None),
            P("frame", "row", "col", None),
            P(None, ("frame", "row", "col")),
            P(),
        ),
        out_specs=P("frame", "row", "col", None),
        check_vma=False,
    )
```

```python
import functools
import math

import jax
import jax.numpy as jnp
from jax import lax
from jax.experimental import pallas as pl
from jax.experimental.pallas import tpu as pltpu
from jax.sharding import PartitionSpec as P

D = 3072
H = 12
HS = 128
HD = 1536
F, R, C = 4, 8, 4
AXES = ("frame", "row", "col")
GROUPS = ((0, 6), (6, 6))
BIG = 1e30
TILE = 384
VMEM = 56 * 1024 * 1024


def index(f, r, c):
    return ((f % F) * R + (r % R)) * C + (c % C)


def every():
    return [(f, r, c) for f in range(F) for r in range(R) for c in range(C)]


def window_pairs(half, dr, dc, back=False):
    pairs = []
    for f, r, c in every():
        step = 1 if (f + half) % 2 == 0 else -1
        here, there = index(f, r, c), index(f, r + step * dr, c + step * dc)
        pairs.append((there, here) if back else (here, there))
    return pairs


def frame_pairs(step):
    return [(index(f, r, c), index(f + step, r, c)) for f, r, c in every() if 0 <= f + step < F]


def core_pairs():
    return [(index(f, r, c), index(f ^ 1, r, c)) for f, r, c in every()]


def plane_pairs(dx, dy):
    pairs = []
    for f, r, c in every():
        zlo, x = divmod(r, 4)
        pairs.append((index(f, r, c), index(f, zlo * 4 + (x + dx) % 4, c + dy)))
    return pairs


def depth_pairs():
    pairs = []
    for f, r, c in every():
        zhi, core = divmod(f, 2)
        zlo, x = divmod(r, 4)
        z = (zhi * 2 + zlo + (1 if core == 0 else -1)) % 4
        pairs.append((index(f, r, c), index((z // 2) * 2 + core, (z % 2) * 4 + x, c)))
    return pairs


def send(value, pairs):
    return lax.ppermute(value, AXES, pairs)


MOVES = ((0, 0), (1, 0), (0, 1), (1, 1))


def relay(moves, sems):
    inward = [pltpu.make_async_copy(src, held, sems.at[0, n]) for n, (src, held, _) in enumerate(moves)]
    outward = [pltpu.make_async_copy(held, dst, sems.at[1, n]) for n, (_, held, dst) in enumerate(moves)]
    for copy in inward:
        copy.start()
    for arrives, leaves in zip(inward, outward):
        arrives.wait()
        leaves.start()
    for copy in outward:
        copy.wait()


def pack_kernel(half, lane, width, sign_ref, q_ref, k_ref, v_ref, *rest):
    outs, held, sems = rest[:4], rest[4], rest[5]
    s = sign_ref[0]
    moves = []
    for piece in (1, 2, 3, 0):
        a, b = MOVES[piece]
        i = s + a * (1 - 2 * s)
        j = s + b * (1 - 2 * s)
        for n, src in enumerate((q_ref, k_ref, v_ref)):
            at = src.at[pl.ds(2 * half, 2), i, :, j, :, pl.ds(lane, width)]
            moves.append((at, held.at[piece, n], outs[piece].at[n]))
    relay(moves, sems)


def pack(half, first, heads, sign, q, k, v):
    width = heads * HS
    any_spec = pl.BlockSpec(memory_space=pl.ANY)
    shape = jax.ShapeDtypeStruct((3, 2, 8, 8, width), jnp.bfloat16)
    outs = pl.pallas_call(
        functools.partial(pack_kernel, half, first * HS, width),
        out_shape=[shape] * 4,
        in_specs=[pl.BlockSpec(memory_space=pltpu.SMEM)] + [any_spec] * 3,
        out_specs=[any_spec] * 4,
        scratch_shapes=[pltpu.VMEM((4, 3, 2, 8, 8, width), jnp.bfloat16), pltpu.SemaphoreType.DMA((2, 12))],
        compiler_params=pltpu.CompilerParams(vmem_limit_bytes=VMEM),
        cost_estimate=pl.CostEstimate(flops=0, bytes_accessed=24 * 128 * width * 2, transcendentals=0),
        name=f"pack_{half}_{first}",
    )(sign, q, k, v)
    return [o.reshape(3, 128, width) for o in outs]


def halo_kernel(*refs):
    srcs, out, held, sems = refs[:4], refs[4], refs[5], refs[6]
    moves = [(src.at[pl.ds(1, 2)], held.at[piece], out.at[piece]) for piece, src in enumerate(srcs)]
    relay(moves, sems)


def halo_pack(pieces):
    width = pieces[0].shape[2]
    any_spec = pl.BlockSpec(memory_space=pl.ANY)
    return pl.pallas_call(
        halo_kernel,
        out_shape=jax.ShapeDtypeStruct((4, 2, 128, width), jnp.bfloat16),
        in_specs=[any_spec] * 4,
        out_specs=any_spec,
        scratch_shapes=[pltpu.VMEM((4, 2, 128, width), jnp.bfloat16), pltpu.SemaphoreType.DMA((2, 4))],
        compiler_params=pltpu.CompilerParams(vmem_limit_bytes=VMEM),
        cost_estimate=pl.CostEstimate(flops=0, bytes_accessed=16 * 128 * width * 2, transcendentals=0),
        name="halo_pack",
    )(*pieces)


def attend_kernel(p0, p1, p2, p3, halo, kf, qf, alive, o0, o1, o2, o3, kaug, vaug, qaug):
    pieces, outs = (p0, p1, p2, p3), (o0, o1, o2, o3)

    @pl.when(pl.program_id(0) == 0)
    def _():
        kaug[:, HS:] = kf[...]
        qaug[:, HS:] = qf[...]
        vaug[:, HS:] = jnp.ones((1024, HS), jnp.bfloat16)

    for n, piece in enumerate(pieces):
        rows = pl.ds(n * 128, 128)
        qaug[rows, :HS] = piece[0]
        kaug[rows, :HS] = piece[1]
        vaug[rows, :HS] = piece[2]
        rows = pl.ds(512 + n * 128, 128)
        kaug[rows, :HS] = halo[n, 0]
        vaug[rows, :HS] = halo[n, 1]
    scale = math.log2(math.e) / math.sqrt(HS)
    for part in range(2):
        rows = pl.ds(part * 256, 256)
        scores = lax.dot_general(
            qaug[rows, :], kaug[...], (((1,), (1,)), ((), ())), preferred_element_type=jnp.float32
        )
        top = jnp.max(scores, axis=1, keepdims=True)
        weights = jnp.exp2((scores - top) * scale).astype(jnp.bfloat16)
        mixed = jnp.dot(weights, vaug[...], preferred_element_type=jnp.float32)
        result = (mixed[:, :HS] / mixed[:, HS:] * alive[rows, :]).astype(jnp.bfloat16)
        outs[2 * part][...] = result[:128]
        outs[2 * part + 1][...] = result[128:]


def attend(pieces, halo, kf, qf, alive):
    width = pieces[0].shape[2]
    heads = width // HS
    out = jax.ShapeDtypeStruct((128, width), jnp.bfloat16)
    return pl.pallas_call(
        attend_kernel,
        grid=(heads,),
        out_shape=[out] * 4,
        in_specs=[pl.BlockSpec((3, 128, HS), lambda h: (0, 0, h))] * 4
        + [
            pl.BlockSpec((4, 2, 128, HS), lambda h: (0, 0, 0, h)),
            pl.BlockSpec((1024, HS), lambda h: (0, 0)),
            pl.BlockSpec((512, HS), lambda h: (0, 0)),
            pl.BlockSpec((512, HS), lambda h: (0, 0)),
        ],
        out_specs=[pl.BlockSpec((128, HS), lambda h: (0, h))] * 4,
        scratch_shapes=[
            pltpu.VMEM((1024, 2 * HS), jnp.bfloat16),
            pltpu.VMEM((1024, 2 * HS), jnp.bfloat16),
            pltpu.VMEM((512, 2 * HS), jnp.bfloat16),
        ],
        compiler_params=pltpu.CompilerParams(vmem_limit_bytes=VMEM),
        cost_estimate=pl.CostEstimate(
            flops=heads * 4 * 512 * 1024 * 256, bytes_accessed=heads * 20 * 128 * 256, transcendentals=heads * 512 * 1024
        ),
        name="attend",
    )(*pieces, halo, kf, qf, alive)


def project_kernel(groups, signs, places, *refs):
    count = 8 * len(groups)
    attended, w_ref, tokens, out, lhs = refs[:count], refs[count], refs[count + 1], refs[count + 2], refs[count + 3]

    @pl.when(pl.program_id(0) == 0)
    def _():
        for half in range(2):
            s = signs[half]
            for piece, (a, b) in enumerate(MOVES):
                i = s + a * (1 - 2 * s)
                j = s + b * (1 - 2 * s)
                for g, (first, heads) in enumerate(groups):
                    lanes = pl.ds(first * HS, heads * HS)
                    lhs[half * 4 + i * 2 + j, :, lanes] = attended[g * 8 + half * 4 + piece][...]

    total = lax.dot_general(
        lhs[...].reshape(1024, HD), w_ref[...], (((1,), (1,)), ((), ())), preferred_element_type=jnp.float32
    ).reshape(2, 2, 2, 2, 8, 8, TILE)
    for half in range(2):
        for i in range(2):
            block = jnp.concatenate([total[half, i, 0], total[half, i, 1]], axis=2)
            at = (slice(2 * half, 2 * half + 2), slice(8 * i, 8 * i + 8))
            out[at] = (block + tokens[at].astype(jnp.float32)).astype(jnp.bfloat16)


def project(groups, attended, signs, places, w, tokens):
    whole = [pl.BlockSpec((128, heads * HS), lambda t, s, p: (0, 0)) for _, heads in groups for _ in range(8)]
    grid_spec = pltpu.PrefetchScalarGridSpec(
        num_scalar_prefetch=2,
        grid=(D // TILE,),
        in_specs=whole
        + [
            pl.BlockSpec((TILE, HD), lambda t, s, p: (t, 0)),
            pl.BlockSpec((4, 16, 16, TILE), lambda t, s, p: (0, 0, 0, p[t])),
        ],
        out_specs=pl.BlockSpec((4, 16, 16, TILE), lambda t, s, p: (0, 0, 0, p[t])),
        scratch_shapes=[pltpu.VMEM((8, 128, HD), jnp.bfloat16)],
    )
    return pl.pallas_call(
        functools.partial(project_kernel, groups),
        grid_spec=grid_spec,
        out_shape=jax.ShapeDtypeStruct((4, 16, 16, D), jnp.bfloat16),
        compiler_params=pltpu.CompilerParams(vmem_limit_bytes=VMEM),
        cost_estimate=pl.CostEstimate(flops=2 * 1024 * HD * D, bytes_accessed=25 * 2**20, transcendentals=0),
        name="project",
    )(signs, places, *attended, w, tokens)


def ring_order(own, first, second, third, place):
    row = jnp.stack([third, second, first, own, third, second, first])
    return lax.dynamic_slice_in_dim(row, 3 - place, 4, axis=0).reshape((-1,) + own.shape[1:])


def gather_weight(out_weight):
    f, r, c = (lax.axis_index(a) for a in AXES)
    core, x, z = f % 2, r % 4, (f // 2) * 2 + r // 4
    mine = out_weight.T
    mine = ring_order(mine, *(send(mine, plane_pairs(0, d)) for d in (1, 2, 3)), c)
    mine = ring_order(mine, *(send(mine, plane_pairs(d, 0)) for d in (1, 2, 3)), x)
    chunks = [mine]
    for _ in range(3):
        chunks.append(send(chunks[-1], depth_pairs()))
    others = [send(chunk, core_pairs()) for chunk in chunks]
    places = []
    for k in (core, 1 - core):
        for n in range(4):
            at = (z + n * (2 * k - 1) + 4) % 4
            places.append(((at // 2) * 2 + k) * 2 + at % 2)
    return jnp.concatenate(chunks + others), jnp.stack(places).astype(jnp.int32)


def masks(half, sign, row_valid):
    f, r, c = (lax.axis_index(a) for a in AXES)
    valid = row_valid.reshape(16, 8)
    stay = 2 * r + sign
    moved = (stay + 2 * sign - 1 + 16) % 16
    pick = lambda at: lax.dynamic_index_in_dim(valid, at, 0, keepdims=False)
    live = jnp.stack([pick(stay), pick(moved)])
    xbit = jnp.array([0, 1, 0, 1], jnp.int32)
    ybit = jnp.array([0, 0, 1, 1], jnp.int32)
    live = jnp.concatenate([live, live])
    live = jnp.broadcast_to(live[:, None, :, None], (4, 2, 8, 8)).reshape(512, 1)
    row_split = jnp.where(sign == 0, r == 0, r == R - 1)
    col_split = jnp.where(sign == 0, c == 0, c == C - 1)
    apart = (row_split & (xbit[:, None] != xbit[None, :])) | (col_split & (ybit[:, None] != ybit[None, :]))
    missing = (f == 0) if half == 0 else (f == F - 1)
    lane = jnp.arange(HS, dtype=jnp.int32)[None, :]
    piece = (jnp.arange(512, dtype=jnp.int32) // 128)[:, None]
    dead = (lane == 4) & (live == 0)
    own = (lane == piece) | dead
    kf = jnp.concatenate([own, own | (lane == 5)]).astype(jnp.bfloat16)
    apart = jnp.pad(apart, ((0, 0), (0, HS - 4)))
    apart = jnp.broadcast_to(apart[:, None, :], (4, 128, HS)).reshape(512, HS)
    qf = jnp.where(apart | (lane == 4) | ((lane == 5) & missing), -BIG, 0.0).astype(jnp.bfloat16)
    alive = jnp.broadcast_to(live, (512, HS)).astype(jnp.float32)
    return kf, qf, alive


def local(tokens_in, queries, key_rows, value_rows, out_weight, row_valid):
    f = lax.axis_index("frame")
    signs = jnp.stack([f % 2, 1 - f % 2]).astype(jnp.int32)
    split = lambda a: a.reshape(4, 2, 8, 2, 8, HD)
    q, k, v = split(queries), split(key_rows), split(value_rows)
    weight, places = gather_weight(out_weight)
    features = [masks(half, signs[half], row_valid) for half in range(2)]
    attended = []
    for first, heads in GROUPS:
        windows = []
        for half in range(2):
            packed = pack(half, first, heads, signs[half : half + 1], q, k, v)
            windows.append(
                [packed[0]] + [send(packed[n], window_pairs(half, *MOVES[n])) for n in (1, 2, 3)]
            )
        kv = [halo_pack(pieces) for pieces in windows]
        halos = [send(kv[1], frame_pairs(1)), send(kv[0], frame_pairs(-1))]
        for half in range(2):
            mixed = attend(windows[half], halos[half], *features[half])
            attended += [mixed[0]] + [send(mixed[n], window_pairs(half, *MOVES[n], back=True)) for n in (1, 2, 3)]
    return project(GROUPS, attended, signs, places, weight, tokens_in)


def solution(mesh):
    return jax.shard_map(
        local,
        mesh=mesh,
        in_specs=(
            P("frame", "row", "col", None),
            P("frame", "row", "col", None),
            P("frame", "row", "col", None),
            P("frame", "row", "col", None),
            P(None, ("frame", "row", "col")),
            P(),
        ),
        out_specs=P("frame", "row", "col", None),
        check_vma=False,
    )
```

```python
import functools
import math

import jax
import jax.numpy as jnp
from jax import lax
from jax.experimental import pallas as pl
from jax.experimental.pallas import tpu as pltpu
from jax.sharding import PartitionSpec as P

D = 3072
H = 12
HS = 128
HD = 1536
F, R, C = 4, 8, 4
AXES = ("frame", "row", "col")
STEP = 2
BIG = 1e30
TILE = 384
VMEM = 56 * 1024 * 1024


def index(f, r, c):
    return ((f % F) * R + (r % R)) * C + (c % C)


def every():
    return [(f, r, c) for f in range(F) for r in range(R) for c in range(C)]


def window_pairs(half, dr, dc, back=False):
    pairs = []
    for f, r, c in every():
        step = 1 if (f + half) % 2 == 0 else -1
        here, there = index(f, r, c), index(f, r + step * dr, c + step * dc)
        pairs.append((there, here) if back else (here, there))
    return pairs


def frame_pairs(step):
    return [(index(f, r, c), index(f + step, r, c)) for f, r, c in every() if 0 <= f + step < F]


def core_pairs():
    return [(index(f, r, c), index(f ^ 1, r, c)) for f, r, c in every()]


def depth_pairs():
    pairs = []
    for f, r, c in every():
        zhi, core = divmod(f, 2)
        zlo, x = divmod(r, 4)
        z = (zhi * 2 + zlo + (1 if core == 0 else -1)) % 4
        pairs.append((index(f, r, c), index((z // 2) * 2 + core, (z % 2) * 4 + x, c)))
    return pairs


def send(value, pairs):
    return lax.ppermute(value, AXES, pairs)


MOVES = ((0, 0), (1, 0), (0, 1), (1, 1))


def after(value, *first):
    return lax.optimization_barrier((value, *first))[0]


def sign_of(half, frame):
    return lax.rem(frame + half, 2)


def relay(moves, sems):
    inward = [pltpu.make_async_copy(src, held, sems.at[0, n]) for n, (src, held, _) in enumerate(moves)]
    outward = [pltpu.make_async_copy(held, dst, sems.at[1, n]) for n, (_, held, dst) in enumerate(moves)]
    for copy in inward:
        copy.start()
    for arrives, leaves in zip(inward, outward):
        arrives.wait()
        leaves.start()
    for copy in outward:
        copy.wait()


def pack_kernel(parts, meta, k_ref, v_ref, q_ref, *rest):
    outs, held, sems = rest[: len(parts)], rest[-2], rest[-1]
    moves = []
    for out, (half, piece, names) in zip(outs, parts):
        s = sign_of(half, meta[0])
        a, b = MOVES[piece]
        i = s + a * (1 - 2 * s)
        j = s + b * (1 - 2 * s)
        for n, name in enumerate(names):
            src = {"k": k_ref, "v": v_ref, "q": q_ref}[name]
            moves.append((src.at[pl.ds(2 * half, 2), i, :, j], held.at[len(moves)], out.at[n]))
    relay(moves, sems)


def pack(parts, meta, k, v, q):
    any_spec = pl.BlockSpec(memory_space=pl.ANY)
    count = sum(len(names) for _, _, names in parts)
    outs = pl.pallas_call(
        functools.partial(pack_kernel, parts),
        out_shape=[jax.ShapeDtypeStruct((len(names), 2, 8, 8, HD), jnp.bfloat16) for _, _, names in parts],
        in_specs=[pl.BlockSpec(memory_space=pltpu.SMEM)] + [any_spec] * 3,
        out_specs=[any_spec] * len(parts),
        scratch_shapes=[pltpu.VMEM((count, 2, 8, 8, HD), jnp.bfloat16), pltpu.SemaphoreType.DMA((2, count))],
        compiler_params=pltpu.CompilerParams(vmem_limit_bytes=VMEM),
        cost_estimate=pl.CostEstimate(flops=0, bytes_accessed=count * 2**20, transcendentals=0),
        name="pack",
    )(meta, k, v, q)
    return [o.reshape(-1, 128, HD) for o in outs]


def halo_kernel(*refs):
    srcs, out, held, sems = refs[:-3], refs[-3], refs[-2], refs[-1]
    relay([(src.at[pl.ds(0, 2)], held.at[n], out.at[n]) for n, src in enumerate(srcs)], sems)


def halo_pack(*pieces):
    any_spec = pl.BlockSpec(memory_space=pl.ANY)
    count = len(pieces)
    return pl.pallas_call(
        halo_kernel,
        out_shape=jax.ShapeDtypeStruct((count, 2, 128, HD), jnp.bfloat16),
        in_specs=[any_spec] * count,
        out_specs=any_spec,
        scratch_shapes=[pltpu.VMEM((count, 2, 128, HD), jnp.bfloat16), pltpu.SemaphoreType.DMA((2, count))],
        compiler_params=pltpu.CompilerParams(vmem_limit_bytes=VMEM),
        cost_estimate=pl.CostEstimate(flops=0, bytes_accessed=count * 3 * 2**19, transcendentals=0),
        name="halo_pack",
    )(*pieces)


def features(half, meta, kaug, qaug, alive):
    f, r, c, live_rows = (meta[n] for n in range(4))
    s = sign_of(half, f)
    stay = 2 * r + s
    moved = lax.rem(stay + 2 * s + 15, 16)
    row_split = r == s * (R - 1)
    col_split = c == s * (C - 1)
    missing = f == half * (F - 1)

    def places(count):
        token = lax.broadcasted_iota(jnp.int32, (count, HS), 0)
        lane = lax.broadcasted_iota(jnp.int32, (count, HS), 1)
        piece = (token // 128) % 4
        row = jnp.where(piece % 2 == 1, moved, stay) * 8 + (token // 8) % 8
        return token, lane, piece, row < live_rows

    token, lane, piece, live = places(1024)
    dead = (lane == 4) & jnp.logical_not(live)
    on = (lane == piece) | dead | ((lane == 5) & (token >= 512))
    kaug[:, HS:] = jnp.where(on, 1.0, 0.0).astype(jnp.bfloat16)
    token, lane, piece, live = places(512)
    rows_apart = (lane % 2 != piece % 2) & row_split
    cols_apart = (lane // 2 != piece // 2) & col_split
    off = ((lane < 4) & (rows_apart | cols_apart)) | (lane == 4) | ((lane == 5) & missing)
    qaug[:, HS:] = jnp.where(off, -BIG, 0.0).astype(jnp.bfloat16)
    alive[...] = jnp.where(live, 1.0, 0.0)


def attend_kernel(half, meta, skv, sq, x, y, dkv, dq, h0, hxy, hd, o0, o1, o2, o3, kaug, vaug, qaug, alive):
    outs = (o0, o1, o2, o3)

    @pl.when(pl.program_id(0) == 0)
    def _():
        features(half, meta, kaug.at[0], qaug.at[0], alive)
        for n in range(1, STEP):
            kaug[n, :, HS:] = kaug[0, :, HS:]
            qaug[n, :, HS:] = qaug[0, :, HS:]
        vaug[:, :, HS:] = jnp.ones((STEP, 1024, HS), jnp.bfloat16)

    keys = (skv, x, y, dkv, h0, hxy.at[0], hxy.at[1], hd)
    asks = (sq.at[0], x.at[2], y.at[2], dq.at[0])
    for h in range(STEP):
        lanes = pl.ds(h * HS, HS)
        for n, ref in enumerate(keys):
            kaug[h, pl.ds(n * 128, 128), :HS] = ref[0, :, lanes]
            vaug[h, pl.ds(n * 128, 128), :HS] = ref[1, :, lanes]
        for n, ref in enumerate(asks):
            qaug[h, pl.ds(n * 128, 128), :HS] = ref[:, lanes]
    scale = math.log2(math.e) / math.sqrt(HS)

    def score(at):
        h, part = divmod(at, 2)
        return lax.dot_general(
            qaug[h, pl.ds(part * 256, 256), :], kaug[h], (((1,), (1,)), ((), ())), preferred_element_type=jnp.float32
        )

    scores = score(0)
    for at in range(2 * STEP):
        later = score(at + 1) if at + 1 < 2 * STEP else None
        h, part = divmod(at, 2)
        lanes = pl.ds(h * HS, HS)
        top = jnp.max(scores, axis=1, keepdims=True)
        weights = jnp.exp2((scores - top) * scale).astype(jnp.bfloat16)
        mixed = jnp.dot(weights, vaug[h], preferred_element_type=jnp.float32)
        result = (mixed[:, :HS] / mixed[:, HS:] * alive[pl.ds(part * 256, 256), :]).astype(jnp.bfloat16)
        outs[2 * part][:, lanes] = result[:128]
        outs[2 * part + 1][:, lanes] = result[128:]
        scores = later


def attend(half, meta, *pieces):
    width = STEP * HS

    def spec(piece):
        lead = piece.shape[:-1]
        return pl.BlockSpec((*lead, width), lambda h: (0,) * len(lead) + (h,))

    return pl.pallas_call(
        functools.partial(attend_kernel, half),
        grid=(H // STEP,),
        out_shape=[jax.ShapeDtypeStruct((128, HD), jnp.bfloat16)] * 4,
        in_specs=[pl.BlockSpec(memory_space=pltpu.SMEM)] + [spec(piece) for piece in pieces],
        out_specs=[pl.BlockSpec((128, width), lambda h: (0, h))] * 4,
        scratch_shapes=[
            pltpu.VMEM((STEP, 1024, 2 * HS), jnp.bfloat16),
            pltpu.VMEM((STEP, 1024, 2 * HS), jnp.bfloat16),
            pltpu.VMEM((STEP, 512, 2 * HS), jnp.bfloat16),
            pltpu.VMEM((512, HS), jnp.float32),
        ],
        compiler_params=pltpu.CompilerParams(vmem_limit_bytes=VMEM),
        cost_estimate=pl.CostEstimate(flops=H * 4 * 512 * 1024 * 256, bytes_accessed=10 * 2**20, transcendentals=H * 2**19),
        name="attend",
    )(meta, *pieces)


def project_kernel(meta, places, *refs):
    attended, (c0, c1, c2, c3, near, far), (tokens, out, lhs, held, sems) = refs[:8], refs[8:14], refs[14:]
    chunks = (c0, c1, c2, c3, near.at[0], near.at[1], near.at[2], far)
    step = pl.program_id(0)

    def fetch(n):
        return pltpu.make_async_copy(chunks[n], held.at[n % 2], sems.at[n % 2])

    @pl.when(step == 0)
    def _():
        fetch(0).start()
        for half in range(2):
            s = sign_of(half, meta[0])
            for piece, (a, b) in enumerate(MOVES):
                i = s + a * (1 - 2 * s)
                j = s + b * (1 - 2 * s)
                lhs[half * 4 + i * 2 + j] = attended[half * 4 + piece][...]

    for n in range(8):

        @pl.when(step == n)
        def _():
            fetch(n).wait()
            if n < 7:
                fetch(n + 1).start()

    total = lax.dot_general(
        lhs[...].reshape(1024, HD), held[lax.rem(step, 2)], (((1,), (1,)), ((), ())), preferred_element_type=jnp.float32
    ).reshape(2, 2, 2, 2, 8, 8, TILE)
    for half in range(2):
        for i in range(2):
            block = jnp.concatenate([total[half, i, 0], total[half, i, 1]], axis=2)
            at = (slice(2 * half, 2 * half + 2), slice(8 * i, 8 * i + 8))
            out[at] = (block + tokens[at].astype(jnp.float32)).astype(jnp.bfloat16)


def project(attended, meta, places, chunks, tokens):
    grid_spec = pltpu.PrefetchScalarGridSpec(
        num_scalar_prefetch=2,
        grid=(D // TILE,),
        in_specs=[pl.BlockSpec((128, HD), lambda t, m, p: (0, 0))] * 8
        + [pl.BlockSpec(memory_space=pl.ANY)] * 6
        + [pl.BlockSpec((4, 16, 16, TILE), lambda t, m, p: (0, 0, 0, p[t]))],
        out_specs=pl.BlockSpec((4, 16, 16, TILE), lambda t, m, p: (0, 0, 0, p[t])),
        scratch_shapes=[
            pltpu.VMEM((8, 128, HD), jnp.bfloat16),
            pltpu.VMEM((2, TILE, HD), jnp.bfloat16),
            pltpu.SemaphoreType.DMA((2,)),
        ],
    )
    return pl.pallas_call(
        project_kernel,
        grid_spec=grid_spec,
        out_shape=jax.ShapeDtypeStruct((4, 16, 16, D), jnp.bfloat16),
        compiler_params=pltpu.CompilerParams(vmem_limit_bytes=VMEM),
        cost_estimate=pl.CostEstimate(flops=2 * 1024 * HD * D, bytes_accessed=25 * 2**20, transcendentals=0),
        name="project",
    )(meta, places, *attended, *chunks, tokens)


def plane_groups():
    return [[index(f, zlo * 4 + x, c) for x in range(4) for c in range(C)] for f in range(F) for zlo in range(2)]


def weight_places(f, r):
    core, z = f % 2, (f // 2) * 2 + r // 4
    places = []
    for k in (core, 1 - core):
        for n in range(4):
            at = (z + n * (2 * k - 1) + 4) % 4
            places.append(((at // 2) * 2 + k) * 2 + at % 2)
    return jnp.stack(places).astype(jnp.int32)


def local(tokens_in, queries, key_rows, value_rows, out_weight, row_valid):
    f, r, c = (lax.axis_index(a) for a in AXES)
    meta = jnp.stack([f, r, c, jnp.sum(row_valid)]).astype(jnp.int32)
    split = lambda a: a.reshape(4, 2, 8, 2, 8, HD)
    arrays = (meta, split(key_rows), split(value_rows), split(queries))
    chunk = lax.all_gather(out_weight.T, AXES, axis=0, tiled=True, axis_index_groups=plane_groups())

    row, col, both = MOVES[1:]
    go = lambda value, half, move: send(value, window_pairs(half, *move))
    skv0, skv1, x0, y0 = pack(((0, 0, "kv"), (1, 0, "kv"), (0, 1, "kvq"), (0, 2, "kvq")), *arrays)
    up0, down0 = send(skv1, frame_pairs(1)), send(skv0, frame_pairs(-1))
    x0, y0 = go(x0, 0, row), go(y0, 0, col)
    x1, y1, dkv0, dkv1, dq0, dq1, sq0, sq1 = pack(
        ((1, 1, "kvq"), (1, 2, "kvq"), (0, 3, "kv"), (1, 3, "kv"), (0, 3, "q"), (1, 3, "q"), (0, 0, "q"), (1, 0, "q")), *arrays
    )
    x1, y1 = go(after(x1, up0), 1, row), go(after(y1, down0), 1, col)
    down1 = send(halo_pack(x0, y0), frame_pairs(-1))
    dkv0, dkv1 = go(after(dkv0, x1), 0, both), go(after(dkv1, y1), 1, both)
    up1 = send(halo_pack(x1, y1), frame_pairs(1))
    dq0, dq1 = go(after(dq0, dkv0), 0, both), go(after(dq1, dkv1), 1, both)
    down2, up2 = send(dkv0, frame_pairs(-1)), send(dkv1, frame_pairs(1))

    ring = [after(chunk, up2)]
    for _ in range(3):
        ring.append(send(ring[-1], depth_pairs()))
    near = send(jnp.stack(ring[:3]), core_pairs())
    far = send(ring[3], core_pairs())

    mixed1 = attend(1, meta, skv1, sq1, x1, y1, dkv1, dq1, down0, down1, down2)
    mixed0 = attend(0, meta, skv0, sq0, x0, y0, dkv0, dq0, up0, up1, up2)
    attended = []
    for half, mixed in enumerate((mixed0, mixed1)):
        attended += [mixed[0]] + [send(mixed[n], window_pairs(half, *MOVES[n], back=True)) for n in (1, 2, 3)]
    return project(attended, meta, weight_places(f, r), (*ring, near, far), tokens_in)


def solution(mesh):
    return jax.shard_map(
        local,
        mesh=mesh,
        in_specs=(
            P("frame", "row", "col", None),
            P("frame", "row", "col", None),
            P("frame", "row", "col", None),
            P("frame", "row", "col", None),
            P(None, ("frame", "row", "col")),
            P(),
        ),
        out_specs=P("frame", "row", "col", None),
        check_vma=False,
    )
```

```python
import functools
import math

import jax
import jax.numpy as jnp
from jax import lax
from jax.experimental import pallas as pl
from jax.experimental.pallas import tpu as pltpu
from jax.sharding import PartitionSpec as P

D = 3072
H = 12
HS = 128
HD = 1536
F, R, C = 4, 8, 4
AXES = ("frame", "row", "col")
STEP = 2
BIG = 1e30
TILE = 384
VMEM = 56 * 1024 * 1024


def index(f, r, c):
    return ((f % F) * R + (r % R)) * C + (c % C)


def every():
    return [(f, r, c) for f in range(F) for r in range(R) for c in range(C)]


def window_pairs(half, dr, dc, back=False):
    pairs = []
    for f, r, c in every():
        step = 1 if (f + half) % 2 == 0 else -1
        here, there = index(f, r, c), index(f, r + step * dr, c + step * dc)
        pairs.append((there, here) if back else (here, there))
    return pairs


def frame_pairs(step):
    return [(index(f, r, c), index(f + step, r, c)) for f, r, c in every() if 0 <= f + step < F]


def core_pairs():
    return [(index(f, r, c), index(f ^ 1, r, c)) for f, r, c in every()]


def plane_pairs(dx, dy):
    pairs = []
    for f, r, c in every():
        zlo, x = divmod(r, 4)
        pairs.append((index(f, r, c), index(f, zlo * 4 + (x + dx) % 4, c + dy)))
    return pairs


def depth_pairs():
    pairs = []
    for f, r, c in every():
        zhi, core = divmod(f, 2)
        zlo, x = divmod(r, 4)
        z = (zhi * 2 + zlo + (1 if core == 0 else -1)) % 4
        pairs.append((index(f, r, c), index((z // 2) * 2 + core, (z % 2) * 4 + x, c)))
    return pairs


def send(value, pairs):
    return lax.ppermute(value, AXES, pairs)


MOVES = ((0, 0), (1, 0), (0, 1), (1, 1))


def sign_of(half, frame):
    return lax.rem(frame + half, 2)


def relay(moves, sems):
    inward = [pltpu.make_async_copy(src, held, sems.at[0, n]) for n, (src, held, _) in enumerate(moves)]
    outward = [pltpu.make_async_copy(held, dst, sems.at[1, n]) for n, (_, held, dst) in enumerate(moves)]
    for copy in inward:
        copy.start()
    for arrives, leaves in zip(inward, outward):
        arrives.wait()
        leaves.start()
    for copy in outward:
        copy.wait()


def pack_kernel(parts, meta, k_ref, v_ref, q_ref, *rest):
    outs, held, sems = rest[: len(parts)], rest[-2], rest[-1]
    moves = []
    for out, (half, piece, names) in zip(outs, parts):
        s = sign_of(half, meta[0])
        a, b = MOVES[piece]
        i = s + a * (1 - 2 * s)
        j = s + b * (1 - 2 * s)
        for n, name in enumerate(names):
            src = {"k": k_ref, "v": v_ref, "q": q_ref}[name]
            moves.append((src.at[pl.ds(2 * half, 2), i, :, j], held.at[len(moves)], out.at[n]))
    relay(moves, sems)


def pack(parts, meta, k, v, q):
    any_spec = pl.BlockSpec(memory_space=pl.ANY)
    count = sum(len(names) for _, _, names in parts)
    outs = pl.pallas_call(
        functools.partial(pack_kernel, parts),
        out_shape=[jax.ShapeDtypeStruct((len(names), 2, 8, 8, HD), jnp.bfloat16) for _, _, names in parts],
        in_specs=[pl.BlockSpec(memory_space=pltpu.SMEM)] + [any_spec] * 3,
        out_specs=[any_spec] * len(parts),
        scratch_shapes=[pltpu.VMEM((count, 2, 8, 8, HD), jnp.bfloat16), pltpu.SemaphoreType.DMA((2, count))],
        compiler_params=pltpu.CompilerParams(vmem_limit_bytes=VMEM),
        cost_estimate=pl.CostEstimate(flops=0, bytes_accessed=count * 2**20, transcendentals=0),
        name="pack",
    )(meta, k, v, q)
    return [o.reshape(-1, 128, HD) for o in outs]


def halo_kernel(*refs):
    srcs, out, held, sems = refs[:-3], refs[-3], refs[-2], refs[-1]
    relay([(src.at[pl.ds(0, 2)], held.at[n], out.at[n]) for n, src in enumerate(srcs)], sems)


def halo_pack(*pieces):
    any_spec = pl.BlockSpec(memory_space=pl.ANY)
    count = len(pieces)
    return pl.pallas_call(
        halo_kernel,
        out_shape=jax.ShapeDtypeStruct((count, 2, 128, HD), jnp.bfloat16),
        in_specs=[any_spec] * count,
        out_specs=any_spec,
        scratch_shapes=[pltpu.VMEM((count, 2, 128, HD), jnp.bfloat16), pltpu.SemaphoreType.DMA((2, count))],
        compiler_params=pltpu.CompilerParams(vmem_limit_bytes=VMEM),
        cost_estimate=pl.CostEstimate(flops=0, bytes_accessed=count * 3 * 2**19, transcendentals=0),
        name="halo_pack",
    )(*pieces)


def features(half, meta, kaug, qaug, alive):
    f, r, c, live_rows = (meta[n] for n in range(4))
    s = sign_of(half, f)
    stay = 2 * r + s
    moved = lax.rem(stay + 2 * s + 15, 16)
    row_split = r == s * (R - 1)
    col_split = c == s * (C - 1)
    missing = f == half * (F - 1)

    def places(count):
        token = lax.broadcasted_iota(jnp.int32, (count, HS), 0)
        lane = lax.broadcasted_iota(jnp.int32, (count, HS), 1)
        piece = (token // 128) % 4
        row = jnp.where(piece % 2 == 1, moved, stay) * 8 + (token // 8) % 8
        return token, lane, piece, row < live_rows

    token, lane, piece, live = places(1024)
    dead = (lane == 4) & jnp.logical_not(live)
    on = (lane == piece) | dead | ((lane == 5) & (token >= 512))
    kaug[:, HS:] = jnp.where(on, 1.0, 0.0).astype(jnp.bfloat16)
    token, lane, piece, live = places(512)
    rows_apart = (lane % 2 != piece % 2) & row_split
    cols_apart = (lane // 2 != piece // 2) & col_split
    off = ((lane < 4) & (rows_apart | cols_apart)) | (lane == 4) | ((lane == 5) & missing)
    qaug[:, HS:] = jnp.where(off, -BIG, 0.0).astype(jnp.bfloat16)
    alive[...] = jnp.where(live, 1.0, 0.0)


def attend_kernel(half, meta, skv, sq, x, y, dkv, dq, h0, hxy, hd, o0, o1, o2, o3, kaug, vaug, qaug, alive):
    outs = (o0, o1, o2, o3)

    @pl.when(pl.program_id(0) == 0)
    def _():
        features(half, meta, kaug.at[0], qaug.at[0], alive)
        for n in range(1, STEP):
            kaug[n, :, HS:] = kaug[0, :, HS:]
            qaug[n, :, HS:] = qaug[0, :, HS:]
        vaug[:, :, HS:] = jnp.ones((STEP, 1024, HS), jnp.bfloat16)

    keys = (skv, x, y, dkv, h0, hxy.at[0], hxy.at[1], hd)
    asks = (sq.at[0], x.at[2], y.at[2], dq.at[0])
    for h in range(STEP):
        lanes = pl.ds(h * HS, HS)
        for n, ref in enumerate(keys):
            kaug[h, pl.ds(n * 128, 128), :HS] = ref[0, :, lanes]
            vaug[h, pl.ds(n * 128, 128), :HS] = ref[1, :, lanes]
        for n, ref in enumerate(asks):
            qaug[h, pl.ds(n * 128, 128), :HS] = ref[:, lanes]
    scale = math.log2(math.e) / math.sqrt(HS)

    def score(at):
        h, part = divmod(at, 2)
        return lax.dot_general(
            qaug[h, pl.ds(part * 256, 256), :], kaug[h], (((1,), (1,)), ((), ())), preferred_element_type=jnp.float32
        )

    scores = score(0)
    for at in range(2 * STEP):
        later = score(at + 1) if at + 1 < 2 * STEP else None
        h, part = divmod(at, 2)
        lanes = pl.ds(h * HS, HS)
        top = jnp.max(scores, axis=1, keepdims=True)
        weights = jnp.exp2((scores - top) * scale).astype(jnp.bfloat16)
        mixed = jnp.dot(weights, vaug[h], preferred_element_type=jnp.float32)
        result = (mixed[:, :HS] / mixed[:, HS:] * alive[pl.ds(part * 256, 256), :]).astype(jnp.bfloat16)
        outs[2 * part][:, lanes] = result[:128]
        outs[2 * part + 1][:, lanes] = result[128:]
        scores = later


def attend(half, meta, *pieces):
    width = STEP * HS

    def spec(piece):
        lead = piece.shape[:-1]
        return pl.BlockSpec((*lead, width), lambda h: (0,) * len(lead) + (h,))

    return pl.pallas_call(
        functools.partial(attend_kernel, half),
        grid=(H // STEP,),
        out_shape=[jax.ShapeDtypeStruct((128, HD), jnp.bfloat16)] * 4,
        in_specs=[pl.BlockSpec(memory_space=pltpu.SMEM)] + [spec(piece) for piece in pieces],
        out_specs=[pl.BlockSpec((128, width), lambda h: (0, h))] * 4,
        scratch_shapes=[
            pltpu.VMEM((STEP, 1024, 2 * HS), jnp.bfloat16),
            pltpu.VMEM((STEP, 1024, 2 * HS), jnp.bfloat16),
            pltpu.VMEM((STEP, 512, 2 * HS), jnp.bfloat16),
            pltpu.VMEM((512, HS), jnp.float32),
        ],
        compiler_params=pltpu.CompilerParams(vmem_limit_bytes=VMEM),
        cost_estimate=pl.CostEstimate(flops=H * 4 * 512 * 1024 * 256, bytes_accessed=10 * 2**20, transcendentals=H * 2**19),
        name="attend",
    )(meta, *pieces)


def project_kernel(first, shapes, meta, places, *refs):
    count = len(shapes)
    attended, sources, (tokens, *rest) = refs[:8], refs[8 : 8 + count], refs[8 + count :]
    out, lhs, held, sems = rest[-4:]
    chunks = [ref.at[n] if lead else ref for ref, lead in zip(sources, shapes) for n in range(lead or 1)]
    step = pl.program_id(0)

    def fetch(n):
        return pltpu.make_async_copy(chunks[n], held.at[n % 2], sems.at[n % 2])

    @pl.when(step == 0)
    def _():
        fetch(0).start()
        for half in range(2):
            s = sign_of(half, meta[0])
            for piece, (a, b) in enumerate(MOVES):
                i = s + a * (1 - 2 * s)
                j = s + b * (1 - 2 * s)
                lhs[half * 4 + i * 2 + j] = attended[half * 4 + piece][...]

    for n in range(len(chunks)):

        @pl.when(step == n)
        def _():
            fetch(n).wait()
            if n + 1 < len(chunks):
                fetch(n + 1).start()

    total = lax.dot_general(
        lhs[...].reshape(1024, HD), held[lax.rem(step, 2)], (((1,), (1,)), ((), ())), preferred_element_type=jnp.float32
    ).reshape(2, 2, 2, 2, 8, 8, TILE)
    for half in range(2):
        for i in range(2):
            block = jnp.concatenate([total[half, i, 0], total[half, i, 1]], axis=2)
            at = (slice(2 * half, 2 * half + 2), slice(8 * i, 8 * i + 8))
            out[at] = (block + tokens[at].astype(jnp.float32)).astype(jnp.bfloat16)


def project(attended, meta, places, chunks, tokens, partial=None):
    shapes = tuple(chunk.shape[0] if chunk.ndim == 3 else 0 for chunk in chunks)
    steps = sum(max(lead, 1) for lead in shapes)
    extra = [] if partial is None else [partial]
    any_spec = pl.BlockSpec(memory_space=pl.ANY)
    block = pl.BlockSpec((4, 16, 16, TILE), lambda t, m, p: (0, 0, 0, p[t]))
    grid_spec = pltpu.PrefetchScalarGridSpec(
        num_scalar_prefetch=2,
        grid=(steps,),
        in_specs=[pl.BlockSpec((128, HD), lambda t, m, p: (0, 0))] * 8
        + [any_spec] * len(chunks)
        + [block]
        + [any_spec] * len(extra),
        out_specs=block,
        scratch_shapes=[
            pltpu.VMEM((8, 128, HD), jnp.bfloat16),
            pltpu.VMEM((2, TILE, HD), jnp.bfloat16),
            pltpu.SemaphoreType.DMA((2,)),
        ],
    )
    return pl.pallas_call(
        functools.partial(project_kernel, partial is None, shapes),
        grid_spec=grid_spec,
        out_shape=jax.ShapeDtypeStruct((4, 16, 16, D), jnp.bfloat16),
        input_output_aliases={} if partial is None else {11 + len(chunks): 0},
        compiler_params=pltpu.CompilerParams(vmem_limit_bytes=VMEM),
        cost_estimate=pl.CostEstimate(flops=2 * 1024 * HD * TILE * steps, bytes_accessed=3 * 2**20 * (steps + 1), transcendentals=0),
        name="project",
    )(meta, places, *attended, *chunks, tokens, *extra)


def ring_order(own, first, second, third, place):
    row = jnp.stack([third, second, first, own, third, second, first])
    return lax.dynamic_slice_in_dim(row, 3 - place, 4, axis=0).reshape((-1,) + own.shape[1:])


def weight_places(f, r):
    core, z = f & 1, (f >> 1) * 2 + (r >> 2)
    places = []
    for k in (core, 1 - core):
        at = [(z + n * (2 * k - 1) + 4) & 3 for n in range(4)]
        places.append([((a >> 1) * 2 + k) * 2 + (a & 1) for a in at])
    (a0, a1, a2, a3), (b0, b1, b2, b3) = places
    return jnp.stack([a0, a1, a2, b0, b1, a3, b2, b3]).astype(jnp.int32)


def together(*values):
    return lax.optimization_barrier(values)


def local(tokens_in, queries, key_rows, value_rows, out_weight, row_valid):
    f, r, c = (lax.axis_index(a) for a in AXES)
    meta = jnp.stack([f, r, c, jnp.sum(row_valid)]).astype(jnp.int32)
    places = weight_places(f, r)
    split = lambda a: a.reshape(4, 2, 8, 2, 8, HD)
    arrays = (meta, split(key_rows), split(value_rows), split(queries))
    shard = out_weight.T
    shards = [send(shard, plane_pairs(0, d)) for d in (1, 2, 3)]

    row, col, both = MOVES[1:]
    go = lambda value, half, move: send(value, window_pairs(half, *move))
    up = lambda value: send(value, frame_pairs(1))
    down = lambda value: send(value, frame_pairs(-1))

    skv0, skv1, x0, y0 = pack(((0, 0, "kv"), (1, 0, "kv"), (0, 1, "kvq"), (0, 2, "kvq")), *arrays)
    x0, y0, skv1, skv0, meta, *shards = together(x0, y0, skv1, skv0, meta, *shards)
    strip = ring_order(shard, *shards, c)
    x1, y1, dkv0, dkv1, dq0, dq1, sq0, sq1 = pack(
        ((1, 1, "kvq"), (1, 2, "kvq"), (0, 3, "kv"), (1, 3, "kv"), (0, 3, "q"), (1, 3, "q"), (0, 0, "q"), (1, 0, "q")), meta, *arrays[1:]
    )
    first = go(x0, 0, row), go(y0, 0, col), up(skv1), down(skv0)
    x1, y1, strip, *first = together(x1, y1, strip, *first)
    x0, y0, up0, down0 = first
    second = go(x1, 1, row), go(y1, 1, col), *(send(strip, plane_pairs(d, 0)) for d in (1, 2, 3))
    dkv0, dkv1, x0, y0, *second = together(dkv0, dkv1, x0, y0, *second)
    x1, y1, *strips = second
    chunk = ring_order(strip, *strips, r & 3)
    third = go(dkv0, 0, both), go(dkv1, 1, both), down(halo_pack(x0, y0)), up(halo_pack(x1, y1))
    dq0, dq1, chunk, *third = together(dq0, dq1, chunk, *third)
    dkv0, dkv1, down1, up1 = third
    fourth = go(dq0, 0, both), go(dq1, 1, both), down(dkv0), up(dkv1)
    chunk, *fourth = together(chunk, *fourth)
    dq0, dq1, down2, up2 = fourth

    ring = [chunk, send(chunk, depth_pairs())]
    mixed1 = attend(1, meta, skv1, sq1, x1, y1, dkv1, dq1, down0, down1, down2)
    ring[1], skv0, *mixed1 = together(ring[1], skv0, *mixed1)
    back = lambda half, mixed: [mixed[0]] + [send(mixed[n], window_pairs(half, *MOVES[n], back=True)) for n in (1, 2, 3)]
    near = send(jnp.stack(ring[:2]), core_pairs())
    ring.append(send(ring[1], depth_pairs()))
    attended1 = back(1, mixed1)
    mixed0 = attend(0, meta, skv0, sq0, x0, y0, dkv0, dq0, up0, up1, up2)
    near, ring[2], *rest = together(near, ring[2], *attended1, *mixed0)
    attended1, mixed0 = rest[:4], rest[4:]
    attended0 = back(0, mixed0)
    ring.append(send(ring[2], depth_pairs()))
    attended = attended0 + attended1
    out = project(attended, meta, places[:5], (*ring[:3], near), tokens_in)
    last = together(ring[3], *attended)[0]
    far = send(jnp.stack([ring[2], last]), core_pairs())
    return project(attended, meta, places[5:], (ring[3], far), tokens_in, out)


def solution(mesh):
    return jax.shard_map(
        local,
        mesh=mesh,
        in_specs=(
            P("frame", "row", "col", None),
            P("frame", "row", "col", None),
            P("frame", "row", "col", None),
            P("frame", "row", "col", None),
            P(None, ("frame", "row", "col")),
            P(),
        ),
        out_specs=P("frame", "row", "col", None),
        check_vma=False,
    )
```

```python
import functools
import math

import jax
import jax.numpy as jnp
from jax import lax
from jax.experimental import pallas as pl
from jax.experimental.pallas import tpu as pltpu
from jax.sharding import PartitionSpec as P

D = 3072
H = 12
HS = 128
HD = 1536
F, R, C = 4, 8, 4
AXES = ("frame", "row", "col")
STEP = 2
BIG = 1e30
TILE = 384
VMEM = 56 * 1024 * 1024


def index(f, r, c):
    return ((f % F) * R + (r % R)) * C + (c % C)


def every():
    return [(f, r, c) for f in range(F) for r in range(R) for c in range(C)]


def window_pairs(half, dr, dc, back=False):
    pairs = []
    for f, r, c in every():
        step = 1 if (f + half) % 2 == 0 else -1
        here, there = index(f, r, c), index(f, r + step * dr, c + step * dc)
        pairs.append((there, here) if back else (here, there))
    return pairs


def frame_pairs(step):
    return [(index(f, r, c), index(f + step, r, c)) for f, r, c in every() if 0 <= f + step < F]


def core_pairs():
    return [(index(f, r, c), index(f ^ 1, r, c)) for f, r, c in every()]


def depth_pairs():
    pairs = []
    for f, r, c in every():
        zhi, core = divmod(f, 2)
        zlo, x = divmod(r, 4)
        z = (zhi * 2 + zlo + (1 if core == 0 else -1)) % 4
        pairs.append((index(f, r, c), index((z // 2) * 2 + core, (z % 2) * 4 + x, c)))
    return pairs


def send(value, pairs):
    return lax.ppermute(value, AXES, pairs)


MOVES = ((0, 0), (1, 0), (0, 1), (1, 1))


def sign_of(half, frame):
    return lax.rem(frame + half, 2)


def relay(moves, sems):
    inward = [pltpu.make_async_copy(src, held, sems.at[0, n]) for n, (src, held, _) in enumerate(moves)]
    outward = [pltpu.make_async_copy(held, dst, sems.at[1, n]) for n, (_, held, dst) in enumerate(moves)]
    for copy in inward:
        copy.start()
    for arrives, leaves in zip(inward, outward):
        arrives.wait()
        leaves.start()
    for copy in outward:
        copy.wait()


def pack_kernel(parts, meta, k_ref, v_ref, q_ref, *rest):
    outs, held, sems = rest[: len(parts)], rest[-2], rest[-1]
    moves = []
    for out, (half, piece, names) in zip(outs, parts):
        s = sign_of(half, meta[0])
        a, b = MOVES[piece]
        i = s + a * (1 - 2 * s)
        j = s + b * (1 - 2 * s)
        for n, name in enumerate(names):
            src = {"k": k_ref, "v": v_ref, "q": q_ref}[name]
            moves.append((src.at[pl.ds(2 * half, 2), i, :, j], held.at[len(moves)], out.at[n]))
    relay(moves, sems)


def pack(parts, meta, k, v, q):
    any_spec = pl.BlockSpec(memory_space=pl.ANY)
    count = sum(len(names) for _, _, names in parts)
    outs = pl.pallas_call(
        functools.partial(pack_kernel, parts),
        out_shape=[jax.ShapeDtypeStruct((len(names), 2, 8, 8, HD), jnp.bfloat16) for _, _, names in parts],
        in_specs=[pl.BlockSpec(memory_space=pltpu.SMEM)] + [any_spec] * 3,
        out_specs=[any_spec] * len(parts),
        scratch_shapes=[pltpu.VMEM((count, 2, 8, 8, HD), jnp.bfloat16), pltpu.SemaphoreType.DMA((2, count))],
        compiler_params=pltpu.CompilerParams(vmem_limit_bytes=VMEM),
        cost_estimate=pl.CostEstimate(flops=0, bytes_accessed=count * 2**20, transcendentals=0),
        name="pack",
    )(meta, k, v, q)
    return [o.reshape(-1, 128, HD) for o in outs]


def halo_kernel(*refs):
    srcs, out, held, sems = refs[:-3], refs[-3], refs[-2], refs[-1]
    relay([(src.at[pl.ds(0, 2)], held.at[n], out.at[n]) for n, src in enumerate(srcs)], sems)


def halo_pack(*pieces):
    any_spec = pl.BlockSpec(memory_space=pl.ANY)
    count = len(pieces)
    return pl.pallas_call(
        halo_kernel,
        out_shape=jax.ShapeDtypeStruct((count, 2, 128, HD), jnp.bfloat16),
        in_specs=[any_spec] * count,
        out_specs=any_spec,
        scratch_shapes=[pltpu.VMEM((count, 2, 128, HD), jnp.bfloat16), pltpu.SemaphoreType.DMA((2, count))],
        compiler_params=pltpu.CompilerParams(vmem_limit_bytes=VMEM),
        cost_estimate=pl.CostEstimate(flops=0, bytes_accessed=count * 3 * 2**19, transcendentals=0),
        name="halo_pack",
    )(*pieces)


def features(half, meta, kaug, qaug, alive):
    f, r, c, live_rows = (meta[n] for n in range(4))
    s = sign_of(half, f)
    stay = 2 * r + s
    moved = lax.rem(stay + 2 * s + 15, 16)
    row_split = r == s * (R - 1)
    col_split = c == s * (C - 1)
    missing = f == half * (F - 1)

    def places(count):
        token = lax.broadcasted_iota(jnp.int32, (count, HS), 0)
        lane = lax.broadcasted_iota(jnp.int32, (count, HS), 1)
        piece = (token // 128) % 4
        row = jnp.where(piece % 2 == 1, moved, stay) * 8 + (token // 8) % 8
        return token, lane, piece, row < live_rows

    token, lane, piece, live = places(1024)
    dead = (lane == 4) & jnp.logical_not(live)
    on = (lane == piece) | dead | ((lane == 5) & (token >= 512))
    kaug[:, HS:] = jnp.where(on, 1.0, 0.0).astype(jnp.bfloat16)
    token, lane, piece, live = places(512)
    rows_apart = (lane % 2 != piece % 2) & row_split
    cols_apart = (lane // 2 != piece // 2) & col_split
    off = ((lane < 4) & (rows_apart | cols_apart)) | (lane == 4) | ((lane == 5) & missing)
    qaug[:, HS:] = jnp.where(off, -BIG, 0.0).astype(jnp.bfloat16)
    alive[...] = jnp.where(live, 1.0, 0.0)


def attend_kernel(half, meta, skv, sq, x, y, d, h3, hd, o0, o1, o2, o3, kaug, vaug, qaug, alive):
    outs = (o0, o1, o2, o3)

    @pl.when(pl.program_id(0) == 0)
    def _():
        features(half, meta, kaug.at[0], qaug.at[0], alive)
        for n in range(1, STEP):
            kaug[n, :, HS:] = kaug[0, :, HS:]
            qaug[n, :, HS:] = qaug[0, :, HS:]
        vaug[:, :, HS:] = jnp.ones((STEP, 1024, HS), jnp.bfloat16)

    keys = (skv, x, y, d, h3.at[0], h3.at[1], h3.at[2], hd)
    asks = (sq.at[0], x.at[2], y.at[2], d.at[2])
    for h in range(STEP):
        lanes = pl.ds(h * HS, HS)
        for n, ref in enumerate(keys):
            kaug[h, pl.ds(n * 128, 128), :HS] = ref[0, :, lanes]
            vaug[h, pl.ds(n * 128, 128), :HS] = ref[1, :, lanes]
        for n, ref in enumerate(asks):
            qaug[h, pl.ds(n * 128, 128), :HS] = ref[:, lanes]
    scale = math.log2(math.e) / math.sqrt(HS)

    def score(at):
        h, part = divmod(at, 2)
        return lax.dot_general(
            qaug[h, pl.ds(part * 256, 256), :], kaug[h], (((1,), (1,)), ((), ())), preferred_element_type=jnp.float32
        )

    scores = score(0)
    for at in range(2 * STEP):
        later = score(at + 1) if at + 1 < 2 * STEP else None
        h, part = divmod(at, 2)
        lanes = pl.ds(h * HS, HS)
        top = jnp.max(scores, axis=1, keepdims=True)
        weights = jnp.exp2((scores - top) * scale).astype(jnp.bfloat16)
        mixed = jnp.dot(weights, vaug[h], preferred_element_type=jnp.float32)
        result = (mixed[:, :HS] / mixed[:, HS:] * alive[pl.ds(part * 256, 256), :]).astype(jnp.bfloat16)
        outs[2 * part][:, lanes] = result[:128]
        outs[2 * part + 1][:, lanes] = result[128:]
        scores = later


def attend(half, meta, *pieces):
    width = STEP * HS

    def spec(piece):
        lead = piece.shape[:-1]
        return pl.BlockSpec((*lead, width), lambda h: (0,) * len(lead) + (h,))

    return pl.pallas_call(
        functools.partial(attend_kernel, half),
        grid=(H // STEP,),
        out_shape=[jax.ShapeDtypeStruct((128, HD), jnp.bfloat16)] * 4,
        in_specs=[pl.BlockSpec(memory_space=pltpu.SMEM)] + [spec(piece) for piece in pieces],
        out_specs=[pl.BlockSpec((128, width), lambda h: (0, h))] * 4,
        scratch_shapes=[
            pltpu.VMEM((STEP, 1024, 2 * HS), jnp.bfloat16),
            pltpu.VMEM((STEP, 1024, 2 * HS), jnp.bfloat16),
            pltpu.VMEM((STEP, 512, 2 * HS), jnp.bfloat16),
            pltpu.VMEM((512, HS), jnp.float32),
        ],
        compiler_params=pltpu.CompilerParams(vmem_limit_bytes=VMEM),
        cost_estimate=pl.CostEstimate(flops=H * 4 * 512 * 1024 * 256, bytes_accessed=10 * 2**20, transcendentals=H * 2**19),
        name="attend",
    )(meta, *pieces)


def project_kernel(shapes, frame, places, *refs):
    count = len(shapes)
    attended, sources, tokens, rest = refs[:8], refs[8 : 8 + count], refs[8 + count], refs[9 + count :]
    out, lhs, held, given, made, sems = rest[-6:]
    chunks = [ref.at[n] if lead else ref for ref, lead in zip(sources, shapes) for n in range(lead or 1)]
    pairs = len(chunks) // 2

    def columns(n):
        return pl.ds(pl.multiple_of(places[n] * TILE, 128), TILE)

    fetches = [
        [pltpu.make_async_copy(chunks[n], held.at[n], sems.at[0, n]) for n in range(len(chunks))],
        [pltpu.make_async_copy(tokens.at[:, :, :, columns(n)], given.at[n], sems.at[1, n]) for n in range(len(chunks))],
    ]
    stores = [pltpu.make_async_copy(made.at[n], out.at[:, :, :, columns(n)], sems.at[2, n]) for n in range(len(chunks))]
    for n in range(len(chunks)):
        fetches[0][n].start()
        fetches[1][n].start()
    for half in range(2):
        s = sign_of(half, frame[0])
        for piece, (a, b) in enumerate(MOVES):
            i = s + a * (1 - 2 * s)
            j = s + b * (1 - 2 * s)
            lhs[half * 4 + i * 2 + j] = attended[half * 4 + piece][...]
    for pair in range(pairs):
        for n in (2 * pair, 2 * pair + 1):
            fetches[0][n].wait()
            fetches[1][n].wait()
        total = lax.dot_general(
            lhs[...].reshape(1024, HD),
            held[2 * pair : 2 * pair + 2].reshape(2 * TILE, HD),
            (((1,), (1,)), ((), ())),
            preferred_element_type=jnp.float32,
        ).reshape(2, 2, 2, 2, 8, 8, 2 * TILE)
        for m in range(2):
            n = 2 * pair + m
            part = total[..., m * TILE : (m + 1) * TILE]
            for half in range(2):
                for i in range(2):
                    block = jnp.concatenate([part[half, i, 0], part[half, i, 1]], axis=2)
                    at = (n, slice(2 * half, 2 * half + 2), slice(8 * i, 8 * i + 8))
                    made[at] = (block + given[at].astype(jnp.float32)).astype(jnp.bfloat16)
            stores[n].start()
    for store in stores:
        store.wait()


def project(attended, frame, places, chunks, tokens, partial=None):
    shapes = tuple(chunk.shape[0] if chunk.ndim == 3 else 0 for chunk in chunks)
    count = sum(max(lead, 1) for lead in shapes)
    extra = [] if partial is None else [partial]
    any_spec = pl.BlockSpec(memory_space=pl.ANY)
    smem = pl.BlockSpec(memory_space=pltpu.SMEM)
    vmem = pl.BlockSpec(memory_space=pltpu.VMEM)
    return pl.pallas_call(
        functools.partial(project_kernel, shapes),
        in_specs=[smem] * 2 + [vmem] * 8 + [any_spec] * (len(chunks) + 1 + len(extra)),
        out_specs=any_spec,
        out_shape=jax.ShapeDtypeStruct((4, 16, 16, D), jnp.bfloat16),
        scratch_shapes=[
            pltpu.VMEM((8, 128, HD), jnp.bfloat16),
            pltpu.VMEM((count, TILE, HD), jnp.bfloat16),
            pltpu.VMEM((count, 4, 16, 16, TILE), jnp.bfloat16),
            pltpu.VMEM((count, 4, 16, 16, TILE), jnp.bfloat16),
            pltpu.SemaphoreType.DMA((3, count)),
        ],
        input_output_aliases={} if partial is None else {11 + len(chunks): 0},
        compiler_params=pltpu.CompilerParams(vmem_limit_bytes=VMEM),
        cost_estimate=pl.CostEstimate(flops=2 * 1024 * HD * TILE * count, bytes_accessed=3 * 2**20 * (count + 1), transcendentals=0),
        name="project",
    )(frame, places, *attended, *chunks, tokens, *extra)


def plane_groups():
    return [[index(f, zlo * 4 + x, c) for x in range(4) for c in range(C)] for f in range(F) for zlo in range(2)]


def weight_places(f, r):
    core, z = f & 1, (f >> 1) * 2 + (r >> 2)
    places = []
    for k in (core, 1 - core):
        at = [(z + n * (2 * k - 1) + 4) & 3 for n in range(4)]
        places.append([((a >> 1) * 2 + k) * 2 + (a & 1) for a in at])
    (a0, a1, a2, a3), (b0, b1, b2, b3) = places
    return jnp.stack([a0, a1, b0, b1, a2, a3, b2, b3]).astype(jnp.int32)


def together(*values):
    return lax.optimization_barrier(values)


def local(tokens_in, queries, key_rows, value_rows, out_weight, row_valid):
    f, r, c = (lax.axis_index(a) for a in AXES)
    frame = f.astype(jnp.int32).reshape(1)
    meta = jnp.stack([f, r, c, jnp.sum(row_valid)]).astype(jnp.int32)
    places = weight_places(f, r)
    split = lambda a: a.reshape(4, 2, 8, 2, 8, HD)
    arrays = (split(key_rows), split(value_rows), split(queries))
    chunk = lax.all_gather(out_weight.T, AXES, axis=0, tiled=True, axis_index_groups=plane_groups())

    row, col, both = MOVES[1:]
    go = lambda value, half, move: send(value, window_pairs(half, *move))
    up = lambda value: send(value, frame_pairs(1))
    down = lambda value: send(value, frame_pairs(-1))
    swap = lambda value: send(value, core_pairs())
    turn = lambda value: send(value, depth_pairs())
    back = lambda half, mixed: [mixed[0]] + [send(mixed[n], window_pairs(half, *MOVES[n], back=True)) for n in (1, 2, 3)]

    x0, y0, x1, y1 = pack(((0, 1, "kvq"), (0, 2, "kvq"), (1, 1, "kvq"), (1, 2, "kvq")), frame, *arrays)
    x0, y0, x1, y1, frame = together(x0, y0, x1, y1, frame)
    first = go(x0, 0, row), go(y0, 0, col), go(x1, 1, row), go(y1, 1, col)
    skv0, skv1, d0, d1, sq0, sq1 = pack(
        ((0, 0, "kv"), (1, 0, "kv"), (0, 3, "kvq"), (1, 3, "kvq"), (0, 0, "q"), (1, 0, "q")), frame, *arrays
    )
    d0, d1, *first = together(d0, d1, *first)
    x0, y0, x1, y1 = first
    second = go(d0, 0, both), go(d1, 1, both), down(halo_pack(skv0, x0, y0)), up(halo_pack(skv1, x1, y1))
    chunk, *second = together(chunk, *second)
    d0, d1, down3, up3 = second
    third = down(d0[:2]), up(d1[:2])
    chunk, downd, upd = together(chunk, *third)

    c1, other0 = turn(chunk), swap(chunk)
    mixed1 = attend(1, meta, skv1, sq1, x1, y1, d1, down3, downd)
    c1, other0, skv0, *mixed1 = together(c1, other0, skv0, *mixed1)
    c2 = turn(c1)
    attended1 = back(1, mixed1)
    mixed0 = attend(0, meta, skv0, sq0, x0, y0, d0, up3, upd)
    c2, *rest = together(c2, *attended1, *mixed0)
    attended1, mixed0 = rest[:4], rest[4:]
    attended0 = back(0, mixed0)
    c3, other1 = turn(c2), swap(c1)
    attended = attended0 + attended1
    out = project(attended, frame, places[:4], (chunk, c1, other0, other1), tokens_in)
    last = together(c3, *attended)[0]
    pair = jnp.stack([c2, last])
    return project(attended, frame, places[4:], (pair, swap(pair)), tokens_in, out)


def solution(mesh):
    return jax.shard_map(
        local,
        mesh=mesh,
        in_specs=(
            P("frame", "row", "col", None),
            P("frame", "row", "col", None),
            P("frame", "row", "col", None),
            P("frame", "row", "col", None),
            P(None, ("frame", "row", "col")),
            P(),
        ),
        out_specs=P("frame", "row", "col", None),
        check_vma=False,
    )
```

```python
import functools
import math

import jax
import jax.numpy as jnp
from jax import lax
from jax.experimental import pallas as pl
from jax.experimental.pallas import tpu as pltpu
from jax.sharding import PartitionSpec as P

D = 3072
H = 12
HS = 128
HD = 1536
F, R, C = 4, 8, 4
AXES = ("frame", "row", "col")
STEP = 2
BIG = 1e30
TILE = 768
VMEM = 56 * 1024 * 1024


def index(f, r, c):
    return ((f % F) * R + (r % R)) * C + (c % C)


def every():
    return [(f, r, c) for f in range(F) for r in range(R) for c in range(C)]


def window_pairs(half, dr, dc, back=False):
    pairs = []
    for f, r, c in every():
        step = 1 if (f + half) % 2 == 0 else -1
        here, there = index(f, r, c), index(f, r + step * dr, c + step * dc)
        pairs.append((there, here) if back else (here, there))
    return pairs


def frame_pairs(step):
    return [(index(f, r, c), index(f + step, r, c)) for f, r, c in every() if 0 <= f + step < F]


def core_pairs():
    return [(index(f, r, c), index(f ^ 1, r, c)) for f, r, c in every()]


def turn_pairs():
    pairs = []
    for f, r, c in every():
        zlo, x = divmod(r, 4)
        pairs.append((index(f, r, c), index(f, zlo * 4 + (x + 1 - 2 * (f % 2)) % 4, c)))
    return pairs


def send(value, pairs):
    return lax.ppermute(value, AXES, pairs)


MOVES = ((0, 0), (1, 0), (0, 1), (1, 1))


def sign_of(half, frame):
    return lax.rem(frame + half, 2)


def relay(moves, sems):
    inward = [pltpu.make_async_copy(src, held, sems.at[0, n]) for n, (src, held, _) in enumerate(moves)]
    outward = [pltpu.make_async_copy(held, dst, sems.at[1, n]) for n, (_, held, dst) in enumerate(moves)]
    for copy in inward:
        copy.start()
    for arrives, leaves in zip(inward, outward):
        arrives.wait()
        leaves.start()
    for copy in outward:
        copy.wait()


def pack_kernel(parts, meta, k_ref, v_ref, q_ref, *rest):
    outs, held, sems = rest[: len(parts)], rest[-2], rest[-1]
    moves = []
    for out, (half, piece, names) in zip(outs, parts):
        s = sign_of(half, meta[0])
        a, b = MOVES[piece]
        i = s + a * (1 - 2 * s)
        j = s + b * (1 - 2 * s)
        for n, name in enumerate(names):
            src = {"k": k_ref, "v": v_ref, "q": q_ref}[name]
            moves.append((src.at[pl.ds(2 * half, 2), i, :, j], held.at[len(moves)], out.at[n]))
    relay(moves, sems)


def pack(parts, meta, k, v, q):
    any_spec = pl.BlockSpec(memory_space=pl.ANY)
    count = sum(len(names) for _, _, names in parts)
    outs = pl.pallas_call(
        functools.partial(pack_kernel, parts),
        out_shape=[jax.ShapeDtypeStruct((len(names), 2, 8, 8, HD), jnp.bfloat16) for _, _, names in parts],
        in_specs=[pl.BlockSpec(memory_space=pltpu.SMEM)] + [any_spec] * 3,
        out_specs=[any_spec] * len(parts),
        scratch_shapes=[pltpu.VMEM((count, 2, 8, 8, HD), jnp.bfloat16), pltpu.SemaphoreType.DMA((2, count))],
        compiler_params=pltpu.CompilerParams(vmem_limit_bytes=VMEM),
        cost_estimate=pl.CostEstimate(flops=0, bytes_accessed=count * 2**20, transcendentals=0),
        name="pack",
    )(meta, k, v, q)
    return [o.reshape(-1, 128, HD) for o in outs]


def halo_kernel(*refs):
    srcs, outs, sems = refs[:6], refs[6:8], refs[8]
    copies = []
    for half in range(2):
        for n in range(3):
            src = srcs[3 * half + n].at[pl.ds(0, 2)]
            copies.append(pltpu.make_async_copy(src, outs[half].at[n], sems.at[half, n]))
    for copy in copies:
        copy.start()
    for copy in copies:
        copy.wait()


def halo_pack(*pieces):
    return pl.pallas_call(
        halo_kernel,
        out_shape=[jax.ShapeDtypeStruct((3, 2, 128, HD), jnp.bfloat16)] * 2,
        in_specs=[pl.BlockSpec(memory_space=pltpu.VMEM)] * 6,
        out_specs=[pl.BlockSpec(memory_space=pl.ANY)] * 2,
        scratch_shapes=[pltpu.SemaphoreType.DMA((2, 3))],
        compiler_params=pltpu.CompilerParams(vmem_limit_bytes=VMEM),
        cost_estimate=pl.CostEstimate(flops=0, bytes_accessed=10 * 2**20, transcendentals=0),
        name="halo_pack",
    )(*pieces)


def features(half, meta, kaug, qaug, alive):
    f, r, c, live_rows = (meta[n] for n in range(4))
    s = sign_of(half, f)
    stay = 2 * r + s
    moved = lax.rem(stay + 2 * s + 15, 16)
    row_split = r == s * (R - 1)
    col_split = c == s * (C - 1)
    missing = f == half * (F - 1)

    def places(count):
        token = lax.broadcasted_iota(jnp.int32, (count, HS), 0)
        lane = lax.broadcasted_iota(jnp.int32, (count, HS), 1)
        piece = (token // 128) % 4
        row = jnp.where(piece % 2 == 1, moved, stay) * 8 + (token // 8) % 8
        return token, lane, piece, row < live_rows

    token, lane, piece, live = places(1024)
    dead = (lane == 4) & jnp.logical_not(live)
    on = (lane == piece) | dead | ((lane == 5) & (token >= 512))
    kaug[:, HS:] = jnp.where(on, 1.0, 0.0).astype(jnp.bfloat16)
    token, lane, piece, live = places(512)
    rows_apart = (lane % 2 != piece % 2) & row_split
    cols_apart = (lane // 2 != piece // 2) & col_split
    off = ((lane < 4) & (rows_apart | cols_apart)) | (lane == 4) | ((lane == 5) & missing)
    qaug[:, HS:] = jnp.where(off, -BIG, 0.0).astype(jnp.bfloat16)
    alive[...] = jnp.where(live, 1.0, 0.0)


def attend_kernel(half, meta, skv, sq, x, y, d, h3, hd, o0, o1, o2, o3, kaug, vaug, qaug, alive):
    outs = (o0, o1, o2, o3)

    @pl.when(pl.program_id(0) == 0)
    def _():
        features(half, meta, kaug.at[0], qaug.at[0], alive)
        for n in range(1, STEP):
            kaug[n, :, HS:] = kaug[0, :, HS:]
            qaug[n, :, HS:] = qaug[0, :, HS:]
        vaug[:, :, HS:] = jnp.ones((STEP, 1024, HS), jnp.bfloat16)

    keys = (skv, x, y, d, h3.at[0], h3.at[1], h3.at[2], hd)
    asks = (sq.at[0], x.at[2], y.at[2], d.at[2])
    for h in range(STEP):
        lanes = pl.ds(h * HS, HS)
        for n, ref in enumerate(keys):
            kaug[h, pl.ds(n * 128, 128), :HS] = ref[0, :, lanes]
            vaug[h, pl.ds(n * 128, 128), :HS] = ref[1, :, lanes]
        for n, ref in enumerate(asks):
            qaug[h, pl.ds(n * 128, 128), :HS] = ref[:, lanes]
    scale = math.log2(math.e) / math.sqrt(HS)

    def score(at):
        h, part = divmod(at, 2)
        return lax.dot_general(
            qaug[h, pl.ds(part * 256, 256), :], kaug[h], (((1,), (1,)), ((), ())), preferred_element_type=jnp.float32
        )

    scores = score(0)
    for at in range(2 * STEP):
        later = score(at + 1) if at + 1 < 2 * STEP else None
        h, part = divmod(at, 2)
        lanes = pl.ds(h * HS, HS)
        top = jnp.max(scores, axis=1, keepdims=True)
        weights = jnp.exp2((scores - top) * scale).astype(jnp.bfloat16)
        mixed = jnp.dot(weights, vaug[h], preferred_element_type=jnp.float32)
        result = (mixed[:, :HS] / mixed[:, HS:] * alive[pl.ds(part * 256, 256), :]).astype(jnp.bfloat16)
        outs[2 * part][:, lanes] = result[:128]
        outs[2 * part + 1][:, lanes] = result[128:]
        scores = later


def attend(half, meta, *pieces):
    width = STEP * HS

    def spec(piece):
        lead = piece.shape[:-1]
        return pl.BlockSpec((*lead, width), lambda h: (0,) * len(lead) + (h,))

    return pl.pallas_call(
        functools.partial(attend_kernel, half),
        grid=(H // STEP,),
        out_shape=[jax.ShapeDtypeStruct((128, HD), jnp.bfloat16)] * 4,
        in_specs=[pl.BlockSpec(memory_space=pltpu.SMEM)] + [spec(piece) for piece in pieces],
        out_specs=[pl.BlockSpec((128, width), lambda h: (0, h))] * 4,
        scratch_shapes=[
            pltpu.VMEM((STEP, 1024, 2 * HS), jnp.bfloat16),
            pltpu.VMEM((STEP, 1024, 2 * HS), jnp.bfloat16),
            pltpu.VMEM((STEP, 512, 2 * HS), jnp.bfloat16),
            pltpu.VMEM((512, HS), jnp.float32),
        ],
        compiler_params=pltpu.CompilerParams(vmem_limit_bytes=VMEM),
        cost_estimate=pl.CostEstimate(flops=H * 4 * 512 * 1024 * 256, bytes_accessed=10 * 2**20, transcendentals=H * 2**19),
        name="attend",
    )(meta, *pieces)


def project_kernel(meta, places, *refs):
    attended, own, other, (tokens, out, lhs, held, sems) = refs[:8], refs[8:12], refs[12:16], refs[16:]
    step = pl.program_id(0)
    core, x = lax.rem(meta[0], 2), lax.rem(meta[1], 4)

    def fetch(n):
        side, zhi = divmod(n, 2)
        k = core if side == 0 else 1 - core
        copies = []
        for turn, src in enumerate(other if side else own):
            at = lax.rem(x + turn * (2 * k - 1) + 4, 4)
            for zlo in range(2):
                to = pl.ds(pl.multiple_of(zlo * 384 + at * 96, 32), 96)
                copies.append(
                    pltpu.make_async_copy(
                        src.at[pl.ds((2 * zhi + zlo) * 96, 96)], held.at[n % 2, to], sems.at[n % 2, 2 * turn + zlo]
                    )
                )
        return copies

    @pl.when(step == 0)
    def _():
        for copy in fetch(0):
            copy.start()
        for half in range(2):
            s = sign_of(half, meta[0])
            for piece, (a, b) in enumerate(MOVES):
                i = s + a * (1 - 2 * s)
                j = s + b * (1 - 2 * s)
                lhs[half * 4 + i * 2 + j] = attended[half * 4 + piece][...]

    for n in range(4):

        @pl.when(step == n)
        def _():
            for copy in fetch(n):
                copy.wait()
            if n < 3:
                for copy in fetch(n + 1):
                    copy.start()

    total = lax.dot_general(
        lhs[...].reshape(1024, HD), held[lax.rem(step, 2)], (((1,), (1,)), ((), ())), preferred_element_type=jnp.float32
    ).reshape(2, 2, 2, 2, 8, 8, TILE)
    for half in range(2):
        for i in range(2):
            block = jnp.concatenate([total[half, i, 0], total[half, i, 1]], axis=2)
            at = (slice(2 * half, 2 * half + 2), slice(8 * i, 8 * i + 8))
            out[at] = (block + tokens[at].astype(jnp.float32)).astype(jnp.bfloat16)


def project(attended, meta, places, chunks, tokens):
    grid_spec = pltpu.PrefetchScalarGridSpec(
        num_scalar_prefetch=2,
        grid=(D // TILE,),
        in_specs=[pl.BlockSpec((128, HD), lambda t, m, p: (0, 0))] * 8
        + [pl.BlockSpec(memory_space=pl.ANY)] * 8
        + [pl.BlockSpec((4, 16, 16, TILE), lambda t, m, p: (0, 0, 0, p[t]))],
        out_specs=pl.BlockSpec((4, 16, 16, TILE), lambda t, m, p: (0, 0, 0, p[t])),
        scratch_shapes=[
            pltpu.VMEM((8, 128, HD), jnp.bfloat16),
            pltpu.VMEM((2, TILE, HD), jnp.bfloat16),
            pltpu.SemaphoreType.DMA((2, 8)),
        ],
    )
    return pl.pallas_call(
        project_kernel,
        grid_spec=grid_spec,
        out_shape=jax.ShapeDtypeStruct((4, 16, 16, D), jnp.bfloat16),
        compiler_params=pltpu.CompilerParams(vmem_limit_bytes=VMEM),
        cost_estimate=pl.CostEstimate(flops=2 * 1024 * HD * D, bytes_accessed=25 * 2**20, transcendentals=0),
        name="project",
    )(meta, places, *attended, *chunks, tokens)


def strip_groups():
    return [
        [index(2 * zhi + core, zlo * 4 + x, c) for zhi in range(2) for zlo in range(2) for c in range(C)]
        for core in range(2)
        for x in range(4)
    ]


def together(*values):
    return lax.optimization_barrier(values)


def local(tokens_in, queries, key_rows, value_rows, out_weight, row_valid):
    f, r, c = (lax.axis_index(a) for a in AXES)
    frame = f.astype(jnp.int32).reshape(1)
    meta = jnp.stack([f, r, c, jnp.sum(row_valid)]).astype(jnp.int32)
    core = f & 1
    places = jnp.stack([core, 2 + core, 1 - core, 3 - core]).astype(jnp.int32)
    split = lambda a: a.reshape(4, 2, 8, 2, 8, HD)
    arrays = (split(key_rows), split(value_rows), split(queries))
    chunk = lax.all_gather(out_weight.T, AXES, axis=0, tiled=True, axis_index_groups=strip_groups())

    row, col, both = MOVES[1:]
    go = lambda value, half, move: send(value, window_pairs(half, *move))
    up = lambda value: send(value, frame_pairs(1))
    down = lambda value: send(value, frame_pairs(-1))
    swap = lambda value: send(value, core_pairs())
    turn = lambda value: send(value, turn_pairs())
    back = lambda half, mixed: [mixed[0]] + [send(mixed[n], window_pairs(half, *MOVES[n], back=True)) for n in (1, 2, 3)]

    x0, y0 = pack(((0, 1, "kvq"), (0, 2, "kvq")), frame, *arrays)
    x0, y0, frame = together(x0, y0, frame)
    x0, y0 = go(x0, 0, row), go(y0, 0, col)
    x1, y1 = pack(((1, 1, "kvq"), (1, 2, "kvq")), frame, *arrays)
    x1, y1, frame = together(x1, y1, frame)
    x1, y1 = go(x1, 1, row), go(y1, 1, col)
    skv0, skv1, d0, d1, sq0, sq1 = pack(
        ((0, 0, "kv"), (1, 0, "kv"), (0, 3, "kvq"), (1, 3, "kvq"), (0, 0, "q"), (1, 0, "q")), frame, *arrays
    )
    d0, x0, y0, meta, places = together(d0, x0, y0, meta, places)
    d1, x1, y1 = together(d1, x1, y1)
    d0, d1 = go(d0, 0, both), go(d1, 1, both)
    h0, h1 = halo_pack(skv0, x0, y0, skv1, x1, y1)
    chunk, h0, h1 = together(chunk, h0, h1)
    down3, up3 = down(h0), up(h1)
    c0, d0, d1 = together(chunk, d0, d1)
    c1 = turn(c0)
    c1, down3, up3, hd0, hd1 = together(c1, down3, up3, d0[:2], d1[:2])
    downd, upd, c2 = down(hd0), up(hd1), turn(c1)
    c2, downd, upd = together(c2, downd, upd)

    c3, s0, s1, s2 = turn(c2), swap(c0), swap(c1), swap(c2)
    mixed1 = attend(1, meta, skv1, sq1, x1, y1, d1, down3, downd)
    c3, s0, s1, s2, skv0, *mixed1 = together(c3, s0, s1, s2, skv0, *mixed1)
    attended1, s3 = back(1, mixed1), swap(c3)
    mixed0 = attend(0, meta, skv0, sq0, x0, y0, d0, up3, upd)
    s3, *rest = together(s3, *attended1, *mixed0)
    attended1, mixed0 = rest[:4], rest[4:]
    attended0 = back(0, mixed0)
    return project(attended0 + attended1, meta, places, (c0, c1, c2, c3, s0, s1, s2, s3), tokens_in)


def solution(mesh):
    return jax.shard_map(
        local,
        mesh=mesh,
        in_specs=(
            P("frame", "row", "col", None),
            P("frame", "row", "col", None),
            P("frame", "row", "col", None),
            P("frame", "row", "col", None),
            P(None, ("frame", "row", "col")),
            P(),
        ),
        out_specs=P("frame", "row", "col", None),
        check_vma=False,
    )
```

```python
import functools
import math

import jax
import jax.numpy as jnp
from jax import lax
from jax.experimental import pallas as pl
from jax.experimental.pallas import tpu as pltpu
from jax.sharding import PartitionSpec as P

D = 3072
H = 12
HS = 128
HD = 1536
F, R, C = 4, 8, 4
AXES = ("frame", "row", "col")
STEP = 2
BIG = 1e30
TILE = 768
VMEM = 56 * 1024 * 1024


def index(f, r, c):
    return ((f % F) * R + (r % R)) * C + (c % C)


def every():
    return [(f, r, c) for f in range(F) for r in range(R) for c in range(C)]


def window_pairs(half, dr, dc, back=False):
    pairs = []
    for f, r, c in every():
        step = 1 if (f + half) % 2 == 0 else -1
        here, there = index(f, r, c), index(f, r + step * dr, c + step * dc)
        pairs.append((there, here) if back else (here, there))
    return pairs


def frame_pairs(step):
    return [(index(f, r, c), index(f + step, r, c)) for f, r, c in every() if 0 <= f + step < F]


def core_pairs():
    return [(index(f, r, c), index(f ^ 1, r, c)) for f, r, c in every()]


def shift_pairs(dx=0, dy=0, dz=0, opposed=False):
    pairs = []
    for f, r, c in every():
        (zhi, core), (zlo, x) = divmod(f, 2), divmod(r, 4)
        way = -1 if opposed and core else 1
        z = (2 * zhi + zlo + way * dz) % 4
        pairs.append((index(f, r, c), index((z // 2) * 2 + core, (z % 2) * 4 + (x + way * dx) % 4, c + way * dy)))
    return pairs


def send(value, pairs):
    return lax.ppermute(value, AXES, pairs)


MOVES = ((0, 0), (1, 0), (0, 1), (1, 1))


def sign_of(half, frame):
    return lax.rem(frame + half, 2)


def relay(moves, sems):
    inward = [pltpu.make_async_copy(src, held, sems.at[0, n]) for n, (src, held, _) in enumerate(moves)]
    outward = [pltpu.make_async_copy(held, dst, sems.at[1, n]) for n, (_, held, dst) in enumerate(moves)]
    for copy in inward:
        copy.start()
    for arrives, leaves in zip(inward, outward):
        arrives.wait()
        leaves.start()
    for copy in outward:
        copy.wait()


def pack_kernel(parts, meta, k_ref, v_ref, q_ref, *rest):
    outs, held, sems = rest[: len(parts)], rest[-2], rest[-1]
    moves = []
    for out, (half, piece, names) in zip(outs, parts):
        s = sign_of(half, meta[0])
        a, b = MOVES[piece]
        i = s + a * (1 - 2 * s)
        j = s + b * (1 - 2 * s)
        for n, name in enumerate(names):
            src = {"k": k_ref, "v": v_ref, "q": q_ref}[name]
            moves.append((src.at[pl.ds(2 * half, 2), i, :, j], held.at[len(moves)], out.at[n]))
    relay(moves, sems)


def pack(parts, meta, k, v, q):
    any_spec = pl.BlockSpec(memory_space=pl.ANY)
    count = sum(len(names) for _, _, names in parts)
    outs = pl.pallas_call(
        functools.partial(pack_kernel, parts),
        out_shape=[jax.ShapeDtypeStruct((len(names), 2, 8, 8, HD), jnp.bfloat16) for _, _, names in parts],
        in_specs=[pl.BlockSpec(memory_space=pltpu.SMEM)] + [any_spec] * 3,
        out_specs=[any_spec] * len(parts),
        scratch_shapes=[pltpu.VMEM((count, 2, 8, 8, HD), jnp.bfloat16), pltpu.SemaphoreType.DMA((2, count))],
        compiler_params=pltpu.CompilerParams(vmem_limit_bytes=VMEM),
        cost_estimate=pl.CostEstimate(flops=0, bytes_accessed=count * 2**20, transcendentals=0),
        name="pack",
    )(meta, k, v, q)
    return [o.reshape(-1, 128, HD) for o in outs]


def halo_kernel(*refs):
    srcs, outs, sems = refs[:6], refs[6:8], refs[8]
    copies = []
    for half in range(2):
        for n in range(3):
            src = srcs[3 * half + n].at[pl.ds(0, 2)]
            copies.append(pltpu.make_async_copy(src, outs[half].at[n], sems.at[half, n]))
    for copy in copies:
        copy.start()
    for copy in copies:
        copy.wait()


def halo_pack(*pieces):
    return pl.pallas_call(
        halo_kernel,
        out_shape=[jax.ShapeDtypeStruct((3, 2, 128, HD), jnp.bfloat16)] * 2,
        in_specs=[pl.BlockSpec(memory_space=pltpu.VMEM)] * 6,
        out_specs=[pl.BlockSpec(memory_space=pl.ANY)] * 2,
        scratch_shapes=[pltpu.SemaphoreType.DMA((2, 3))],
        compiler_params=pltpu.CompilerParams(vmem_limit_bytes=VMEM),
        cost_estimate=pl.CostEstimate(flops=0, bytes_accessed=10 * 2**20, transcendentals=0),
        name="halo_pack",
    )(*pieces)


def features(half, meta, kaug, qaug, alive):
    f, r, c, live_rows = (meta[n] for n in range(4))
    s = sign_of(half, f)
    stay = 2 * r + s
    moved = lax.rem(stay + 2 * s + 15, 16)
    row_split = r == s * (R - 1)
    col_split = c == s * (C - 1)
    missing = f == half * (F - 1)

    def places(count):
        token = lax.broadcasted_iota(jnp.int32, (count, HS), 0)
        lane = lax.broadcasted_iota(jnp.int32, (count, HS), 1)
        piece = (token // 128) % 4
        row = jnp.where(piece % 2 == 1, moved, stay) * 8 + (token // 8) % 8
        return token, lane, piece, row < live_rows

    token, lane, piece, live = places(1024)
    dead = (lane == 4) & jnp.logical_not(live)
    on = (lane == piece) | dead | ((lane == 5) & (token >= 512))
    kaug[:, HS:] = jnp.where(on, 1.0, 0.0).astype(jnp.bfloat16)
    token, lane, piece, live = places(512)
    rows_apart = (lane % 2 != piece % 2) & row_split
    cols_apart = (lane // 2 != piece // 2) & col_split
    off = ((lane < 4) & (rows_apart | cols_apart)) | (lane == 4) | ((lane == 5) & missing)
    qaug[:, HS:] = jnp.where(off, -BIG, 0.0).astype(jnp.bfloat16)
    alive[...] = jnp.where(live, 1.0, 0.0)


def attend_kernel(half, meta, skv, sq, x, y, d, h3, hd, o0, o1, o2, o3, kaug, vaug, qaug, alive):
    outs = (o0, o1, o2, o3)

    @pl.when(pl.program_id(0) == 0)
    def _():
        features(half, meta, kaug.at[0], qaug.at[0], alive)
        for n in range(1, STEP):
            kaug[n, :, HS:] = kaug[0, :, HS:]
            qaug[n, :, HS:] = qaug[0, :, HS:]
        vaug[:, :, HS:] = jnp.ones((STEP, 1024, HS), jnp.bfloat16)

    keys = (skv, x, y, d, h3.at[0], h3.at[1], h3.at[2], hd)
    asks = (sq.at[0], x.at[2], y.at[2], d.at[2])
    for h in range(STEP):
        lanes = pl.ds(h * HS, HS)
        for n, ref in enumerate(keys):
            kaug[h, pl.ds(n * 128, 128), :HS] = ref[0, :, lanes]
            vaug[h, pl.ds(n * 128, 128), :HS] = ref[1, :, lanes]
        for n, ref in enumerate(asks):
            qaug[h, pl.ds(n * 128, 128), :HS] = ref[:, lanes]
    scale = math.log2(math.e) / math.sqrt(HS)

    def score(at):
        h, part = divmod(at, 2)
        return lax.dot_general(
            qaug[h, pl.ds(part * 256, 256), :], kaug[h], (((1,), (1,)), ((), ())), preferred_element_type=jnp.float32
        )

    scores = score(0)
    for at in range(2 * STEP):
        later = score(at + 1) if at + 1 < 2 * STEP else None
        h, part = divmod(at, 2)
        lanes = pl.ds(h * HS, HS)
        top = jnp.max(scores, axis=1, keepdims=True)
        weights = jnp.exp2((scores - top) * scale).astype(jnp.bfloat16)
        mixed = jnp.dot(weights, vaug[h], preferred_element_type=jnp.float32)
        result = (mixed[:, :HS] / mixed[:, HS:] * alive[pl.ds(part * 256, 256), :]).astype(jnp.bfloat16)
        outs[2 * part][:, lanes] = result[:128]
        outs[2 * part + 1][:, lanes] = result[128:]
        scores = later


def attend(half, meta, *pieces):
    width = STEP * HS

    def spec(piece):
        lead = piece.shape[:-1]
        return pl.BlockSpec((*lead, width), lambda h: (0,) * len(lead) + (h,))

    return pl.pallas_call(
        functools.partial(attend_kernel, half),
        grid=(H // STEP,),
        out_shape=[jax.ShapeDtypeStruct((128, HD), jnp.bfloat16)] * 4,
        in_specs=[pl.BlockSpec(memory_space=pltpu.SMEM)] + [spec(piece) for piece in pieces],
        out_specs=[pl.BlockSpec((128, width), lambda h: (0, h))] * 4,
        scratch_shapes=[
            pltpu.VMEM((STEP, 1024, 2 * HS), jnp.bfloat16),
            pltpu.VMEM((STEP, 1024, 2 * HS), jnp.bfloat16),
            pltpu.VMEM((STEP, 512, 2 * HS), jnp.bfloat16),
            pltpu.VMEM((512, HS), jnp.float32),
        ],
        compiler_params=pltpu.CompilerParams(vmem_limit_bytes=VMEM),
        cost_estimate=pl.CostEstimate(flops=H * 4 * 512 * 1024 * 256, bytes_accessed=10 * 2**20, transcendentals=H * 2**19),
        name="attend",
    )(meta, *pieces)


def project_kernel(meta, places, *refs):
    attended, own, other, (tokens, out, lhs, held, sems) = refs[:8], refs[8:12], refs[12:16], refs[16:]
    step = pl.program_id(0)
    core, x = lax.rem(meta[0], 2), lax.rem(meta[1], 4)

    def fetch(n):
        side, zhi = divmod(n, 2)
        k = core if side == 0 else 1 - core
        copies = []
        for turn, src in enumerate(other if side else own):
            at = lax.rem(x + turn * (2 * k - 1) + 4, 4)
            for zlo in range(2):
                to = pl.ds(pl.multiple_of(zlo * 384 + at * 96, 32), 96)
                copies.append(
                    pltpu.make_async_copy(
                        src.at[pl.ds((2 * zhi + zlo) * 96, 96)], held.at[n % 2, to], sems.at[n % 2, 2 * turn + zlo]
                    )
                )
        return copies

    @pl.when(step == 0)
    def _():
        for copy in fetch(0):
            copy.start()
        for half in range(2):
            s = sign_of(half, meta[0])
            for piece, (a, b) in enumerate(MOVES):
                i = s + a * (1 - 2 * s)
                j = s + b * (1 - 2 * s)
                lhs[half * 4 + i * 2 + j] = attended[half * 4 + piece][...]

    for n in range(4):

        @pl.when(step == n)
        def _():
            for copy in fetch(n):
                copy.wait()
            if n < 3:
                for copy in fetch(n + 1):
                    copy.start()

    total = lax.dot_general(
        lhs[...].reshape(1024, HD), held[lax.rem(step, 2)], (((1,), (1,)), ((), ())), preferred_element_type=jnp.float32
    ).reshape(2, 2, 2, 2, 8, 8, TILE)
    for half in range(2):
        for i in range(2):
            block = jnp.concatenate([total[half, i, 0], total[half, i, 1]], axis=2)
            at = (slice(2 * half, 2 * half + 2), slice(8 * i, 8 * i + 8))
            out[at] = (block + tokens[at].astype(jnp.float32)).astype(jnp.bfloat16)


def project(attended, meta, places, chunks, tokens):
    grid_spec = pltpu.PrefetchScalarGridSpec(
        num_scalar_prefetch=2,
        grid=(D // TILE,),
        in_specs=[pl.BlockSpec((128, HD), lambda t, m, p: (0, 0))] * 8
        + [pl.BlockSpec(memory_space=pl.ANY)] * 8
        + [pl.BlockSpec((4, 16, 16, TILE), lambda t, m, p: (0, 0, 0, p[t]))],
        out_specs=pl.BlockSpec((4, 16, 16, TILE), lambda t, m, p: (0, 0, 0, p[t])),
        scratch_shapes=[
            pltpu.VMEM((8, 128, HD), jnp.bfloat16),
            pltpu.VMEM((2, TILE, HD), jnp.bfloat16),
            pltpu.SemaphoreType.DMA((2, 8)),
        ],
    )
    return pl.pallas_call(
        project_kernel,
        grid_spec=grid_spec,
        out_shape=jax.ShapeDtypeStruct((4, 16, 16, D), jnp.bfloat16),
        compiler_params=pltpu.CompilerParams(vmem_limit_bytes=VMEM),
        cost_estimate=pl.CostEstimate(flops=2 * 1024 * HD * D, bytes_accessed=25 * 2**20, transcendentals=0),
        name="project",
    )(meta, places, *attended, *chunks, tokens)


def ring_order(own, first, second, third, place):
    row = jnp.stack([third, second, first, own, third, second, first])
    return lax.dynamic_slice_in_dim(row, 3 - place, 4, axis=0)


def together(*values):
    return lax.optimization_barrier(values)


def local(tokens_in, queries, key_rows, value_rows, out_weight, row_valid):
    f, r, c = (lax.axis_index(a) for a in AXES)
    frame = f.astype(jnp.int32).reshape(1)
    meta = jnp.stack([f, r, c, jnp.sum(row_valid)]).astype(jnp.int32)
    core = f & 1
    places = jnp.stack([core, 2 + core, 1 - core, 3 - core]).astype(jnp.int32)
    split = lambda a: a.reshape(4, 2, 8, 2, 8, HD)
    arrays = (split(key_rows), split(value_rows), split(queries))
    shard = out_weight.T

    row, col, both = MOVES[1:]
    go = lambda value, half, move: send(value, window_pairs(half, *move))
    up = lambda value: send(value, frame_pairs(1))
    down = lambda value: send(value, frame_pairs(-1))
    swap = lambda value: send(value, core_pairs())
    turn = lambda value: send(value, shift_pairs(dx=1, opposed=True))
    back = lambda half, mixed: [mixed[0]] + [send(mixed[n], window_pairs(half, *MOVES[n], back=True)) for n in (1, 2, 3)]

    x0, y0 = pack(((0, 1, "kvq"), (0, 2, "kvq")), frame, *arrays)
    x0, y0, frame, shard = together(x0, y0, frame, shard)
    x0, y0 = go(x0, 0, row), go(y0, 0, col)
    shards = [send(shard, shift_pairs(dz=n)) for n in (1, 2, 3)]
    x1, y1 = pack(((1, 1, "kvq"), (1, 2, "kvq")), frame, *arrays)
    x1, y1, frame, *shards = together(x1, y1, frame, *shards)
    x1, y1 = go(x1, 1, row), go(y1, 1, col)
    skv0, skv1, d0, d1, sq0, sq1 = pack(
        ((0, 0, "kv"), (1, 0, "kv"), (0, 3, "kvq"), (1, 3, "kvq"), (0, 0, "q"), (1, 0, "q")), frame, *arrays
    )
    strip = ring_order(shard, *shards, (f >> 1) * 2 + (r >> 2))
    d0, x0, y0, meta, places, strip = together(d0, x0, y0, meta, places, strip)
    h0, h1 = halo_pack(skv0, x0, y0, skv1, x1, y1)
    d1, h0, h1 = together(d1, h0, h1)
    d0, d1 = go(d0, 0, both), go(d1, 1, both)
    down3, up3 = down(h0), up(h1)
    strips = [send(strip, shift_pairs(dy=n)) for n in (1, 2, 3)]
    c0 = ring_order(strip, *strips, c).swapaxes(0, 1).reshape(384, HD)
    c0, d0, d1, down3, up3 = together(c0, d0, d1, down3, up3)
    downd, upd, c1 = down(d0[:2]), up(d1[:2]), turn(c0)
    c1, downd, upd = together(c1, downd, upd)

    c2, s0, s1 = turn(c1), swap(c0), swap(c1)
    mixed1 = attend(1, meta, skv1, sq1, x1, y1, d1, down3, downd)
    c2, s0, s1, skv0, *mixed1 = together(c2, s0, s1, skv0, *mixed1)
    attended1, c3 = back(1, mixed1), turn(c2)
    s2 = swap(c2)
    mixed0 = attend(0, meta, skv0, sq0, x0, y0, d0, up3, upd)
    s2, *rest = together(s2, *attended1, *mixed0)
    attended1, mixed0 = rest[:4], rest[4:]
    attended0 = back(0, mixed0)
    c3, *attended0 = together(c3, *attended0)
    s3 = swap(c3)
    return project(attended0 + attended1, meta, places, (c0, c1, c2, c3, s0, s1, s2, s3), tokens_in)


def solution(mesh):
    return jax.shard_map(
        local,
        mesh=mesh,
        in_specs=(
            P("frame", "row", "col", None),
            P("frame", "row", "col", None),
            P("frame", "row", "col", None),
            P("frame", "row", "col", None),
            P(None, ("frame", "row", "col")),
            P(),
        ),
        out_specs=P("frame", "row", "col", None),
        check_vma=False,
    )
```

```python
import functools
import math

import jax
import jax.numpy as jnp
from jax import lax
from jax.experimental import pallas as pl
from jax.experimental.pallas import tpu as pltpu
from jax.sharding import PartitionSpec as P

D = 3072
H = 12
HS = 128
HD = 1536
F, R, C = 4, 8, 4
AXES = ("frame", "row", "col")
STEP = 2
BIG = 1e30
TILE = 768
VMEM = 56 * 1024 * 1024


def index(f, r, c):
    return ((f % F) * R + (r % R)) * C + (c % C)


def every():
    return [(f, r, c) for f in range(F) for r in range(R) for c in range(C)]


def window_pairs(half, dr, dc, back=False):
    pairs = []
    for f, r, c in every():
        step = 1 if (f + half) % 2 == 0 else -1
        here, there = index(f, r, c), index(f, r + step * dr, c + step * dc)
        pairs.append((there, here) if back else (here, there))
    return pairs


def frame_pairs(step):
    return [(index(f, r, c), index(f + step, r, c)) for f, r, c in every() if 0 <= f + step < F]


def core_pairs():
    return [(index(f, r, c), index(f ^ 1, r, c)) for f, r, c in every()]


def turn_pairs(step):
    pairs = []
    for f, r, c in every():
        zlo, x = divmod(r, 4)
        pairs.append((index(f, r, c), index(f, zlo * 4 + (x + step * (1 - 2 * (f % 2))) % 4, c)))
    return pairs


def send(value, pairs):
    return lax.ppermute(value, AXES, pairs)


MOVES = ((0, 0), (1, 0), (0, 1), (1, 1))


def sign_of(half, frame):
    return lax.rem(frame + half, 2)


def relay(moves, sems):
    inward = [pltpu.make_async_copy(src, held, sems.at[0, n]) for n, (src, held, _) in enumerate(moves)]
    outward = [pltpu.make_async_copy(held, dst, sems.at[1, n]) for n, (_, held, dst) in enumerate(moves)]
    for copy in inward:
        copy.start()
    for arrives, leaves in zip(inward, outward):
        arrives.wait()
        leaves.start()
    for copy in outward:
        copy.wait()


def pack_kernel(parts, meta, k_ref, v_ref, q_ref, *rest):
    outs, held, sems = rest[: len(parts)], rest[-2], rest[-1]
    moves = []
    for out, (half, piece, names) in zip(outs, parts):
        s = sign_of(half, meta[0])
        a, b = MOVES[piece]
        i = s + a * (1 - 2 * s)
        j = s + b * (1 - 2 * s)
        for n, name in enumerate(names):
            src = {"k": k_ref, "v": v_ref, "q": q_ref}[name]
            moves.append((src.at[pl.ds(2 * half, 2), i, :, j], held.at[len(moves)], out.at[n]))
    relay(moves, sems)


def pack(parts, meta, k, v, q):
    any_spec = pl.BlockSpec(memory_space=pl.ANY)
    count = sum(len(names) for _, _, names in parts)
    outs = pl.pallas_call(
        functools.partial(pack_kernel, parts),
        out_shape=[jax.ShapeDtypeStruct((len(names), 2, 8, 8, HD), jnp.bfloat16) for _, _, names in parts],
        in_specs=[pl.BlockSpec(memory_space=pltpu.SMEM)] + [any_spec] * 3,
        out_specs=[any_spec] * len(parts),
        scratch_shapes=[pltpu.VMEM((count, 2, 8, 8, HD), jnp.bfloat16), pltpu.SemaphoreType.DMA((2, count))],
        compiler_params=pltpu.CompilerParams(vmem_limit_bytes=VMEM),
        cost_estimate=pl.CostEstimate(flops=0, bytes_accessed=count * 2**20, transcendentals=0),
        name="pack",
    )(meta, k, v, q)
    return [o.reshape(-1, 128, HD) for o in outs]


def features(half, meta, kaug, qaug, alive):
    f, r, c, live_rows = (meta[n] for n in range(4))
    s = sign_of(half, f)
    stay = 2 * r + s
    moved = lax.rem(stay + 2 * s + 15, 16)
    row_split = r == s * (R - 1)
    col_split = c == s * (C - 1)
    missing = f == half * (F - 1)

    def places(count):
        token = lax.broadcasted_iota(jnp.int32, (count, HS), 0)
        lane = lax.broadcasted_iota(jnp.int32, (count, HS), 1)
        piece = (token // 128) % 4
        row = jnp.where(piece % 2 == 1, moved, stay) * 8 + (token // 8) % 8
        return token, lane, piece, row < live_rows

    token, lane, piece, live = places(1024)
    dead = (lane == 4) & jnp.logical_not(live)
    on = (lane == piece) | dead | ((lane == 5) & (token >= 512))
    kaug[:, HS:] = jnp.where(on, 1.0, 0.0).astype(jnp.bfloat16)
    token, lane, piece, live = places(512)
    rows_apart = (lane % 2 != piece % 2) & row_split
    cols_apart = (lane // 2 != piece // 2) & col_split
    off = ((lane < 4) & (rows_apart | cols_apart)) | (lane == 4) | ((lane == 5) & missing)
    qaug[:, HS:] = jnp.where(off, -BIG, 0.0).astype(jnp.bfloat16)
    alive[...] = jnp.where(live, 1.0, 0.0)


def attend_kernel(half, meta, skv, sq, x, y, d, h3, hd, o0, o1, o2, o3, kaug, vaug, qaug, alive):
    outs = (o0, o1, o2, o3)

    @pl.when(pl.program_id(0) == 0)
    def _():
        features(half, meta, kaug.at[0], qaug.at[0], alive)
        for n in range(1, STEP):
            kaug[n, :, HS:] = kaug[0, :, HS:]
            qaug[n, :, HS:] = qaug[0, :, HS:]
        vaug[:, :, HS:] = jnp.ones((STEP, 1024, HS), jnp.bfloat16)

    keys = (skv, x, y, d, h3.at[0], h3.at[1], h3.at[2], hd)
    asks = (sq.at[0], x.at[2], y.at[2], d.at[2])
    for h in range(STEP):
        lanes = pl.ds(h * HS, HS)
        for n, ref in enumerate(keys):
            kaug[h, pl.ds(n * 128, 128), :HS] = ref[0, :, lanes]
            vaug[h, pl.ds(n * 128, 128), :HS] = ref[1, :, lanes]
        for n, ref in enumerate(asks):
            qaug[h, pl.ds(n * 128, 128), :HS] = ref[:, lanes]
    scale = math.log2(math.e) / math.sqrt(HS)

    def score(at):
        h, part = divmod(at, 2)
        return lax.dot_general(
            qaug[h, pl.ds(part * 256, 256), :], kaug[h], (((1,), (1,)), ((), ())), preferred_element_type=jnp.float32
        )

    scores = score(0)
    for at in range(2 * STEP):
        later = score(at + 1) if at + 1 < 2 * STEP else None
        h, part = divmod(at, 2)
        lanes = pl.ds(h * HS, HS)
        top = jnp.max(scores, axis=1, keepdims=True)
        weights = jnp.exp2((scores - top) * scale).astype(jnp.bfloat16)
        mixed = jnp.dot(weights, vaug[h], preferred_element_type=jnp.float32)
        result = (mixed[:, :HS] / mixed[:, HS:] * alive[pl.ds(part * 256, 256), :]).astype(jnp.bfloat16)
        outs[2 * part][:, lanes] = result[:128]
        outs[2 * part + 1][:, lanes] = result[128:]
        scores = later


def attend(half, meta, *pieces):
    width = STEP * HS

    def spec(piece):
        lead = piece.shape[:-1]
        return pl.BlockSpec((*lead, width), lambda h: (0,) * len(lead) + (h,))

    return pl.pallas_call(
        functools.partial(attend_kernel, half),
        grid=(H // STEP,),
        out_shape=[jax.ShapeDtypeStruct((128, HD), jnp.bfloat16)] * 4,
        in_specs=[pl.BlockSpec(memory_space=pltpu.SMEM)] + [spec(piece) for piece in pieces],
        out_specs=[pl.BlockSpec((128, width), lambda h: (0, h))] * 4,
        scratch_shapes=[
            pltpu.VMEM((STEP, 1024, 2 * HS), jnp.bfloat16),
            pltpu.VMEM((STEP, 1024, 2 * HS), jnp.bfloat16),
            pltpu.VMEM((STEP, 512, 2 * HS), jnp.bfloat16),
            pltpu.VMEM((512, HS), jnp.float32),
        ],
        compiler_params=pltpu.CompilerParams(vmem_limit_bytes=VMEM),
        cost_estimate=pl.CostEstimate(flops=H * 4 * 512 * 1024 * 256, bytes_accessed=10 * 2**20, transcendentals=H * 2**19),
        name="attend",
    )(meta, *pieces)


def project_kernel(meta, places, *refs):
    attended, own, other, (tokens, out, lhs, held, sems) = refs[:8], refs[8:12], refs[12:16], refs[16:]
    step = pl.program_id(0)
    core, x = lax.rem(meta[0], 2), lax.rem(meta[1], 4)

    def fetch(n):
        side, zhi = divmod(n, 2)
        k = core if side == 0 else 1 - core
        copies = []
        for turn, src in enumerate(other if side else own):
            at = lax.rem(x + turn * (2 * k - 1) + 4, 4)
            for zlo in range(2):
                to = pl.ds(pl.multiple_of(zlo * 384 + at * 96, 32), 96)
                copies.append(
                    pltpu.make_async_copy(
                        src.at[pl.ds((2 * zhi + zlo) * 96, 96)], held.at[n % 2, to], sems.at[n % 2, 2 * turn + zlo]
                    )
                )
        return copies

    @pl.when(step == 0)
    def _():
        for copy in fetch(0):
            copy.start()
        for half in range(2):
            s = sign_of(half, meta[0])
            for piece, (a, b) in enumerate(MOVES):
                i = s + a * (1 - 2 * s)
                j = s + b * (1 - 2 * s)
                lhs[half * 4 + i * 2 + j] = attended[half * 4 + piece][...]

    for n in range(4):

        @pl.when(step == n)
        def _():
            for copy in fetch(n):
                copy.wait()
            if n < 3:
                for copy in fetch(n + 1):
                    copy.start()

    total = lax.dot_general(
        lhs[...].reshape(1024, HD), held[lax.rem(step, 2)], (((1,), (1,)), ((), ())), preferred_element_type=jnp.float32
    ).reshape(2, 2, 2, 2, 8, 8, TILE)
    for half in range(2):
        for i in range(2):
            block = jnp.concatenate([total[half, i, 0], total[half, i, 1]], axis=2)
            at = (slice(2 * half, 2 * half + 2), slice(8 * i, 8 * i + 8))
            out[at] = (block + tokens[at].astype(jnp.float32)).astype(jnp.bfloat16)


def project(attended, meta, places, chunks, tokens):
    grid_spec = pltpu.PrefetchScalarGridSpec(
        num_scalar_prefetch=2,
        grid=(D // TILE,),
        in_specs=[pl.BlockSpec((128, HD), lambda t, m, p: (0, 0))] * 8
        + [pl.BlockSpec(memory_space=pl.ANY)] * 8
        + [pl.BlockSpec((4, 16, 16, TILE), lambda t, m, p: (0, 0, 0, p[t]))],
        out_specs=pl.BlockSpec((4, 16, 16, TILE), lambda t, m, p: (0, 0, 0, p[t])),
        scratch_shapes=[
            pltpu.VMEM((8, 128, HD), jnp.bfloat16),
            pltpu.VMEM((2, TILE, HD), jnp.bfloat16),
            pltpu.SemaphoreType.DMA((2, 8)),
        ],
    )
    return pl.pallas_call(
        project_kernel,
        grid_spec=grid_spec,
        out_shape=jax.ShapeDtypeStruct((4, 16, 16, D), jnp.bfloat16),
        compiler_params=pltpu.CompilerParams(vmem_limit_bytes=VMEM),
        cost_estimate=pl.CostEstimate(flops=2 * 1024 * HD * D, bytes_accessed=25 * 2**20, transcendentals=0),
        name="project",
    )(meta, places, *attended, *chunks, tokens)


def strip_groups():
    return [
        [index(2 * zhi + core, zlo * 4 + x, c) for zhi in range(2) for zlo in range(2) for c in range(C)]
        for core in range(2)
        for x in range(4)
    ]


def together(*values):
    return lax.optimization_barrier(values)


def local(tokens_in, queries, key_rows, value_rows, out_weight, row_valid):
    f, r, c = (lax.axis_index(a) for a in AXES)
    frame = f.astype(jnp.int32).reshape(1)
    meta = jnp.stack([f, r, c, jnp.sum(row_valid)]).astype(jnp.int32)
    core = f & 1
    places = jnp.stack([core, 2 + core, 1 - core, 3 - core]).astype(jnp.int32)
    split = lambda a: a.reshape(4, 2, 8, 2, 8, HD)
    arrays = (split(key_rows), split(value_rows), split(queries))
    chunk = lax.all_gather(out_weight.T, AXES, axis=0, tiled=True, axis_index_groups=strip_groups())

    row, col, both = MOVES[1:]
    go = lambda value, half, move: send(value, window_pairs(half, *move))
    up = lambda value: send(value, frame_pairs(1))
    down = lambda value: send(value, frame_pairs(-1))
    swap = lambda value: send(value, core_pairs())
    turn = lambda value, step=1: send(value, turn_pairs(step))
    back = lambda half, mixed: [mixed[0]] + [send(mixed[n], window_pairs(half, *MOVES[n], back=True)) for n in (1, 2, 3)]

    x0, y0 = pack(((0, 1, "kvq"), (0, 2, "kvq")), frame, *arrays)
    x0, y0, frame = together(x0, y0, frame)
    x0, y0 = go(x0, 0, row), go(y0, 0, col)
    x1, y1 = pack(((1, 1, "kvq"), (1, 2, "kvq")), frame, *arrays)
    x1, y1, frame = together(x1, y1, frame)
    x1, y1 = go(x1, 1, row), go(y1, 1, col)
    skv0, skv1, d0, d1, sq0, sq1 = pack(
        ((0, 0, "kv"), (1, 0, "kv"), (0, 3, "kvq"), (1, 3, "kvq"), (0, 0, "q"), (1, 0, "q")), frame, *arrays
    )
    d0, x0, y0, meta, places = together(d0, x0, y0, meta, places)
    d1, x1, y1 = together(d1, x1, y1)
    d0, d1 = go(d0, 0, both), go(d1, 1, both)
    down3, up3 = down(jnp.stack([skv0, x0[:2], y0[:2]])), up(jnp.stack([skv1, x1[:2], y1[:2]]))
    c0, d0, d1, down3, up3 = together(chunk, d0, d1, down3, up3)
    downd, upd, c1 = down(d0[:2]), up(d1[:2]), turn(c0)
    c0, c1, downd, upd = together(c0, c1, downd, upd)

    c2, c3, s0, s1 = turn(c1), turn(c0, -1), swap(c0), swap(c1)
    mixed1 = attend(1, meta, skv1, sq1, x1, y1, d1, down3, downd)
    s0, s1, skv0, *mixed1 = together(s0, s1, skv0, *mixed1)
    attended1 = back(1, mixed1)
    mixed0 = attend(0, meta, skv0, sq0, x0, y0, d0, up3, upd)
    c2, c3, *rest = together(c2, c3, *attended1, *mixed0)
    attended1, mixed0 = rest[:4], rest[4:]
    attended0, s2, s3 = back(0, mixed0), swap(c2), swap(c3)
    return project(attended0 + attended1, meta, places, (c0, c1, c2, c3, s0, s1, s2, s3), tokens_in)


def solution(mesh):
    return jax.shard_map(
        local,
        mesh=mesh,
        in_specs=(
            P("frame", "row", "col", None),
            P("frame", "row", "col", None),
            P("frame", "row", "col", None),
            P("frame", "row", "col", None),
            P(None, ("frame", "row", "col")),
            P(),
        ),
        out_specs=P("frame", "row", "col", None),
        check_vma=False,
    )
```

```python
import functools
import math

import jax
import jax.numpy as jnp
from jax import lax
from jax.experimental import pallas as pl
from jax.experimental.pallas import tpu as pltpu
from jax.sharding import PartitionSpec as P

D = 3072
H = 12
HS = 128
HD = 1536
F, R, C = 4, 8, 4
AXES = ("frame", "row", "col")
STEP = 2
BIG = 1e30
TILE = 768
VMEM = 56 * 1024 * 1024


def index(f, r, c):
    return ((f % F) * R + (r % R)) * C + (c % C)


def every():
    return [(f, r, c) for f in range(F) for r in range(R) for c in range(C)]


def window_pairs(half, dr, dc, back=False):
    pairs = []
    for f, r, c in every():
        step = 1 if (f + half) % 2 == 0 else -1
        here, there = index(f, r, c), index(f, r + step * dr, c + step * dc)
        pairs.append((there, here) if back else (here, there))
    return pairs


def frame_pairs(step):
    return [(index(f, r, c), index(f + step, r, c)) for f, r, c in every() if 0 <= f + step < F]


def core_pairs():
    return [(index(f, r, c), index(f ^ 1, r, c)) for f, r, c in every()]


def shift_pairs(dx=0, dy=0, dz=0, opposed=False):
    pairs = []
    for f, r, c in every():
        (zhi, core), (zlo, x) = divmod(f, 2), divmod(r, 4)
        way = -1 if opposed and core else 1
        z = (2 * zhi + zlo + way * dz) % 4
        pairs.append((index(f, r, c), index((z // 2) * 2 + core, (z % 2) * 4 + (x + way * dx) % 4, c + way * dy)))
    return pairs


def send(value, pairs):
    return lax.ppermute(value, AXES, pairs)


MOVES = ((0, 0), (1, 0), (0, 1), (1, 1))


def sign_of(half, frame):
    return lax.rem(frame + half, 2)


def relay(moves, sems):
    inward = [pltpu.make_async_copy(src, held, sems.at[0, n]) for n, (src, held, _) in enumerate(moves)]
    outward = [pltpu.make_async_copy(held, dst, sems.at[1, n]) for n, (_, held, dst) in enumerate(moves)]
    for copy in inward:
        copy.start()
    for arrives, leaves in zip(inward, outward):
        arrives.wait()
        leaves.start()
    for copy in outward:
        copy.wait()


def pack_kernel(parts, meta, k_ref, v_ref, q_ref, *rest):
    outs, held, sems = rest[: len(parts)], rest[-2], rest[-1]
    moves = []
    for out, (half, piece, names) in zip(outs, parts):
        s = sign_of(half, meta[0])
        a, b = MOVES[piece]
        i = s + a * (1 - 2 * s)
        j = s + b * (1 - 2 * s)
        for n, name in enumerate(names):
            src = {"k": k_ref, "v": v_ref, "q": q_ref}[name]
            moves.append((src.at[pl.ds(2 * half, 2), i, :, j], held.at[len(moves)], out.at[n]))
    relay(moves, sems)


def pack(parts, meta, k, v, q):
    any_spec = pl.BlockSpec(memory_space=pl.ANY)
    count = sum(len(names) for _, _, names in parts)
    outs = pl.pallas_call(
        functools.partial(pack_kernel, parts),
        out_shape=[jax.ShapeDtypeStruct((len(names), 2, 8, 8, HD), jnp.bfloat16) for _, _, names in parts],
        in_specs=[pl.BlockSpec(memory_space=pltpu.SMEM)] + [any_spec] * 3,
        out_specs=[any_spec] * len(parts),
        scratch_shapes=[pltpu.VMEM((count, 2, 8, 8, HD), jnp.bfloat16), pltpu.SemaphoreType.DMA((2, count))],
        compiler_params=pltpu.CompilerParams(vmem_limit_bytes=VMEM),
        cost_estimate=pl.CostEstimate(flops=0, bytes_accessed=count * 2**20, transcendentals=0),
        name="pack",
    )(meta, k, v, q)
    return [o.reshape(-1, 128, HD) for o in outs]


def features(half, meta, kaug, qaug, alive):
    f, r, c, live_rows = (meta[n] for n in range(4))
    s = sign_of(half, f)
    stay = 2 * r + s
    moved = lax.rem(stay + 2 * s + 15, 16)
    row_split = r == s * (R - 1)
    col_split = c == s * (C - 1)
    missing = f == half * (F - 1)

    def places(count):
        token = lax.broadcasted_iota(jnp.int32, (count, HS), 0)
        lane = lax.broadcasted_iota(jnp.int32, (count, HS), 1)
        piece = (token // 128) % 4
        row = jnp.where(piece % 2 == 1, moved, stay) * 8 + (token // 8) % 8
        return token, lane, piece, row < live_rows

    token, lane, piece, live = places(1024)
    dead = (lane == 4) & jnp.logical_not(live)
    on = (lane == piece) | dead | ((lane == 5) & (token >= 512))
    kaug[:, HS:] = jnp.where(on, 1.0, 0.0).astype(jnp.bfloat16)
    token, lane, piece, live = places(512)
    rows_apart = (lane % 2 != piece % 2) & row_split
    cols_apart = (lane // 2 != piece // 2) & col_split
    off = ((lane < 4) & (rows_apart | cols_apart)) | (lane == 4) | ((lane == 5) & missing)
    qaug[:, HS:] = jnp.where(off, -BIG, 0.0).astype(jnp.bfloat16)
    alive[...] = jnp.where(live, 1.0, 0.0)


def attend_kernel(half, meta, skv, sq, x, y, d, h3, hd, o0, o1, o2, o3, kaug, vaug, qaug, alive):
    outs = (o0, o1, o2, o3)

    @pl.when(pl.program_id(0) == 0)
    def _():
        features(half, meta, kaug.at[0], qaug.at[0], alive)
        for n in range(1, STEP):
            kaug[n, :, HS:] = kaug[0, :, HS:]
            qaug[n, :, HS:] = qaug[0, :, HS:]
        vaug[:, :, HS:] = jnp.ones((STEP, 1024, HS), jnp.bfloat16)

    keys = (skv, x, y, d, h3.at[0], h3.at[1], h3.at[2], hd)
    asks = (sq.at[0], x.at[2], y.at[2], d.at[2])
    for h in range(STEP):
        lanes = pl.ds(h * HS, HS)
        for n, ref in enumerate(keys):
            kaug[h, pl.ds(n * 128, 128), :HS] = ref[0, :, lanes]
            vaug[h, pl.ds(n * 128, 128), :HS] = ref[1, :, lanes]
        for n, ref in enumerate(asks):
            qaug[h, pl.ds(n * 128, 128), :HS] = ref[:, lanes]
    scale = math.log2(math.e) / math.sqrt(HS)

    def score(at):
        h, part = divmod(at, 2)
        return lax.dot_general(
            qaug[h, pl.ds(part * 256, 256), :], kaug[h], (((1,), (1,)), ((), ())), preferred_element_type=jnp.float32
        )

    scores = score(0)
    for at in range(2 * STEP):
        later = score(at + 1) if at + 1 < 2 * STEP else None
        h, part = divmod(at, 2)
        lanes = pl.ds(h * HS, HS)
        top = jnp.max(scores, axis=1, keepdims=True)
        weights = jnp.exp2((scores - top) * scale).astype(jnp.bfloat16)
        mixed = jnp.dot(weights, vaug[h], preferred_element_type=jnp.float32)
        result = (mixed[:, :HS] / mixed[:, HS:] * alive[pl.ds(part * 256, 256), :]).astype(jnp.bfloat16)
        outs[2 * part][:, lanes] = result[:128]
        outs[2 * part + 1][:, lanes] = result[128:]
        scores = later


def attend(half, meta, *pieces):
    width = STEP * HS

    def spec(piece):
        lead = piece.shape[:-1]
        return pl.BlockSpec((*lead, width), lambda h: (0,) * len(lead) + (h,))

    return pl.pallas_call(
        functools.partial(attend_kernel, half),
        grid=(H // STEP,),
        out_shape=[jax.ShapeDtypeStruct((128, HD), jnp.bfloat16)] * 4,
        in_specs=[pl.BlockSpec(memory_space=pltpu.SMEM)] + [spec(piece) for piece in pieces],
        out_specs=[pl.BlockSpec((128, width), lambda h: (0, h))] * 4,
        scratch_shapes=[
            pltpu.VMEM((STEP, 1024, 2 * HS), jnp.bfloat16),
            pltpu.VMEM((STEP, 1024, 2 * HS), jnp.bfloat16),
            pltpu.VMEM((STEP, 512, 2 * HS), jnp.bfloat16),
            pltpu.VMEM((512, HS), jnp.float32),
        ],
        compiler_params=pltpu.CompilerParams(vmem_limit_bytes=VMEM),
        cost_estimate=pl.CostEstimate(flops=H * 4 * 512 * 1024 * 256, bytes_accessed=10 * 2**20, transcendentals=H * 2**19),
        name="attend",
    )(meta, *pieces)


def project_kernel(meta, places, *refs):
    attended, own, other, (tokens, out, lhs, held, sems) = refs[:8], refs[8:12], refs[12:16], refs[16:]
    step = pl.program_id(0)
    core, x = lax.rem(meta[0], 2), lax.rem(meta[1], 4)

    def fetch(n):
        side, zhi = divmod(n, 2)
        k = core if side == 0 else 1 - core
        copies = []
        for turn, src in enumerate(other if side else own):
            at = lax.rem(x + turn * (2 * k - 1) + 4, 4)
            for zlo in range(2):
                to = pl.ds(pl.multiple_of(zlo * 384 + at * 96, 32), 96)
                copies.append(
                    pltpu.make_async_copy(
                        src.at[pl.ds((2 * zhi + zlo) * 96, 96)], held.at[n % 2, to], sems.at[n % 2, 2 * turn + zlo]
                    )
                )
        return copies

    @pl.when(step == 0)
    def _():
        for copy in fetch(0):
            copy.start()
        for half in range(2):
            s = sign_of(half, meta[0])
            for piece, (a, b) in enumerate(MOVES):
                i = s + a * (1 - 2 * s)
                j = s + b * (1 - 2 * s)
                lhs[half * 4 + i * 2 + j] = attended[half * 4 + piece][...]

    for n in range(4):

        @pl.when(step == n)
        def _():
            for copy in fetch(n):
                copy.wait()
            if n < 3:
                for copy in fetch(n + 1):
                    copy.start()

    total = lax.dot_general(
        lhs[...].reshape(1024, HD), held[lax.rem(step, 2)], (((1,), (1,)), ((), ())), preferred_element_type=jnp.float32
    ).reshape(2, 2, 2, 2, 8, 8, TILE)
    for half in range(2):
        for i in range(2):
            block = jnp.concatenate([total[half, i, 0], total[half, i, 1]], axis=2)
            at = (slice(2 * half, 2 * half + 2), slice(8 * i, 8 * i + 8))
            out[at] = (block + tokens[at].astype(jnp.float32)).astype(jnp.bfloat16)


def project(attended, meta, places, chunks, tokens):
    grid_spec = pltpu.PrefetchScalarGridSpec(
        num_scalar_prefetch=2,
        grid=(D // TILE,),
        in_specs=[pl.BlockSpec((128, HD), lambda t, m, p: (0, 0))] * 8
        + [pl.BlockSpec(memory_space=pl.ANY)] * 8
        + [pl.BlockSpec((4, 16, 16, TILE), lambda t, m, p: (0, 0, 0, p[t]))],
        out_specs=pl.BlockSpec((4, 16, 16, TILE), lambda t, m, p: (0, 0, 0, p[t])),
        scratch_shapes=[
            pltpu.VMEM((8, 128, HD), jnp.bfloat16),
            pltpu.VMEM((2, TILE, HD), jnp.bfloat16),
            pltpu.SemaphoreType.DMA((2, 8)),
        ],
    )
    return pl.pallas_call(
        project_kernel,
        grid_spec=grid_spec,
        out_shape=jax.ShapeDtypeStruct((4, 16, 16, D), jnp.bfloat16),
        compiler_params=pltpu.CompilerParams(vmem_limit_bytes=VMEM),
        cost_estimate=pl.CostEstimate(flops=2 * 1024 * HD * D, bytes_accessed=25 * 2**20, transcendentals=0),
        name="project",
    )(meta, places, *attended, *chunks, tokens)


def ring_order(own, first, second, third, place):
    row = jnp.stack([third, second, first, own, third, second, first])
    return lax.dynamic_slice_in_dim(row, 3 - place, 4, axis=0)


def together(*values):
    return lax.optimization_barrier(values)


def local(tokens_in, queries, key_rows, value_rows, out_weight, row_valid):
    f, r, c = (lax.axis_index(a) for a in AXES)
    frame = f.astype(jnp.int32).reshape(1)
    meta = jnp.stack([f, r, c, jnp.sum(row_valid)]).astype(jnp.int32)
    core = f & 1
    places = jnp.stack([core, 2 + core, 1 - core, 3 - core]).astype(jnp.int32)
    split = lambda a: a.reshape(4, 2, 8, 2, 8, HD)
    arrays = (split(key_rows), split(value_rows), split(queries))
    shard = out_weight.T

    row, col, both = MOVES[1:]
    go = lambda value, half, move: send(value, window_pairs(half, *move))
    up = lambda value: send(value, frame_pairs(1))
    down = lambda value: send(value, frame_pairs(-1))
    swap = lambda value: send(value, core_pairs())
    turn = lambda value, step=1: send(value, shift_pairs(dx=step, opposed=True))
    back = lambda half, mixed: [mixed[0]] + [send(mixed[n], window_pairs(half, *MOVES[n], back=True)) for n in (1, 2, 3)]

    x0, y0 = pack(((0, 1, "kvq"), (0, 2, "kvq")), frame, *arrays)
    x0, y0, frame, shard = together(x0, y0, frame, shard)
    x0, y0 = go(x0, 0, row), go(y0, 0, col)
    shards = [send(shard, shift_pairs(dz=n)) for n in (1, 2, 3)]
    x1, y1 = pack(((1, 1, "kvq"), (1, 2, "kvq")), frame, *arrays)
    x1, y1, frame, *shards = together(x1, y1, frame, *shards)
    x1, y1 = go(x1, 1, row), go(y1, 1, col)
    skv0, skv1, d0, d1, sq0, sq1 = pack(
        ((0, 0, "kv"), (1, 0, "kv"), (0, 3, "kvq"), (1, 3, "kvq"), (0, 0, "q"), (1, 0, "q")), frame, *arrays
    )
    strip = ring_order(shard, *shards, (f >> 1) * 2 + (r >> 2))
    strips = [send(strip, shift_pairs(dy=n)) for n in (1, 2, 3)]
    h0, h1 = jnp.stack([skv0, x0[:2], y0[:2]]), jnp.stack([skv1, x1[:2], y1[:2]])
    d0, d1, h0, h1, x0, y0, x1, y1, meta, places, *strips = together(d0, d1, h0, h1, x0, y0, x1, y1, meta, places, *strips)
    d0, d1, down3, up3 = go(d0, 0, both), go(d1, 1, both), down(h0), up(h1)
    c0 = ring_order(strip, *strips, c).swapaxes(0, 1).reshape(384, HD)
    c0, d0, d1 = together(c0, d0, d1)
    downd, upd, c1 = down(d0[:2]), up(d1[:2]), turn(c0)
    c0, c1, downd, upd, down3, up3 = together(c0, c1, downd, upd, down3, up3)

    c2, c3, s0, s1 = turn(c1), turn(c0, -1), swap(c0), swap(c1)
    mixed1 = attend(1, meta, skv1, sq1, x1, y1, d1, down3, downd)
    s0, s1, skv0, *mixed1 = together(s0, s1, skv0, *mixed1)
    attended1 = back(1, mixed1)
    mixed0 = attend(0, meta, skv0, sq0, x0, y0, d0, up3, upd)
    c2, c3, *rest = together(c2, c3, *attended1, *mixed0)
    attended1, mixed0 = rest[:4], rest[4:]
    attended0, s2, s3 = back(0, mixed0), swap(c2), swap(c3)
    return project(attended0 + attended1, meta, places, (c0, c1, c2, c3, s0, s1, s2, s3), tokens_in)


def solution(mesh):
    return jax.shard_map(
        local,
        mesh=mesh,
        in_specs=(
            P("frame", "row", "col", None),
            P("frame", "row", "col", None),
            P("frame", "row", "col", None),
            P("frame", "row", "col", None),
            P(None, ("frame", "row", "col")),
            P(),
        ),
        out_specs=P("frame", "row", "col", None),
        check_vma=False,
    )
```

```python
import functools
import math

import jax
import jax.numpy as jnp
from jax import lax
from jax.experimental import pallas as pl
from jax.experimental.pallas import tpu as pltpu
from jax.sharding import PartitionSpec as P

D = 3072
H = 12
HS = 128
HD = 1536
F, R, C = 4, 8, 4
AXES = ("frame", "row", "col")
STEP = 2
BIG = 1e30
TILE = 768
VMEM = 56 * 1024 * 1024


def index(f, r, c):
    return ((f % F) * R + (r % R)) * C + (c % C)


def every():
    return [(f, r, c) for f in range(F) for r in range(R) for c in range(C)]


def window_pairs(half, dr, dc, back=False):
    pairs = []
    for f, r, c in every():
        step = 1 if (f + half) % 2 == 0 else -1
        here, there = index(f, r, c), index(f, r + step * dr, c + step * dc)
        pairs.append((there, here) if back else (here, there))
    return pairs


def frame_pairs(step):
    return [(index(f, r, c), index(f + step, r, c)) for f, r, c in every() if 0 <= f + step < F]


def core_pairs():
    return [(index(f, r, c), index(f ^ 1, r, c)) for f, r, c in every()]


def shift_pairs(dx=0, dy=0, dz=0, opposed=False):
    pairs = []
    for f, r, c in every():
        (zhi, core), (zlo, x) = divmod(f, 2), divmod(r, 4)
        way = -1 if opposed and core else 1
        z = (2 * zhi + zlo + way * dz) % 4
        pairs.append((index(f, r, c), index((z // 2) * 2 + core, (z % 2) * 4 + (x + way * dx) % 4, c + way * dy)))
    return pairs


def send(value, pairs):
    return lax.ppermute(value, AXES, pairs)


MOVES = ((0, 0), (1, 0), (0, 1), (1, 1))


def sign_of(half, frame):
    return lax.rem(frame + half, 2)


def relay(moves, sems):
    inward = [pltpu.make_async_copy(src, held, sems.at[0, n]) for n, (src, held, _) in enumerate(moves)]
    outward = [pltpu.make_async_copy(held, dst, sems.at[1, n]) for n, (_, held, dst) in enumerate(moves)]
    for copy in inward:
        copy.start()
    for arrives, leaves in zip(inward, outward):
        arrives.wait()
        leaves.start()
    for copy in outward:
        copy.wait()


def pack_kernel(parts, meta, k_ref, v_ref, q_ref, *rest):
    outs, held, sems = rest[: len(parts)], rest[-2], rest[-1]
    moves = []
    for out, (half, piece, names) in zip(outs, parts):
        s = sign_of(half, meta[0])
        a, b = MOVES[piece]
        i = s + a * (1 - 2 * s)
        j = s + b * (1 - 2 * s)
        for n, name in enumerate(names):
            src = {"k": k_ref, "v": v_ref, "q": q_ref}[name]
            moves.append((src.at[pl.ds(2 * half, 2), i, :, j], held.at[len(moves)], out.at[n]))
    relay(moves, sems)


def pack(parts, meta, k, v, q):
    any_spec = pl.BlockSpec(memory_space=pl.ANY)
    count = sum(len(names) for _, _, names in parts)
    outs = pl.pallas_call(
        functools.partial(pack_kernel, parts),
        out_shape=[jax.ShapeDtypeStruct((len(names), 2, 8, 8, HD), jnp.bfloat16) for _, _, names in parts],
        in_specs=[pl.BlockSpec(memory_space=pltpu.SMEM)] + [any_spec] * 3,
        out_specs=[any_spec] * len(parts),
        scratch_shapes=[pltpu.VMEM((count, 2, 8, 8, HD), jnp.bfloat16), pltpu.SemaphoreType.DMA((2, count))],
        compiler_params=pltpu.CompilerParams(vmem_limit_bytes=VMEM),
        cost_estimate=pl.CostEstimate(flops=0, bytes_accessed=count * 2**20, transcendentals=0),
        name="pack",
    )(meta, k, v, q)
    return [o.reshape(-1, 128, HD) for o in outs]


def features(half, meta, kaug, qaug, alive):
    f, r, c, live_rows = (meta[n] for n in range(4))
    s = sign_of(half, f)
    stay = 2 * r + s
    moved = lax.rem(stay + 2 * s + 15, 16)
    row_split = r == s * (R - 1)
    col_split = c == s * (C - 1)
    missing = f == half * (F - 1)

    def places(count):
        token = lax.broadcasted_iota(jnp.int32, (count, HS), 0)
        lane = lax.broadcasted_iota(jnp.int32, (count, HS), 1)
        piece = (token // 128) % 4
        row = jnp.where(piece % 2 == 1, moved, stay) * 8 + (token // 8) % 8
        return token, lane, piece, row < live_rows

    token, lane, piece, live = places(1024)
    dead = (lane == 4) & jnp.logical_not(live)
    on = (lane == piece) | dead | ((lane == 5) & (token >= 512))
    kaug[:, HS:] = jnp.where(on, 1.0, 0.0).astype(jnp.bfloat16)
    token, lane, piece, live = places(512)
    rows_apart = (lane % 2 != piece % 2) & row_split
    cols_apart = (lane // 2 != piece // 2) & col_split
    off = ((lane < 4) & (rows_apart | cols_apart)) | (lane == 4) | ((lane == 5) & missing)
    qaug[:, HS:] = jnp.where(off, -BIG, 0.0).astype(jnp.bfloat16)
    alive[...] = jnp.where(live, 1.0, 0.0)


def attend_kernel(half, meta, skv, sq, x, y, d, h3, hd, o0, o1, o2, o3, kaug, vaug, qaug, alive):
    outs = (o0, o1, o2, o3)

    @pl.when(pl.program_id(0) == 0)
    def _():
        features(half, meta, kaug.at[0], qaug.at[0], alive)
        for n in range(1, STEP):
            kaug[n, :, HS:] = kaug[0, :, HS:]
            qaug[n, :, HS:] = qaug[0, :, HS:]
        vaug[:, :, HS:] = jnp.ones((STEP, 1024, HS), jnp.bfloat16)

    keys = (skv, x, y, d, h3.at[0], h3.at[1], h3.at[2], hd)
    asks = (sq.at[0], x.at[2], y.at[2], d.at[2])
    for h in range(STEP):
        lanes = pl.ds(h * HS, HS)
        for n, ref in enumerate(keys):
            kaug[h, pl.ds(n * 128, 128), :HS] = ref[0, :, lanes]
            vaug[h, pl.ds(n * 128, 128), :HS] = ref[1, :, lanes]
        for n, ref in enumerate(asks):
            qaug[h, pl.ds(n * 128, 128), :HS] = ref[:, lanes]
    scale = math.log2(math.e) / math.sqrt(HS)

    def score(at):
        h, part = divmod(at, 2)
        return lax.dot_general(
            qaug[h, pl.ds(part * 256, 256), :], kaug[h], (((1,), (1,)), ((), ())), preferred_element_type=jnp.float32
        )

    scores = score(0)
    for at in range(2 * STEP):
        later = score(at + 1) if at + 1 < 2 * STEP else None
        h, part = divmod(at, 2)
        lanes = pl.ds(h * HS, HS)
        top = jnp.max(scores, axis=1, keepdims=True)
        weights = jnp.exp2((scores - top) * scale).astype(jnp.bfloat16)
        mixed = jnp.dot(weights, vaug[h], preferred_element_type=jnp.float32)
        result = (mixed[:, :HS] / mixed[:, HS:] * alive[pl.ds(part * 256, 256), :]).astype(jnp.bfloat16)
        outs[2 * part][:, lanes] = result[:128]
        outs[2 * part + 1][:, lanes] = result[128:]
        scores = later


def attend(half, meta, *pieces):
    width = STEP * HS

    def spec(piece):
        lead = piece.shape[:-1]
        return pl.BlockSpec((*lead, width), lambda h: (0,) * len(lead) + (h,))

    return pl.pallas_call(
        functools.partial(attend_kernel, half),
        grid=(H // STEP,),
        out_shape=[jax.ShapeDtypeStruct((128, HD), jnp.bfloat16)] * 4,
        in_specs=[pl.BlockSpec(memory_space=pltpu.SMEM)] + [spec(piece) for piece in pieces],
        out_specs=[pl.BlockSpec((128, width), lambda h: (0, h))] * 4,
        scratch_shapes=[
            pltpu.VMEM((STEP, 1024, 2 * HS), jnp.bfloat16),
            pltpu.VMEM((STEP, 1024, 2 * HS), jnp.bfloat16),
            pltpu.VMEM((STEP, 512, 2 * HS), jnp.bfloat16),
            pltpu.VMEM((512, HS), jnp.float32),
        ],
        compiler_params=pltpu.CompilerParams(vmem_limit_bytes=VMEM),
        cost_estimate=pl.CostEstimate(flops=H * 4 * 512 * 1024 * 256, bytes_accessed=10 * 2**20, transcendentals=H * 2**19),
        name="attend",
    )(meta, *pieces)


def project_kernel(half, meta, places, *refs):
    attended, own, other, tokens = refs[:4], refs[4:8], refs[8:12], refs[12]
    out, lhs, held, sems = refs[-4:]
    step = pl.program_id(0)
    core, x = lax.rem(meta[0], 2), lax.rem(meta[1], 4)

    def fetch(n):
        side, zhi = divmod(n, 2)
        k = core if side == 0 else 1 - core
        copies = []
        for turn, src in enumerate(other if side else own):
            at = lax.rem(x + turn * (2 * k - 1) + 4, 4)
            for zlo in range(2):
                to = pl.ds(pl.multiple_of(zlo * 384 + at * 96, 32), 96)
                copies.append(
                    pltpu.make_async_copy(
                        src.at[pl.ds((2 * zhi + zlo) * 96, 96)], held.at[n % 2, to], sems.at[n % 2, 2 * turn + zlo]
                    )
                )
        return copies

    @pl.when(step == 0)
    def _():
        for copy in fetch(0):
            copy.start()
        s = sign_of(half, meta[0])
        for piece, (a, b) in enumerate(MOVES):
            i = s + a * (1 - 2 * s)
            j = s + b * (1 - 2 * s)
            lhs[i * 2 + j] = attended[piece][...]

    for n in range(4):

        @pl.when(step == n)
        def _():
            for copy in fetch(n):
                copy.wait()
            if n < 3:
                for copy in fetch(n + 1):
                    copy.start()

    total = lax.dot_general(
        lhs[...].reshape(512, HD), held[lax.rem(step, 2)], (((1,), (1,)), ((), ())), preferred_element_type=jnp.float32
    ).reshape(2, 2, 2, 8, 8, TILE)
    for i in range(2):
        block = jnp.concatenate([total[i, 0], total[i, 1]], axis=2)
        at = (slice(0, 2), slice(8 * i, 8 * i + 8))
        out[at] = (block + tokens[at].astype(jnp.float32)).astype(jnp.bfloat16)


def project(half, attended, meta, places, chunks, tokens, partial=None):
    extra = [] if partial is None else [partial]
    block = pl.BlockSpec((2, 16, 16, TILE), lambda t, m, p: (half, 0, 0, p[t]))
    grid_spec = pltpu.PrefetchScalarGridSpec(
        num_scalar_prefetch=2,
        grid=(D // TILE,),
        in_specs=[pl.BlockSpec((128, HD), lambda t, m, p: (0, 0))] * 4
        + [pl.BlockSpec(memory_space=pl.ANY)] * 8
        + [block]
        + [pl.BlockSpec(memory_space=pl.ANY)] * len(extra),
        out_specs=block,
        scratch_shapes=[
            pltpu.VMEM((4, 128, HD), jnp.bfloat16),
            pltpu.VMEM((2, TILE, HD), jnp.bfloat16),
            pltpu.SemaphoreType.DMA((2, 8)),
        ],
    )
    return pl.pallas_call(
        functools.partial(project_kernel, half),
        grid_spec=grid_spec,
        out_shape=jax.ShapeDtypeStruct((4, 16, 16, D), jnp.bfloat16),
        input_output_aliases={} if partial is None else {15: 0},
        compiler_params=pltpu.CompilerParams(vmem_limit_bytes=VMEM),
        cost_estimate=pl.CostEstimate(flops=1024 * HD * D, bytes_accessed=17 * 2**20, transcendentals=0),
        name="project",
    )(meta, places, *attended, *chunks, tokens, *extra)


def ring_order(own, first, second, third, place):
    row = jnp.stack([third, second, first, own, third, second, first])
    return lax.dynamic_slice_in_dim(row, 3 - place, 4, axis=0)


def together(*values):
    return lax.optimization_barrier(values)


def local(tokens_in, queries, key_rows, value_rows, out_weight, row_valid):
    f, r, c = (lax.axis_index(a) for a in AXES)
    frame = f.astype(jnp.int32).reshape(1)
    meta = jnp.stack([f, r, c, jnp.sum(row_valid)]).astype(jnp.int32)
    core = f & 1
    places = jnp.stack([core, 2 + core, 1 - core, 3 - core]).astype(jnp.int32)
    split = lambda a: a.reshape(4, 2, 8, 2, 8, HD)
    arrays = (split(key_rows), split(value_rows), split(queries))
    shard = out_weight.T

    row, col, both = MOVES[1:]
    go = lambda value, half, move: send(value, window_pairs(half, *move))
    up = lambda value: send(value, frame_pairs(1))
    down = lambda value: send(value, frame_pairs(-1))
    swap = lambda value: send(value, core_pairs())
    turn = lambda value, step=1: send(value, shift_pairs(dx=step, opposed=True))
    back = lambda half, mixed: [mixed[0]] + [send(mixed[n], window_pairs(half, *MOVES[n], back=True)) for n in (1, 2, 3)]

    x0, y0 = pack(((0, 1, "kvq"), (0, 2, "kvq")), frame, *arrays)
    x0, y0, frame, shard = together(x0, y0, frame, shard)
    x0, y0 = go(x0, 0, row), go(y0, 0, col)
    shards = [send(shard, shift_pairs(dz=n)) for n in (1, 2, 3)]
    x1, y1 = pack(((1, 1, "kvq"), (1, 2, "kvq")), frame, *arrays)
    x1, y1, frame, *shards = together(x1, y1, frame, *shards)
    x1, y1 = go(x1, 1, row), go(y1, 1, col)
    skv0, skv1, d0, d1, sq0, sq1 = pack(
        ((0, 0, "kv"), (1, 0, "kv"), (0, 3, "kvq"), (1, 3, "kvq"), (0, 0, "q"), (1, 0, "q")), frame, *arrays
    )
    strip = ring_order(shard, *shards, (f >> 1) * 2 + (r >> 2))
    h0, h1 = jnp.stack([skv0, x0[:2], y0[:2]]), jnp.stack([skv1, x1[:2], y1[:2]])
    d0, d1, h0, h1, x0, y0, x1, y1, meta, places, strip = together(d0, d1, h0, h1, x0, y0, x1, y1, meta, places, strip)
    d0, d1, down3, up3 = go(d0, 0, both), go(d1, 1, both), down(h0), up(h1)
    strips = lax.all_gather(strip.reshape(96, HD), "col", axis=0, tiled=True)
    c0 = strips.reshape(4, 4, 24, HD).swapaxes(0, 1).reshape(384, HD)
    c0, d0, d1 = together(c0, d0, d1)
    downd, upd, c1 = down(d0[:2]), up(d1[:2]), turn(c0)
    c0, c1, downd, upd, down3, up3 = together(c0, c1, downd, upd, down3, up3)

    c2, c3, s0, s1 = turn(c1), turn(c0, -1), swap(c0), swap(c1)
    mixed1 = attend(1, meta, skv1, sq1, x1, y1, d1, down3, downd)
    s0, s1, skv0, *mixed1 = together(s0, s1, skv0, *mixed1)
    attended1 = back(1, mixed1)
    mixed0 = attend(0, meta, skv0, sq0, x0, y0, d0, up3, upd)
    c2, c3, *rest = together(c2, c3, *attended1, *mixed0)
    attended1, mixed0 = rest[:4], rest[4:]
    attended0, s2, s3 = back(0, mixed0), swap(c2), swap(c3)
    chunks = (c0, c1, c2, c3, s0, s1, s2, s3)
    out = project(1, attended1, meta, places, chunks, tokens_in)
    return project(0, attended0, meta, places, chunks, tokens_in, out)


def solution(mesh):
    return jax.shard_map(
        local,
        mesh=mesh,
        in_specs=(
            P("frame", "row", "col", None),
            P("frame", "row", "col", None),
            P("frame", "row", "col", None),
            P("frame", "row", "col", None),
            P(None, ("frame", "row", "col")),
            P(),
        ),
        out_specs=P("frame", "row", "col", None),
        check_vma=False,
    )
```

```python
import functools
import math

import jax
import jax.numpy as jnp
from jax import lax
from jax.experimental import pallas as pl
from jax.experimental.pallas import tpu as pltpu
from jax.sharding import PartitionSpec as P

D = 3072
H = 12
HS = 128
HD = 1536
F, R, C = 4, 8, 4
AXES = ("frame", "row", "col")
STEP = 2
BIG = 1e30
TILE = 768
VMEM = 56 * 1024 * 1024


def index(f, r, c):
    return ((f % F) * R + (r % R)) * C + (c % C)


def every():
    return [(f, r, c) for f in range(F) for r in range(R) for c in range(C)]


def window_pairs(half, dr, dc, back=False):
    pairs = []
    for f, r, c in every():
        step = 1 if (f + half) % 2 == 0 else -1
        here, there = index(f, r, c), index(f, r + step * dr, c + step * dc)
        pairs.append((there, here) if back else (here, there))
    return pairs


def frame_pairs(step):
    return [(index(f, r, c), index(f + step, r, c)) for f, r, c in every() if 0 <= f + step < F]


def core_pairs():
    return [(index(f, r, c), index(f ^ 1, r, c)) for f, r, c in every()]


def shift_pairs(dx=0, dy=0, dz=0, opposed=False):
    pairs = []
    for f, r, c in every():
        (zhi, core), (zlo, x) = divmod(f, 2), divmod(r, 4)
        way = -1 if opposed and core else 1
        z = (2 * zhi + zlo + way * dz) % 4
        pairs.append((index(f, r, c), index((z // 2) * 2 + core, (z % 2) * 4 + (x + way * dx) % 4, c + way * dy)))
    return pairs


def send(value, pairs):
    return lax.ppermute(value, AXES, pairs)


MOVES = ((0, 0), (1, 0), (0, 1), (1, 1))


def sign_of(half, frame):
    return lax.rem(frame + half, 2)


def relay(moves, sems):
    inward = [pltpu.make_async_copy(src, held, sems.at[0, n]) for n, (src, held, _) in enumerate(moves)]
    outward = [pltpu.make_async_copy(held, dst, sems.at[1, n]) for n, (_, held, dst) in enumerate(moves)]
    for copy in inward:
        copy.start()
    for arrives, leaves in zip(inward, outward):
        arrives.wait()
        leaves.start()
    for copy in outward:
        copy.wait()


def pack_kernel(parts, meta, k_ref, v_ref, q_ref, *rest):
    outs, held, sems = rest[: len(parts)], rest[-2], rest[-1]
    moves = []
    for out, (half, piece, names) in zip(outs, parts):
        s = sign_of(half, meta[0])
        a, b = MOVES[piece]
        i = s + a * (1 - 2 * s)
        j = s + b * (1 - 2 * s)
        for n, name in enumerate(names):
            src = {"k": k_ref, "v": v_ref, "q": q_ref}[name]
            moves.append((src.at[pl.ds(2 * half, 2), i, :, j], held.at[len(moves)], out.at[n]))
    relay(moves, sems)


def pack(parts, meta, k, v, q):
    any_spec = pl.BlockSpec(memory_space=pl.ANY)
    count = sum(len(names) for _, _, names in parts)
    outs = pl.pallas_call(
        functools.partial(pack_kernel, parts),
        out_shape=[jax.ShapeDtypeStruct((len(names), 2, 8, 8, HD), jnp.bfloat16) for _, _, names in parts],
        in_specs=[pl.BlockSpec(memory_space=pltpu.SMEM)] + [any_spec] * 3,
        out_specs=[any_spec] * len(parts),
        scratch_shapes=[pltpu.VMEM((count, 2, 8, 8, HD), jnp.bfloat16), pltpu.SemaphoreType.DMA((2, count))],
        compiler_params=pltpu.CompilerParams(vmem_limit_bytes=VMEM),
        cost_estimate=pl.CostEstimate(flops=0, bytes_accessed=count * 2**20, transcendentals=0),
        name="pack",
    )(meta, k, v, q)
    return [o.reshape(-1, 128, HD) for o in outs]


def features(half, meta, kaug, qaug, alive):
    f, r, c, live_rows = (meta[n] for n in range(4))
    s = sign_of(half, f)
    stay = 2 * r + s
    moved = lax.rem(stay + 2 * s + 15, 16)
    row_split = r == s * (R - 1)
    col_split = c == s * (C - 1)
    missing = f == half * (F - 1)

    def places(count):
        token = lax.broadcasted_iota(jnp.int32, (count, HS), 0)
        lane = lax.broadcasted_iota(jnp.int32, (count, HS), 1)
        piece = (token // 128) % 4
        row = jnp.where(piece % 2 == 1, moved, stay) * 8 + (token // 8) % 8
        return token, lane, piece, row < live_rows

    token, lane, piece, live = places(1024)
    dead = (lane == 4) & jnp.logical_not(live)
    on = (lane == piece) | dead | ((lane == 5) & (token >= 512))
    kaug[:, HS:] = jnp.where(on, 1.0, 0.0).astype(jnp.bfloat16)
    token, lane, piece, live = places(512)
    rows_apart = (lane % 2 != piece % 2) & row_split
    cols_apart = (lane // 2 != piece // 2) & col_split
    off = ((lane < 4) & (rows_apart | cols_apart)) | (lane == 4) | ((lane == 5) & missing)
    qaug[:, HS:] = jnp.where(off, -BIG, 0.0).astype(jnp.bfloat16)
    alive[...] = jnp.where(live, 1.0, 0.0)


def attend_kernel(half, meta, skv, sq, x, y, d, hs, h2, hd, o0, o1, o2, o3, kaug, vaug, qaug, alive):
    outs = (o0, o1, o2, o3)

    @pl.when(pl.program_id(0) == 0)
    def _():
        features(half, meta, kaug.at[0], qaug.at[0], alive)
        for n in range(1, STEP):
            kaug[n, :, HS:] = kaug[0, :, HS:]
            qaug[n, :, HS:] = qaug[0, :, HS:]
        vaug[:, :, HS:] = jnp.ones((STEP, 1024, HS), jnp.bfloat16)

    keys = (skv, x, y, d, hs, h2.at[0], h2.at[1], hd)
    asks = (sq.at[0], x.at[2], y.at[2], d.at[2])
    for h in range(STEP):
        lanes = pl.ds(h * HS, HS)
        for n, ref in enumerate(keys):
            kaug[h, pl.ds(n * 128, 128), :HS] = ref[0, :, lanes]
            vaug[h, pl.ds(n * 128, 128), :HS] = ref[1, :, lanes]
        for n, ref in enumerate(asks):
            qaug[h, pl.ds(n * 128, 128), :HS] = ref[:, lanes]
    scale = math.log2(math.e) / math.sqrt(HS)

    def score(at):
        h, part = divmod(at, 2)
        return lax.dot_general(
            qaug[h, pl.ds(part * 256, 256), :], kaug[h], (((1,), (1,)), ((), ())), preferred_element_type=jnp.float32
        )

    scores = score(0)
    for at in range(2 * STEP):
        later = score(at + 1) if at + 1 < 2 * STEP else None
        h, part = divmod(at, 2)
        lanes = pl.ds(h * HS, HS)
        top = jnp.max(scores, axis=1, keepdims=True)
        weights = jnp.exp2((scores - top) * scale).astype(jnp.bfloat16)
        mixed = jnp.dot(weights, vaug[h], preferred_element_type=jnp.float32)
        result = (mixed[:, :HS] / mixed[:, HS:] * alive[pl.ds(part * 256, 256), :]).astype(jnp.bfloat16)
        outs[2 * part][:, lanes] = result[:128]
        outs[2 * part + 1][:, lanes] = result[128:]
        scores = later


def attend(half, meta, *pieces):
    width = STEP * HS

    def spec(piece):
        lead = piece.shape[:-1]
        return pl.BlockSpec((*lead, width), lambda h: (0,) * len(lead) + (h,))

    return pl.pallas_call(
        functools.partial(attend_kernel, half),
        grid=(H // STEP,),
        out_shape=[jax.ShapeDtypeStruct((128, HD), jnp.bfloat16)] * 4,
        in_specs=[pl.BlockSpec(memory_space=pltpu.SMEM)] + [spec(piece) for piece in pieces],
        out_specs=[pl.BlockSpec((128, width), lambda h: (0, h))] * 4,
        scratch_shapes=[
            pltpu.VMEM((STEP, 1024, 2 * HS), jnp.bfloat16),
            pltpu.VMEM((STEP, 1024, 2 * HS), jnp.bfloat16),
            pltpu.VMEM((STEP, 512, 2 * HS), jnp.bfloat16),
            pltpu.VMEM((512, HS), jnp.float32),
        ],
        compiler_params=pltpu.CompilerParams(vmem_limit_bytes=VMEM),
        cost_estimate=pl.CostEstimate(flops=H * 4 * 512 * 1024 * 256, bytes_accessed=10 * 2**20, transcendentals=H * 2**19),
        name="attend",
    )(meta, *pieces)


def project_kernel(half, meta, places, *refs):
    attended, own, other, tokens = refs[:4], refs[4:8], refs[8:12], refs[12]
    out, lhs, held, sems = refs[-4:]
    step = pl.program_id(0)
    core, x = lax.rem(meta[0], 2), lax.rem(meta[1], 4)

    def fetch(n):
        side, zhi = divmod(n, 2)
        k = core if side == 0 else 1 - core
        copies = []
        for turn, src in enumerate(other if side else own):
            at = lax.rem(x + turn * (2 * k - 1) + 4, 4)
            for zlo in range(2):
                to = pl.ds(pl.multiple_of(zlo * 384 + at * 96, 32), 96)
                copies.append(
                    pltpu.make_async_copy(
                        src.at[pl.ds((2 * zhi + zlo) * 96, 96)], held.at[n % 2, to], sems.at[n % 2, 2 * turn + zlo]
                    )
                )
        return copies

    @pl.when(step == 0)
    def _():
        for copy in fetch(0):
            copy.start()
        ahead = sign_of(half, meta[0]) == 0
        pieces = [piece[...].astype(jnp.float32).reshape(2, 8, 8, HD) for piece in attended]
        for i in range(2):
            left = jnp.where(ahead, pieces[i], pieces[3 - i])
            right = jnp.where(ahead, pieces[2 + i], pieces[1 - i])
            lhs[:, 8 * i : 8 * i + 8] = jnp.concatenate([left, right], axis=2).astype(jnp.bfloat16)

    for n in range(4):

        @pl.when(step == n)
        def _():
            for copy in fetch(n):
                copy.wait()
            if n < 3:
                for copy in fetch(n + 1):
                    copy.start()

    total = lax.dot_general(
        lhs[...].reshape(512, HD), held[lax.rem(step, 2)], (((1,), (1,)), ((), ())), preferred_element_type=jnp.float32
    ).reshape(2, 16, 16, TILE)
    out[...] = (total + tokens[...].astype(jnp.float32)).astype(jnp.bfloat16)


def project(half, attended, meta, places, chunks, tokens, partial=None):
    extra = [] if partial is None else [partial]
    block = pl.BlockSpec((2, 16, 16, TILE), lambda t, m, p: (half, 0, 0, p[t]))
    grid_spec = pltpu.PrefetchScalarGridSpec(
        num_scalar_prefetch=2,
        grid=(D // TILE,),
        in_specs=[pl.BlockSpec((128, HD), lambda t, m, p: (0, 0))] * 4
        + [pl.BlockSpec(memory_space=pl.ANY)] * 8
        + [block]
        + [pl.BlockSpec(memory_space=pl.ANY)] * len(extra),
        out_specs=block,
        scratch_shapes=[
            pltpu.VMEM((2, 16, 16, HD), jnp.bfloat16),
            pltpu.VMEM((2, TILE, HD), jnp.bfloat16),
            pltpu.SemaphoreType.DMA((2, 8)),
        ],
    )
    return pl.pallas_call(
        functools.partial(project_kernel, half),
        grid_spec=grid_spec,
        out_shape=jax.ShapeDtypeStruct((4, 16, 16, D), jnp.bfloat16),
        input_output_aliases={} if partial is None else {15: 0},
        compiler_params=pltpu.CompilerParams(vmem_limit_bytes=VMEM),
        cost_estimate=pl.CostEstimate(flops=1024 * HD * D, bytes_accessed=17 * 2**20, transcendentals=0),
        name="project",
    )(meta, places, *attended, *chunks, tokens, *extra)


def ring_order(own, first, second, third, place):
    row = jnp.stack([third, second, first, own, third, second, first])
    return lax.dynamic_slice_in_dim(row, 3 - place, 4, axis=0)


def together(*values):
    return lax.optimization_barrier(values)


def local(tokens_in, queries, key_rows, value_rows, out_weight, row_valid):
    f, r, c = (lax.axis_index(a) for a in AXES)
    frame = f.astype(jnp.int32).reshape(1)
    meta = jnp.stack([f, r, c, jnp.sum(row_valid)]).astype(jnp.int32)
    core = f & 1
    places = jnp.stack([core, 2 + core, 1 - core, 3 - core]).astype(jnp.int32)
    split = lambda a: a.reshape(4, 2, 8, 2, 8, HD)
    arrays = (split(key_rows), split(value_rows), split(queries))
    shard = out_weight.T

    row, col, both = MOVES[1:]
    go = lambda value, half, move: send(value, window_pairs(half, *move))
    up = lambda value: send(value, frame_pairs(1))
    down = lambda value: send(value, frame_pairs(-1))
    swap = lambda value: send(value, core_pairs())
    turn = lambda value, step=1: send(value, shift_pairs(dx=step, opposed=True))
    back = lambda half, mixed: [mixed[0]] + [send(mixed[n], window_pairs(half, *MOVES[n], back=True)) for n in (1, 2, 3)]

    x0, y0 = pack(((0, 1, "kvq"), (0, 2, "kvq")), frame, *arrays)
    x0, y0, frame, shard = together(x0, y0, frame, shard)
    x0, y0 = go(x0, 0, row), go(y0, 0, col)
    shards = [send(shard, shift_pairs(dz=n)) for n in (1, 2, 3)]
    skv0, skv1, x1, y1 = pack(((0, 0, "kv"), (1, 0, "kv"), (1, 1, "kvq"), (1, 2, "kvq")), frame, *arrays)
    skv0, skv1, x1, y1, frame = together(skv0, skv1, x1, y1, frame)
    downs, ups = down(skv0), up(skv1)
    x1, x0 = together(x1, x0)
    y1, y0 = together(y1, y0)
    x1, y1 = go(x1, 1, row), go(y1, 1, col)
    d0, d1, sq0, sq1 = pack(((0, 3, "kvq"), (1, 3, "kvq"), (0, 0, "q"), (1, 0, "q")), frame, *arrays)
    strip = ring_order(shard, *shards, (f >> 1) * 2 + (r >> 2))
    h0, h1 = jnp.stack([x0[:2], y0[:2]]), jnp.stack([x1[:2], y1[:2]])
    d0, d1, h0, h1, x0, y0, x1, y1, downs, ups, meta, places, strip = together(
        d0, d1, h0, h1, x0, y0, x1, y1, downs, ups, meta, places, strip
    )
    d0, d1, down2, up2 = go(d0, 0, both), go(d1, 1, both), down(h0), up(h1)
    strips = lax.all_gather(strip.reshape(96, HD), "col", axis=0, tiled=True)
    c0 = strips.reshape(4, 4, 24, HD).swapaxes(0, 1).reshape(384, HD)
    c0, d0, d1 = together(c0, d0, d1)
    downd, upd, c1 = down(d0[:2]), up(d1[:2]), turn(c0)
    c0, c1, downd, upd, down2, up2 = together(c0, c1, downd, upd, down2, up2)

    c2, c3, s0, s1 = turn(c1), turn(c0, -1), swap(c0), swap(c1)
    mixed1 = attend(1, meta, skv1, sq1, x1, y1, d1, downs, down2, downd)
    s0, s1, skv0, *mixed1 = together(s0, s1, skv0, *mixed1)
    attended1 = back(1, mixed1)
    mixed0 = attend(0, meta, skv0, sq0, x0, y0, d0, ups, up2, upd)
    c2, c3, *rest = together(c2, c3, *attended1, *mixed0)
    attended1, mixed0 = rest[:4], rest[4:]
    attended0, s2, s3 = back(0, mixed0), swap(c2), swap(c3)
    chunks = (c0, c1, c2, c3, s0, s1, s2, s3)
    out = project(1, attended1, meta, places, chunks, tokens_in)
    return project(0, attended0, meta, places, chunks, tokens_in, out)


def solution(mesh):
    return jax.shard_map(
        local,
        mesh=mesh,
        in_specs=(
            P("frame", "row", "col", None),
            P("frame", "row", "col", None),
            P("frame", "row", "col", None),
            P("frame", "row", "col", None),
            P(None, ("frame", "row", "col")),
            P(),
        ),
        out_specs=P("frame", "row", "col", None),
        check_vma=False,
    )
```

```python
import functools
import math

import jax
import jax.numpy as jnp
from jax import lax
from jax.experimental import pallas as pl
from jax.experimental.pallas import tpu as pltpu
from jax.sharding import PartitionSpec as P

D = 3072
H = 12
HS = 128
HD = 1536
F, R, C = 4, 8, 4
AXES = ("frame", "row", "col")
STEP = 2
BIG = 1e30
TILE = 768
VMEM = 56 * 1024 * 1024


def index(f, r, c):
    return ((f % F) * R + (r % R)) * C + (c % C)


def every():
    return [(f, r, c) for f in range(F) for r in range(R) for c in range(C)]


def window_pairs(half, dr, dc, back=False):
    pairs = []
    for f, r, c in every():
        step = 1 if (f + half) % 2 == 0 else -1
        here, there = index(f, r, c), index(f, r + step * dr, c + step * dc)
        pairs.append((there, here) if back else (here, there))
    return pairs


def frame_pairs(step):
    return [(index(f, r, c), index(f + step, r, c)) for f, r, c in every() if 0 <= f + step < F]


def core_pairs():
    return [(index(f, r, c), index(f ^ 1, r, c)) for f, r, c in every()]


def shift_pairs(dx=0, dy=0, dz=0, opposed=False):
    pairs = []
    for f, r, c in every():
        (zhi, core), (zlo, x) = divmod(f, 2), divmod(r, 4)
        way = -1 if opposed and core else 1
        z = (2 * zhi + zlo + way * dz) % 4
        pairs.append((index(f, r, c), index((z // 2) * 2 + core, (z % 2) * 4 + (x + way * dx) % 4, c + way * dy)))
    return pairs


def send(value, pairs):
    return lax.ppermute(value, AXES, pairs)


MOVES = ((0, 0), (1, 0), (0, 1), (1, 1))


def sign_of(half, frame):
    return lax.rem(frame + half, 2)


def relay(moves, sems):
    inward = [pltpu.make_async_copy(src, held, sems.at[0, n]) for n, (src, held, _) in enumerate(moves)]
    outward = [pltpu.make_async_copy(held, dst, sems.at[1, n]) for n, (_, held, dst) in enumerate(moves)]
    for copy in inward:
        copy.start()
    for arrives, leaves in zip(inward, outward):
        arrives.wait()
        leaves.start()
    for copy in outward:
        copy.wait()


def pack_kernel(parts, meta, k_ref, v_ref, q_ref, *rest):
    outs, held, sems = rest[: len(parts)], rest[-2], rest[-1]
    moves = []
    for out, (half, piece, names) in zip(outs, parts):
        s = sign_of(half, meta[0])
        a, b = MOVES[piece]
        i = s + a * (1 - 2 * s)
        j = s + b * (1 - 2 * s)
        for n, name in enumerate(names):
            src = {"k": k_ref, "v": v_ref, "q": q_ref}[name]
            moves.append((src.at[pl.ds(2 * half, 2), i, :, j], held.at[len(moves)], out.at[n]))
    relay(moves, sems)


def pack(parts, meta, k, v, q):
    any_spec = pl.BlockSpec(memory_space=pl.ANY)
    count = sum(len(names) for _, _, names in parts)
    outs = pl.pallas_call(
        functools.partial(pack_kernel, parts),
        out_shape=[jax.ShapeDtypeStruct((len(names), 2, 8, 8, HD), jnp.bfloat16) for _, _, names in parts],
        in_specs=[pl.BlockSpec(memory_space=pltpu.SMEM)] + [any_spec] * 3,
        out_specs=[any_spec] * len(parts),
        scratch_shapes=[pltpu.VMEM((count, 2, 8, 8, HD), jnp.bfloat16), pltpu.SemaphoreType.DMA((2, count))],
        compiler_params=pltpu.CompilerParams(vmem_limit_bytes=VMEM),
        cost_estimate=pl.CostEstimate(flops=0, bytes_accessed=count * 2**20, transcendentals=0),
        name="pack",
    )(meta, k, v, q)
    return [o.reshape(-1, 128, HD) for o in outs]


def features(half, meta, kaug, qaug, alive):
    f, r, c, live_rows = (meta[n] for n in range(4))
    s = sign_of(half, f)
    stay = 2 * r + s
    moved = lax.rem(stay + 2 * s + 15, 16)
    row_split = r == s * (R - 1)
    col_split = c == s * (C - 1)
    missing = f == half * (F - 1)

    def places(count):
        token = lax.broadcasted_iota(jnp.int32, (count, HS), 0)
        lane = lax.broadcasted_iota(jnp.int32, (count, HS), 1)
        piece = (token // 128) % 4
        row = jnp.where(piece % 2 == 1, moved, stay) * 8 + (token // 8) % 8
        return token, lane, piece, row < live_rows

    token, lane, piece, live = places(1024)
    dead = (lane == 4) & jnp.logical_not(live)
    on = (lane == piece) | dead | ((lane == 5) & (token >= 512))
    kaug[:, HS:] = jnp.where(on, 1.0, 0.0).astype(jnp.bfloat16)
    token, lane, piece, live = places(512)
    rows_apart = (lane % 2 != piece % 2) & row_split
    cols_apart = (lane // 2 != piece // 2) & col_split
    off = ((lane < 4) & (rows_apart | cols_apart)) | (lane == 4) | ((lane == 5) & missing)
    qaug[:, HS:] = jnp.where(off, -BIG, 0.0).astype(jnp.bfloat16)
    alive[...] = jnp.where(live, 1.0, 0.0)


def attend_kernel(half, meta, skv, sq, x, y, d, hs, h2, hd, o0, o1, o2, o3, kaug, vaug, qaug, alive):
    outs = (o0, o1, o2, o3)

    @pl.when(pl.program_id(0) == 0)
    def _():
        features(half, meta, kaug.at[0], qaug.at[0], alive)
        for n in range(1, STEP):
            kaug[n, :, HS:] = kaug[0, :, HS:]
            qaug[n, :, HS:] = qaug[0, :, HS:]
        vaug[:, :, HS:] = jnp.ones((STEP, 1024, HS), jnp.bfloat16)

    keys = (skv, x, y, d, hs, h2.at[0], h2.at[1], hd)
    asks = (sq.at[0], x.at[2], y.at[2], d.at[2])
    for h in range(STEP):
        lanes = pl.ds(h * HS, HS)
        for n, ref in enumerate(keys):
            kaug[h, pl.ds(n * 128, 128), :HS] = ref[0, :, lanes]
            vaug[h, pl.ds(n * 128, 128), :HS] = ref[1, :, lanes]
        for n, ref in enumerate(asks):
            qaug[h, pl.ds(n * 128, 128), :HS] = ref[:, lanes]
    scale = math.log2(math.e) / math.sqrt(HS)

    def score(at):
        h, part = divmod(at, 2)
        return lax.dot_general(
            qaug[h, pl.ds(part * 256, 256), :], kaug[h], (((1,), (1,)), ((), ())), preferred_element_type=jnp.float32
        )

    scores = score(0)
    for at in range(2 * STEP):
        later = score(at + 1) if at + 1 < 2 * STEP else None
        h, part = divmod(at, 2)
        lanes = pl.ds(h * HS, HS)
        top = jnp.max(scores, axis=1, keepdims=True)
        weights = jnp.exp2((scores - top) * scale).astype(jnp.bfloat16)
        mixed = jnp.dot(weights, vaug[h], preferred_element_type=jnp.float32)
        result = (mixed[:, :HS] / mixed[:, HS:] * alive[pl.ds(part * 256, 256), :]).astype(jnp.bfloat16)
        outs[2 * part][:, lanes] = result[:128]
        outs[2 * part + 1][:, lanes] = result[128:]
        scores = later


def attend(half, meta, *pieces):
    width = STEP * HS

    def spec(piece):
        lead = piece.shape[:-1]
        return pl.BlockSpec((*lead, width), lambda h: (0,) * len(lead) + (h,))

    return pl.pallas_call(
        functools.partial(attend_kernel, half),
        grid=(H // STEP,),
        out_shape=[jax.ShapeDtypeStruct((128, HD), jnp.bfloat16)] * 4,
        in_specs=[pl.BlockSpec(memory_space=pltpu.SMEM)] + [spec(piece) for piece in pieces],
        out_specs=[pl.BlockSpec((128, width), lambda h: (0, h))] * 4,
        scratch_shapes=[
            pltpu.VMEM((STEP, 1024, 2 * HS), jnp.bfloat16),
            pltpu.VMEM((STEP, 1024, 2 * HS), jnp.bfloat16),
            pltpu.VMEM((STEP, 512, 2 * HS), jnp.bfloat16),
            pltpu.VMEM((512, HS), jnp.float32),
        ],
        compiler_params=pltpu.CompilerParams(vmem_limit_bytes=VMEM),
        cost_estimate=pl.CostEstimate(flops=H * 4 * 512 * 1024 * 256, bytes_accessed=10 * 2**20, transcendentals=H * 2**19),
        name="attend",
    )(meta, *pieces)


def project_kernel(meta, places, *refs):
    attended, own, (s0, s13, s2), (tokens, out, lhs, held, sems) = refs[:8], refs[8:12], refs[12:15], refs[15:]
    other = (s0, s13.at[0], s2, s13.at[1])
    step = pl.program_id(0)
    core, x = lax.rem(meta[0], 2), lax.rem(meta[1], 4)

    def fetch(n):
        side, zhi = divmod(n, 2)
        k = core if side == 0 else 1 - core
        copies = []
        for turn, src in enumerate(other if side else own):
            at = lax.rem(x + turn * (2 * k - 1) + 4, 4)
            for zlo in range(2):
                to = pl.ds(pl.multiple_of(zlo * 384 + at * 96, 32), 96)
                copies.append(
                    pltpu.make_async_copy(
                        src.at[pl.ds((2 * zhi + zlo) * 96, 96)], held.at[n % 2, to], sems.at[n % 2, 2 * turn + zlo]
                    )
                )
        return copies

    @pl.when(step == 0)
    def _():
        for copy in fetch(0):
            copy.start()
        for half in range(2):
            s = sign_of(half, meta[0])
            for piece, (a, b) in enumerate(MOVES):
                i = s + a * (1 - 2 * s)
                j = s + b * (1 - 2 * s)
                lhs[half * 4 + i * 2 + j] = attended[half * 4 + piece][...]

    for n in range(4):

        @pl.when(step == n)
        def _():
            for copy in fetch(n):
                copy.wait()
            if n < 3:
                for copy in fetch(n + 1):
                    copy.start()

    total = lax.dot_general(
        lhs[...].reshape(1024, HD), held[lax.rem(step, 2)], (((1,), (1,)), ((), ())), preferred_element_type=jnp.float32
    ).reshape(2, 2, 2, 2, 8, 8, TILE)
    for half in range(2):
        for i in range(2):
            block = jnp.concatenate([total[half, i, 0], total[half, i, 1]], axis=2)
            at = (slice(2 * half, 2 * half + 2), slice(8 * i, 8 * i + 8))
            out[at] = (block + tokens[at].astype(jnp.float32)).astype(jnp.bfloat16)


def project(attended, meta, places, chunks, tokens):
    grid_spec = pltpu.PrefetchScalarGridSpec(
        num_scalar_prefetch=2,
        grid=(D // TILE,),
        in_specs=[pl.BlockSpec((128, HD), lambda t, m, p: (0, 0))] * 8
        + [pl.BlockSpec(memory_space=pl.ANY)] * 7
        + [pl.BlockSpec((4, 16, 16, TILE), lambda t, m, p: (0, 0, 0, p[t]))],
        out_specs=pl.BlockSpec((4, 16, 16, TILE), lambda t, m, p: (0, 0, 0, p[t])),
        scratch_shapes=[
            pltpu.VMEM((8, 128, HD), jnp.bfloat16),
            pltpu.VMEM((2, TILE, HD), jnp.bfloat16),
            pltpu.SemaphoreType.DMA((2, 8)),
        ],
    )
    return pl.pallas_call(
        project_kernel,
        grid_spec=grid_spec,
        out_shape=jax.ShapeDtypeStruct((4, 16, 16, D), jnp.bfloat16),
        compiler_params=pltpu.CompilerParams(vmem_limit_bytes=VMEM),
        cost_estimate=pl.CostEstimate(flops=2 * 1024 * HD * D, bytes_accessed=25 * 2**20, transcendentals=0),
        name="project",
    )(meta, places, *attended, *chunks, tokens)


def ring_order(own, first, second, third, place):
    row = jnp.stack([third, second, first, own, third, second, first])
    return lax.dynamic_slice_in_dim(row, 3 - place, 4, axis=0)


def together(*values):
    return lax.optimization_barrier(values)


def local(tokens_in, queries, key_rows, value_rows, out_weight, row_valid):
    f, r, c = (lax.axis_index(a) for a in AXES)
    frame = f.astype(jnp.int32).reshape(1)
    meta = jnp.stack([f, r, c, jnp.sum(row_valid)]).astype(jnp.int32)
    core = f & 1
    places = jnp.stack([core, 2 + core, 1 - core, 3 - core]).astype(jnp.int32)
    split = lambda a: a.reshape(4, 2, 8, 2, 8, HD)
    arrays = (split(key_rows), split(value_rows), split(queries))
    shard = out_weight.T

    row, col, both = MOVES[1:]
    go = lambda value, half, move: send(value, window_pairs(half, *move))
    up = lambda value: send(value, frame_pairs(1))
    down = lambda value: send(value, frame_pairs(-1))
    swap = lambda value: send(value, core_pairs())
    turn = lambda value, step=1: send(value, shift_pairs(dx=step, opposed=True))
    back = lambda half, mixed: [mixed[0]] + [send(mixed[n], window_pairs(half, *MOVES[n], back=True)) for n in (1, 2, 3)]

    x0, y0 = pack(((0, 1, "kvq"), (0, 2, "kvq")), frame, *arrays)
    x0, y0, frame, shard = together(x0, y0, frame, shard)
    x0, y0 = go(x0, 0, row), go(y0, 0, col)
    shards = [send(shard, shift_pairs(dz=n)) for n in (1, 2, 3)]
    frame, *shards = together(frame, *shards)
    skv0, skv1, x1, y1 = pack(((0, 0, "kv"), (1, 0, "kv"), (1, 1, "kvq"), (1, 2, "kvq")), frame, *arrays)
    skv0, skv1, x1, y1, frame = together(skv0, skv1, x1, y1, frame)
    downs, ups = down(skv0), up(skv1)
    x1, y1 = go(x1, 1, row), go(y1, 1, col)
    d0, d1, sq0, sq1 = pack(((0, 3, "kvq"), (1, 3, "kvq"), (0, 0, "q"), (1, 0, "q")), frame, *arrays)
    strip = ring_order(shard, *shards, (f >> 1) * 2 + (r >> 2))
    h0, h1 = jnp.stack([x0[:2], y0[:2]]), jnp.stack([x1[:2], y1[:2]])
    d0, d1, h0, h1, x0, y0, x1, y1, downs, ups, meta, places, strip = together(
        d0, d1, h0, h1, x0, y0, x1, y1, downs, ups, meta, places, strip
    )
    d0, d1, down2, up2 = go(d0, 0, both), go(d1, 1, both), down(h0), up(h1)
    strips = lax.all_gather(strip.reshape(96, HD), "col", axis=0, tiled=True)
    c0 = strips.reshape(4, 4, 24, HD).swapaxes(0, 1).reshape(384, HD)
    downd, upd = down(d0[:2]), up(d1[:2])
    c0, down2 = together(c0, down2)
    c1 = turn(c0)
    c0, downd, upd, down2, up2 = together(c0, downd, upd, down2, up2)

    c3, s0 = turn(c0, -1), swap(c0)
    mixed1 = attend(1, meta, skv1, sq1, x1, y1, d1, downs, down2, downd)
    c1, s0, skv0, *mixed1 = together(c1, s0, skv0, *mixed1)
    attended1, c2 = back(1, mixed1), turn(c1)
    mixed0 = attend(0, meta, skv0, sq0, x0, y0, d0, ups, up2, upd)
    c1, c3, *rest = together(c1, c3, *attended1, *mixed0)
    attended1, mixed0 = rest[:4], rest[4:]
    attended0, s13 = back(0, mixed0), swap(jnp.stack([c1, c3]))
    c2, s13, *attended0 = together(c2, s13, *attended0)
    return project(attended0 + attended1, meta, places, (c0, c1, c2, c3, s0, s13, swap(c2)), tokens_in)


def solution(mesh):
    return jax.shard_map(
        local,
        mesh=mesh,
        in_specs=(
            P("frame", "row", "col", None),
            P("frame", "row", "col", None),
            P("frame", "row", "col", None),
            P("frame", "row", "col", None),
            P(None, ("frame", "row", "col")),
            P(),
        ),
        out_specs=P("frame", "row", "col", None),
        check_vma=False,
    )
```

```python
import functools
import math

import jax
import jax.numpy as jnp
from jax import lax
from jax.experimental import pallas as pl
from jax.experimental.pallas import tpu as pltpu
from jax.sharding import PartitionSpec as P

D = 3072
H = 12
HS = 128
HD = 1536
F, R, C = 4, 8, 4
AXES = ("frame", "row", "col")
STEP = 4
BIG = 1e30
TILE = 768
VMEM = 56 * 1024 * 1024


def index(f, r, c):
    return ((f % F) * R + (r % R)) * C + (c % C)


def every():
    return [(f, r, c) for f in range(F) for r in range(R) for c in range(C)]


def window_pairs(half, dr, dc, back=False):
    pairs = []
    for f, r, c in every():
        step = 1 if (f + half) % 2 == 0 else -1
        here, there = index(f, r, c), index(f, r + step * dr, c + step * dc)
        pairs.append((there, here) if back else (here, there))
    return pairs


def frame_pairs(step):
    return [(index(f, r, c), index(f + step, r, c)) for f, r, c in every() if 0 <= f + step < F]


def core_pairs():
    return [(index(f, r, c), index(f ^ 1, r, c)) for f, r, c in every()]


def shift_pairs(dx=0, dy=0, dz=0, opposed=False):
    pairs = []
    for f, r, c in every():
        (zhi, core), (zlo, x) = divmod(f, 2), divmod(r, 4)
        way = -1 if opposed and core else 1
        z = (2 * zhi + zlo + way * dz) % 4
        pairs.append((index(f, r, c), index((z // 2) * 2 + core, (z % 2) * 4 + (x + way * dx) % 4, c + way * dy)))
    return pairs


def send(value, pairs):
    return lax.ppermute(value, AXES, pairs)


MOVES = ((0, 0), (1, 0), (0, 1), (1, 1))


def sign_of(half, frame):
    return lax.rem(frame + half, 2)


def relay(moves, sems):
    inward = [pltpu.make_async_copy(src, held, sems.at[0, n]) for n, (src, held, _) in enumerate(moves)]
    outward = [pltpu.make_async_copy(held, dst, sems.at[1, n]) for n, (_, held, dst) in enumerate(moves)]
    for copy in inward:
        copy.start()
    for arrives, leaves in zip(inward, outward):
        arrives.wait()
        leaves.start()
    for copy in outward:
        copy.wait()


def pack_kernel(parts, meta, k_ref, v_ref, q_ref, *rest):
    outs, held, sems = rest[: len(parts)], rest[-2], rest[-1]
    moves = []
    for out, (half, piece, names) in zip(outs, parts):
        s = sign_of(half, meta[0])
        a, b = MOVES[piece]
        i = s + a * (1 - 2 * s)
        j = s + b * (1 - 2 * s)
        for n, name in enumerate(names):
            src = {"k": k_ref, "v": v_ref, "q": q_ref}[name]
            moves.append((src.at[pl.ds(2 * half, 2), i, :, j], held.at[len(moves)], out.at[n]))
    relay(moves, sems)


def pack(parts, meta, k, v, q):
    any_spec = pl.BlockSpec(memory_space=pl.ANY)
    count = sum(len(names) for _, _, names in parts)
    outs = pl.pallas_call(
        functools.partial(pack_kernel, parts),
        out_shape=[jax.ShapeDtypeStruct((len(names), 2, 8, 8, HD), jnp.bfloat16) for _, _, names in parts],
        in_specs=[pl.BlockSpec(memory_space=pltpu.SMEM)] + [any_spec] * 3,
        out_specs=[any_spec] * len(parts),
        scratch_shapes=[pltpu.VMEM((count, 2, 8, 8, HD), jnp.bfloat16), pltpu.SemaphoreType.DMA((2, count))],
        compiler_params=pltpu.CompilerParams(vmem_limit_bytes=VMEM),
        cost_estimate=pl.CostEstimate(flops=0, bytes_accessed=count * 2**20, transcendentals=0),
        name="pack",
    )(meta, k, v, q)
    return [o.reshape(-1, 128, HD) for o in outs]


def features(half, meta, kaug, qaug, alive):
    f, r, c, live_rows = (meta[n] for n in range(4))
    s = sign_of(half, f)
    stay = 2 * r + s
    moved = lax.rem(stay + 2 * s + 15, 16)
    row_split = r == s * (R - 1)
    col_split = c == s * (C - 1)
    missing = f == half * (F - 1)

    def places(count):
        token = lax.broadcasted_iota(jnp.int32, (count, HS), 0)
        lane = lax.broadcasted_iota(jnp.int32, (count, HS), 1)
        piece = (token // 128) % 4
        row = jnp.where(piece % 2 == 1, moved, stay) * 8 + (token // 8) % 8
        return token, lane, piece, row < live_rows

    token, lane, piece, live = places(1024)
    dead = (lane == 4) & jnp.logical_not(live)
    on = (lane == piece) | dead | ((lane == 5) & (token >= 512))
    kaug[:, HS:] = jnp.where(on, 1.0, 0.0).astype(jnp.bfloat16)
    token, lane, piece, live = places(512)
    rows_apart = (lane % 2 != piece % 2) & row_split
    cols_apart = (lane // 2 != piece // 2) & col_split
    off = ((lane < 4) & (rows_apart | cols_apart)) | (lane == 4) | ((lane == 5) & missing)
    qaug[:, HS:] = jnp.where(off, -BIG, 0.0).astype(jnp.bfloat16)
    alive[...] = jnp.where(live, 1.0, 0.0)


def attend_kernel(half, meta, skv, sq, x, y, d, h3, hd, o0, o1, o2, o3, kaug, vaug, qaug, alive):
    outs = (o0, o1, o2, o3)

    @pl.when(pl.program_id(0) == 0)
    def _():
        features(half, meta, kaug.at[0], qaug.at[0], alive)
        for n in range(1, STEP):
            kaug[n, :, HS:] = kaug[0, :, HS:]
            qaug[n, :, HS:] = qaug[0, :, HS:]
        vaug[:, :, HS:] = jnp.ones((STEP, 1024, HS), jnp.bfloat16)

    keys = (skv, x, y, d, h3.at[0], h3.at[1], h3.at[2], hd)
    asks = (sq.at[0], x.at[2], y.at[2], d.at[2])
    for h in range(STEP):
        lanes = pl.ds(h * HS, HS)
        for n, ref in enumerate(keys):
            kaug[h, pl.ds(n * 128, 128), :HS] = ref[0, :, lanes]
            vaug[h, pl.ds(n * 128, 128), :HS] = ref[1, :, lanes]
        for n, ref in enumerate(asks):
            qaug[h, pl.ds(n * 128, 128), :HS] = ref[:, lanes]
    scale = math.log2(math.e) / math.sqrt(HS)

    def score(at):
        h, part = divmod(at, 2)
        return lax.dot_general(
            qaug[h, pl.ds(part * 256, 256), :], kaug[h], (((1,), (1,)), ((), ())), preferred_element_type=jnp.float32
        )

    scores = score(0)
    for at in range(2 * STEP):
        later = score(at + 1) if at + 1 < 2 * STEP else None
        h, part = divmod(at, 2)
        lanes = pl.ds(h * HS, HS)
        top = jnp.max(scores, axis=1, keepdims=True)
        weights = jnp.exp2((scores - top) * scale).astype(jnp.bfloat16)
        mixed = jnp.dot(weights, vaug[h], preferred_element_type=jnp.float32)
        result = (mixed[:, :HS] / mixed[:, HS:] * alive[pl.ds(part * 256, 256), :]).astype(jnp.bfloat16)
        outs[2 * part][:, lanes] = result[:128]
        outs[2 * part + 1][:, lanes] = result[128:]
        scores = later


def attend(half, meta, *pieces):
    width = STEP * HS

    def spec(piece):
        lead = piece.shape[:-1]
        return pl.BlockSpec((*lead, width), lambda h: (0,) * len(lead) + (h,))

    return pl.pallas_call(
        functools.partial(attend_kernel, half),
        grid=(H // STEP,),
        out_shape=[jax.ShapeDtypeStruct((128, HD), jnp.bfloat16)] * 4,
        in_specs=[pl.BlockSpec(memory_space=pltpu.SMEM)] + [spec(piece) for piece in pieces],
        out_specs=[pl.BlockSpec((128, width), lambda h: (0, h))] * 4,
        scratch_shapes=[
            pltpu.VMEM((STEP, 1024, 2 * HS), jnp.bfloat16),
            pltpu.VMEM((STEP, 1024, 2 * HS), jnp.bfloat16),
            pltpu.VMEM((STEP, 512, 2 * HS), jnp.bfloat16),
            pltpu.VMEM((512, HS), jnp.float32),
        ],
        compiler_params=pltpu.CompilerParams(vmem_limit_bytes=VMEM),
        cost_estimate=pl.CostEstimate(flops=H * 4 * 512 * 1024 * 256, bytes_accessed=10 * 2**20, transcendentals=H * 2**19),
        name="attend",
    )(meta, *pieces)


def project_kernel(half, meta, places, *refs):
    attended, own, other, tokens = refs[:4], refs[4:8], refs[8:12], refs[12]
    out, lhs, held, sems = refs[-4:]
    step = pl.program_id(0)
    core, x = lax.rem(meta[0], 2), lax.rem(meta[1], 4)

    def fetch(n):
        side, zhi = divmod(n, 2)
        k = core if side == 0 else 1 - core
        copies = []
        for turn, src in enumerate(other if side else own):
            at = lax.rem(x + turn * (2 * k - 1) + 4, 4)
            for zlo in range(2):
                to = pl.ds(pl.multiple_of(zlo * 384 + at * 96, 32), 96)
                copies.append(
                    pltpu.make_async_copy(
                        src.at[pl.ds((2 * zhi + zlo) * 96, 96)], held.at[n % 2, to], sems.at[n % 2, 2 * turn + zlo]
                    )
                )
        return copies

    @pl.when(step == 0)
    def _():
        for copy in fetch(0):
            copy.start()
        s = sign_of(half, meta[0])
        for piece, (a, b) in enumerate(MOVES):
            i = s + a * (1 - 2 * s)
            j = s + b * (1 - 2 * s)
            lhs[i * 2 + j] = attended[piece][...]

    for n in range(4):

        @pl.when(step == n)
        def _():
            for copy in fetch(n):
                copy.wait()
            if n < 3:
                for copy in fetch(n + 1):
                    copy.start()

    total = lax.dot_general(
        lhs[...].reshape(512, HD), held[lax.rem(step, 2)], (((1,), (1,)), ((), ())), preferred_element_type=jnp.float32
    ).reshape(2, 2, 2, 8, 8, TILE)
    for i in range(2):
        block = jnp.concatenate([total[i, 0], total[i, 1]], axis=2)
        at = (slice(0, 2), slice(8 * i, 8 * i + 8))
        out[at] = (block + tokens[at].astype(jnp.float32)).astype(jnp.bfloat16)


def project(half, attended, meta, places, chunks, tokens, partial=None):
    extra = [] if partial is None else [partial]
    block = pl.BlockSpec((2, 16, 16, TILE), lambda t, m, p: (half, 0, 0, p[t]))
    grid_spec = pltpu.PrefetchScalarGridSpec(
        num_scalar_prefetch=2,
        grid=(D // TILE,),
        in_specs=[pl.BlockSpec((128, HD), lambda t, m, p: (0, 0))] * 4
        + [pl.BlockSpec(memory_space=pl.ANY)] * 8
        + [block]
        + [pl.BlockSpec(memory_space=pl.ANY)] * len(extra),
        out_specs=block,
        scratch_shapes=[
            pltpu.VMEM((4, 128, HD), jnp.bfloat16),
            pltpu.VMEM((2, TILE, HD), jnp.bfloat16),
            pltpu.SemaphoreType.DMA((2, 8)),
        ],
    )
    return pl.pallas_call(
        functools.partial(project_kernel, half),
        grid_spec=grid_spec,
        out_shape=jax.ShapeDtypeStruct((4, 16, 16, D), jnp.bfloat16),
        input_output_aliases={} if partial is None else {15: 0},
        compiler_params=pltpu.CompilerParams(vmem_limit_bytes=VMEM),
        cost_estimate=pl.CostEstimate(flops=1024 * HD * D, bytes_accessed=17 * 2**20, transcendentals=0),
        name="project",
    )(meta, places, *attended, *chunks, tokens, *extra)


def depth_groups():
    return [
        [index(2 * zhi + core, zlo * 4 + x, c) for zhi in range(2) for zlo in range(2)]
        for core in range(2)
        for x in range(4)
        for c in range(C)
    ]


def together(*values):
    return lax.optimization_barrier(values)


def local(tokens_in, queries, key_rows, value_rows, out_weight, row_valid):
    f, r, c = (lax.axis_index(a) for a in AXES)
    frame = f.astype(jnp.int32).reshape(1)
    meta = jnp.stack([f, r, c, jnp.sum(row_valid)]).astype(jnp.int32)
    core = f & 1
    places = jnp.stack([core, 2 + core, 1 - core, 3 - core]).astype(jnp.int32)
    split = lambda a: a.reshape(4, 2, 8, 2, 8, HD)
    arrays = (split(key_rows), split(value_rows), split(queries))
    shard = out_weight.T

    row, col, both = MOVES[1:]
    go = lambda value, half, move: send(value, window_pairs(half, *move))
    up = lambda value: send(value, frame_pairs(1))
    down = lambda value: send(value, frame_pairs(-1))
    swap = lambda value: send(value, core_pairs())
    turn = lambda value, step=1: send(value, shift_pairs(dx=step, opposed=True))
    back = lambda half, mixed: [mixed[0]] + [send(mixed[n], window_pairs(half, *MOVES[n], back=True)) for n in (1, 2, 3)]

    x0, y0 = pack(((0, 1, "kvq"), (0, 2, "kvq")), frame, *arrays)
    x0, y0, frame = together(x0, y0, frame)
    x0, y0 = go(x0, 0, row), go(y0, 0, col)
    x1, y1 = pack(((1, 1, "kvq"), (1, 2, "kvq")), frame, *arrays)
    x1, y1, frame = together(x1, y1, frame)
    x1, y1 = go(x1, 1, row), go(y1, 1, col)
    skv0, skv1, d0, d1, sq0, sq1 = pack(
        ((0, 0, "kv"), (1, 0, "kv"), (0, 3, "kvq"), (1, 3, "kvq"), (0, 0, "q"), (1, 0, "q")), frame, *arrays
    )
    d0, shard = together(d0, shard)
    strip = lax.all_gather(shard, AXES, axis=0, tiled=True, axis_index_groups=depth_groups())
    h0, h1 = jnp.stack([skv0, x0[:2], y0[:2]]), jnp.stack([skv1, x1[:2], y1[:2]])
    d0, d1, h0, h1, x0, y0, x1, y1, meta, places, strip = together(d0, d1, h0, h1, x0, y0, x1, y1, meta, places, strip)
    d0, d1, down3, up3 = go(d0, 0, both), go(d1, 1, both), down(h0), up(h1)
    strips = lax.all_gather(strip, "col", axis=0, tiled=True)
    c0 = strips.reshape(4, 4, 24, HD).swapaxes(0, 1).reshape(384, HD)
    c0, d0, d1 = together(c0, d0, d1)
    downd, upd, c1 = down(d0[:2]), up(d1[:2]), turn(c0)
    c0, c1, downd, upd, down3, up3 = together(c0, c1, downd, upd, down3, up3)

    c2, c3, s0, s1 = turn(c1), turn(c0, -1), swap(c0), swap(c1)
    mixed1 = attend(1, meta, skv1, sq1, x1, y1, d1, down3, downd)
    s0, s1, skv0, *mixed1 = together(s0, s1, skv0, *mixed1)
    attended1 = back(1, mixed1)
    mixed0 = attend(0, meta, skv0, sq0, x0, y0, d0, up3, upd)
    c2, c3, *rest = together(c2, c3, *attended1, *mixed0)
    attended1, mixed0 = rest[:4], rest[4:]
    attended0, s2, s3 = back(0, mixed0), swap(c2), swap(c3)
    chunks = (c0, c1, c2, c3, s0, s1, s2, s3)
    out = project(1, attended1, meta, places, chunks, tokens_in)
    return project(0, attended0, meta, places, chunks, tokens_in, out)


def solution(mesh):
    return jax.shard_map(
        local,
        mesh=mesh,
        in_specs=(
            P("frame", "row", "col", None),
            P("frame", "row", "col", None),
            P("frame", "row", "col", None),
            P("frame", "row", "col", None),
            P(None, ("frame", "row", "col")),
            P(),
        ),
        out_specs=P("frame", "row", "col", None),
        check_vma=False,
    )
```

```python
import functools
import math

import jax
import jax.numpy as jnp
from jax import lax
from jax.experimental import pallas as pl
from jax.experimental.pallas import tpu as pltpu
from jax.sharding import PartitionSpec as P

D = 3072
H = 12
HS = 128
HD = 1536
F, R, C = 4, 8, 4
AXES = ("frame", "row", "col")
STEP = 4
BIG = 1e30
TILE = 768
VMEM = 56 * 1024 * 1024


def index(f, r, c):
    return ((f % F) * R + (r % R)) * C + (c % C)


def every():
    return [(f, r, c) for f in range(F) for r in range(R) for c in range(C)]


def window_pairs(half, dr, dc, back=False):
    pairs = []
    for f, r, c in every():
        step = 1 if (f + half) % 2 == 0 else -1
        here, there = index(f, r, c), index(f, r + step * dr, c + step * dc)
        pairs.append((there, here) if back else (here, there))
    return pairs


def frame_pairs(step):
    return [(index(f, r, c), index(f + step, r, c)) for f, r, c in every() if 0 <= f + step < F]


def core_pairs():
    return [(index(f, r, c), index(f ^ 1, r, c)) for f, r, c in every()]


def shift_pairs(dx=0, dy=0, dz=0, opposed=False):
    pairs = []
    for f, r, c in every():
        (zhi, core), (zlo, x) = divmod(f, 2), divmod(r, 4)
        way = -1 if opposed and core else 1
        z = (2 * zhi + zlo + way * dz) % 4
        pairs.append((index(f, r, c), index((z // 2) * 2 + core, (z % 2) * 4 + (x + way * dx) % 4, c + way * dy)))
    return pairs


def send(value, pairs):
    return lax.ppermute(value, AXES, pairs)


MOVES = ((0, 0), (1, 0), (0, 1), (1, 1))


def sign_of(half, frame):
    return lax.rem(frame + half, 2)


def relay(moves, sems):
    inward = [pltpu.make_async_copy(src, held, sems.at[0, n]) for n, (src, held, _) in enumerate(moves)]
    outward = [pltpu.make_async_copy(held, dst, sems.at[1, n]) for n, (_, held, dst) in enumerate(moves)]
    for copy in inward:
        copy.start()
    for arrives, leaves in zip(inward, outward):
        arrives.wait()
        leaves.start()
    for copy in outward:
        copy.wait()


def pack_kernel(parts, meta, k_ref, v_ref, q_ref, *rest):
    outs, held, sems = rest[: len(parts)], rest[-2], rest[-1]
    moves = []
    for out, (half, piece, names) in zip(outs, parts):
        s = sign_of(half, meta[0])
        a, b = MOVES[piece]
        i = s + a * (1 - 2 * s)
        j = s + b * (1 - 2 * s)
        for n, name in enumerate(names):
            src = {"k": k_ref, "v": v_ref, "q": q_ref}[name]
            moves.append((src.at[pl.ds(2 * half, 2), i, :, j], held.at[len(moves)], out.at[n]))
    relay(moves, sems)


def pack(parts, meta, k, v, q):
    any_spec = pl.BlockSpec(memory_space=pl.ANY)
    count = sum(len(names) for _, _, names in parts)
    outs = pl.pallas_call(
        functools.partial(pack_kernel, parts),
        out_shape=[jax.ShapeDtypeStruct((len(names), 2, 8, 8, HD), jnp.bfloat16) for _, _, names in parts],
        in_specs=[pl.BlockSpec(memory_space=pltpu.SMEM)] + [any_spec] * 3,
        out_specs=[any_spec] * len(parts),
        scratch_shapes=[pltpu.VMEM((count, 2, 8, 8, HD), jnp.bfloat16), pltpu.SemaphoreType.DMA((2, count))],
        compiler_params=pltpu.CompilerParams(vmem_limit_bytes=VMEM),
        cost_estimate=pl.CostEstimate(flops=0, bytes_accessed=count * 2**20, transcendentals=0),
        name="pack",
    )(meta, k, v, q)
    return [o.reshape(-1, 128, HD) for o in outs]


def features(half, meta, kaug, qaug, alive):
    f, r, c, live_rows = (meta[n] for n in range(4))
    s = sign_of(half, f)
    stay = 2 * r + s
    moved = lax.rem(stay + 2 * s + 15, 16)
    row_split = r == s * (R - 1)
    col_split = c == s * (C - 1)
    missing = f == half * (F - 1)

    def places(count):
        token = lax.broadcasted_iota(jnp.int32, (count, HS), 0)
        lane = lax.broadcasted_iota(jnp.int32, (count, HS), 1)
        piece = (token // 128) % 4
        row = jnp.where(piece % 2 == 1, moved, stay) * 8 + (token // 8) % 8
        return token, lane, piece, row < live_rows

    token, lane, piece, live = places(1024)
    dead = (lane == 4) & jnp.logical_not(live)
    on = (lane == piece) | dead | ((lane == 5) & (token >= 512))
    kaug[:, HS:] = jnp.where(on, 1.0, 0.0).astype(jnp.bfloat16)
    token, lane, piece, live = places(512)
    rows_apart = (lane % 2 != piece % 2) & row_split
    cols_apart = (lane // 2 != piece // 2) & col_split
    off = ((lane < 4) & (rows_apart | cols_apart)) | (lane == 4) | ((lane == 5) & missing)
    qaug[:, HS:] = jnp.where(off, -BIG, 0.0).astype(jnp.bfloat16)
    alive[...] = jnp.where(live, 1.0, 0.0)


def attend_kernel(half, meta, skv, sq, x, y, d, h3, hd, o0, o1, o2, o3, kaug, vaug, qaug, alive):
    outs = (o0, o1, o2, o3)

    @pl.when(pl.program_id(0) == 0)
    def _():
        features(half, meta, kaug.at[0], qaug.at[0], alive)
        for n in range(1, STEP):
            kaug[n, :, HS:] = kaug[0, :, HS:]
            qaug[n, :, HS:] = qaug[0, :, HS:]
        vaug[:, :, HS:] = jnp.ones((STEP, 1024, HS), jnp.bfloat16)

    keys = (skv, x, y, d, h3.at[0], h3.at[1], h3.at[2], hd)
    asks = (sq.at[0], x.at[2], y.at[2], d.at[2])
    for h in range(STEP):
        lanes = pl.ds(h * HS, HS)
        for n, ref in enumerate(keys):
            kaug[h, pl.ds(n * 128, 128), :HS] = ref[0, :, lanes]
            vaug[h, pl.ds(n * 128, 128), :HS] = ref[1, :, lanes]
        for n, ref in enumerate(asks):
            qaug[h, pl.ds(n * 128, 128), :HS] = ref[:, lanes]
    scale = math.log2(math.e) / math.sqrt(HS)

    def score(at):
        h, part = divmod(at, 2)
        return lax.dot_general(
            qaug[h, pl.ds(part * 256, 256), :], kaug[h], (((1,), (1,)), ((), ())), preferred_element_type=jnp.float32
        )

    scores = score(0)
    for at in range(2 * STEP):
        later = score(at + 1) if at + 1 < 2 * STEP else None
        h, part = divmod(at, 2)
        lanes = pl.ds(h * HS, HS)
        top = jnp.max(scores, axis=1, keepdims=True)
        weights = jnp.exp2((scores - top) * scale).astype(jnp.bfloat16)
        mixed = jnp.dot(weights, vaug[h], preferred_element_type=jnp.float32)
        result = (mixed[:, :HS] / mixed[:, HS:] * alive[pl.ds(part * 256, 256), :]).astype(jnp.bfloat16)
        outs[2 * part][:, lanes] = result[:128]
        outs[2 * part + 1][:, lanes] = result[128:]
        scores = later


def attend(half, meta, *pieces):
    width = STEP * HS

    def spec(piece):
        lead = piece.shape[:-1]
        return pl.BlockSpec((*lead, width), lambda h: (0,) * len(lead) + (h,))

    return pl.pallas_call(
        functools.partial(attend_kernel, half),
        grid=(H // STEP,),
        out_shape=[jax.ShapeDtypeStruct((128, HD), jnp.bfloat16)] * 4,
        in_specs=[pl.BlockSpec(memory_space=pltpu.SMEM)] + [spec(piece) for piece in pieces],
        out_specs=[pl.BlockSpec((128, width), lambda h: (0, h))] * 4,
        scratch_shapes=[
            pltpu.VMEM((STEP, 1024, 2 * HS), jnp.bfloat16),
            pltpu.VMEM((STEP, 1024, 2 * HS), jnp.bfloat16),
            pltpu.VMEM((STEP, 512, 2 * HS), jnp.bfloat16),
            pltpu.VMEM((512, HS), jnp.float32),
        ],
        compiler_params=pltpu.CompilerParams(vmem_limit_bytes=VMEM),
        cost_estimate=pl.CostEstimate(flops=H * 4 * 512 * 1024 * 256, bytes_accessed=10 * 2**20, transcendentals=H * 2**19),
        name="attend",
    )(meta, *pieces)


def project_kernel(half, meta, places, *refs):
    attended, own, other, tokens = refs[:4], refs[4:8], refs[8:12], refs[12]
    out, lhs, held, sems = refs[-4:]
    step = pl.program_id(0)
    core, x = lax.rem(meta[0], 2), lax.rem(meta[1], 4)

    def fetch(n):
        side, zhi = divmod(n, 2)
        k = core if side == 0 else 1 - core
        copies = []
        for turn, src in enumerate(other if side else own):
            at = lax.rem(x + turn * (2 * k - 1) + 4, 4)
            for zlo in range(2):
                to = pl.ds(pl.multiple_of(zlo * 384 + at * 96, 32), 96)
                copies.append(
                    pltpu.make_async_copy(
                        src.at[pl.ds((2 * zhi + zlo) * 96, 96)], held.at[n % 2, to], sems.at[n % 2, 2 * turn + zlo]
                    )
                )
        return copies

    @pl.when(step == 0)
    def _():
        for copy in fetch(0):
            copy.start()
        s = sign_of(half, meta[0])
        for piece, (a, b) in enumerate(MOVES):
            i = s + a * (1 - 2 * s)
            j = s + b * (1 - 2 * s)
            lhs[i * 2 + j] = attended[piece][...]

    for n in range(4):

        @pl.when(step == n)
        def _():
            for copy in fetch(n):
                copy.wait()
            if n < 3:
                for copy in fetch(n + 1):
                    copy.start()

    total = lax.dot_general(
        lhs[...].reshape(512, HD), held[lax.rem(step, 2)], (((1,), (1,)), ((), ())), preferred_element_type=jnp.float32
    ).reshape(2, 2, 2, 8, 8, TILE)
    for i in range(2):
        block = jnp.concatenate([total[i, 0], total[i, 1]], axis=2)
        at = (slice(0, 2), slice(8 * i, 8 * i + 8))
        out[at] = (block + tokens[at].astype(jnp.float32)).astype(jnp.bfloat16)


def project(half, attended, meta, places, chunks, tokens, partial=None):
    extra = [] if partial is None else [partial]
    block = pl.BlockSpec((2, 16, 16, TILE), lambda t, m, p: (half, 0, 0, p[t]))
    grid_spec = pltpu.PrefetchScalarGridSpec(
        num_scalar_prefetch=2,
        grid=(D // TILE,),
        in_specs=[pl.BlockSpec((128, HD), lambda t, m, p: (0, 0))] * 4
        + [pl.BlockSpec(memory_space=pl.ANY)] * 8
        + [block]
        + [pl.BlockSpec(memory_space=pl.ANY)] * len(extra),
        out_specs=block,
        scratch_shapes=[
            pltpu.VMEM((4, 128, HD), jnp.bfloat16),
            pltpu.VMEM((2, TILE, HD), jnp.bfloat16),
            pltpu.SemaphoreType.DMA((2, 8)),
        ],
    )
    return pl.pallas_call(
        functools.partial(project_kernel, half),
        grid_spec=grid_spec,
        out_shape=jax.ShapeDtypeStruct((4, 16, 16, D), jnp.bfloat16),
        input_output_aliases={} if partial is None else {15: 0},
        compiler_params=pltpu.CompilerParams(vmem_limit_bytes=VMEM),
        cost_estimate=pl.CostEstimate(flops=1024 * HD * D, bytes_accessed=17 * 2**20, transcendentals=0),
        name="project",
    )(meta, places, *attended, *chunks, tokens, *extra)


def ring_order(own, first, second, third, place):
    row = jnp.stack([third, second, first, own, third, second, first])
    return lax.dynamic_slice_in_dim(row, 3 - place, 4, axis=0)


def together(*values):
    return lax.optimization_barrier(values)


def local(tokens_in, queries, key_rows, value_rows, out_weight, row_valid):
    f, r, c = (lax.axis_index(a) for a in AXES)
    frame = f.astype(jnp.int32).reshape(1)
    meta = jnp.stack([f, r, c, jnp.sum(row_valid)]).astype(jnp.int32)
    core = f & 1
    places = jnp.stack([core, 2 + core, 1 - core, 3 - core]).astype(jnp.int32)
    split = lambda a: a.reshape(4, 2, 8, 2, 8, HD)
    arrays = (split(key_rows), split(value_rows), split(queries))
    shard = out_weight.T

    row, col, both = MOVES[1:]
    go = lambda value, half, move: send(value, window_pairs(half, *move))
    up = lambda value: send(value, frame_pairs(1))
    down = lambda value: send(value, frame_pairs(-1))
    swap = lambda value: send(value, core_pairs())
    turn = lambda value, step=1: send(value, shift_pairs(dx=step, opposed=True))
    back = lambda half, mixed: [mixed[0]] + [send(mixed[n], window_pairs(half, *MOVES[n], back=True)) for n in (1, 2, 3)]

    x0, y0 = pack(((0, 1, "kvq"), (0, 2, "kvq")), frame, *arrays)
    x0, y0, frame, shard = together(x0, y0, frame, shard)
    x0, y0 = go(x0, 0, row), go(y0, 0, col)
    shards = [send(shard, shift_pairs(dz=n)) for n in (1, 2, 3)]
    x1, y1 = pack(((1, 1, "kvq"), (1, 2, "kvq")), frame, *arrays)
    x1, y1, frame, *shards = together(x1, y1, frame, *shards)
    x1, y1 = go(x1, 1, row), go(y1, 1, col)
    skv0, skv1, d0, d1, sq0, sq1 = pack(
        ((0, 0, "kv"), (1, 0, "kv"), (0, 3, "kvq"), (1, 3, "kvq"), (0, 0, "q"), (1, 0, "q")), frame, *arrays
    )
    strip = ring_order(shard, *shards, (f >> 1) * 2 + (r >> 2))
    h0, h1 = jnp.stack([skv0, x0[:2], y0[:2]]), jnp.stack([skv1, x1[:2], y1[:2]])
    d0, d1, h0, h1, x0, y0, x1, y1, meta, places, strip = together(d0, d1, h0, h1, x0, y0, x1, y1, meta, places, strip)
    d0, d1, down3, up3 = go(d0, 0, both), go(d1, 1, both), down(h0), up(h1)
    strips = lax.all_gather(strip.reshape(96, HD), "col", axis=0, tiled=True)
    c0 = strips.reshape(4, 4, 24, HD).swapaxes(0, 1).reshape(384, HD)
    downd, upd = down(d0[:2]), up(d1[:2])
    c1 = turn(c0)
    c0, c1, downd, upd, down3, up3 = together(c0, c1, downd, upd, down3, up3)

    c2, c3, s0, s1 = turn(c1), turn(c0, -1), swap(c0), swap(c1)
    mixed1 = attend(1, meta, skv1, sq1, x1, y1, d1, down3, downd)
    s0, s1, skv0, *mixed1 = together(s0, s1, skv0, *mixed1)
    attended1 = back(1, mixed1)
    mixed0 = attend(0, meta, skv0, sq0, x0, y0, d0, up3, upd)
    c2, c3, *rest = together(c2, c3, *attended1, *mixed0)
    attended1, mixed0 = rest[:4], rest[4:]
    attended0, s2, s3 = back(0, mixed0), swap(c2), swap(c3)
    chunks = (c0, c1, c2, c3, s0, s1, s2, s3)
    out = project(1, attended1, meta, places, chunks, tokens_in)
    return project(0, attended0, meta, places, chunks, tokens_in, out)


def solution(mesh):
    return jax.shard_map(
        local,
        mesh=mesh,
        in_specs=(
            P("frame", "row", "col", None),
            P("frame", "row", "col", None),
            P("frame", "row", "col", None),
            P("frame", "row", "col", None),
            P(None, ("frame", "row", "col")),
            P(),
        ),
        out_specs=P("frame", "row", "col", None),
        check_vma=False,
    )
```

```python
import functools
import math

import jax
import jax.numpy as jnp
from jax import lax
from jax.experimental import pallas as pl
from jax.experimental.pallas import tpu as pltpu
from jax.sharding import PartitionSpec as P

D = 3072
H = 12
HS = 128
HD = 1536
F, R, C = 4, 8, 4
AXES = ("frame", "row", "col")
STEP = 4
BIG = 1e30
TILE = 768
VMEM = 56 * 1024 * 1024


def index(f, r, c):
    return ((f % F) * R + (r % R)) * C + (c % C)


def every():
    return [(f, r, c) for f in range(F) for r in range(R) for c in range(C)]


def window_pairs(half, dr, dc, back=False):
    pairs = []
    for f, r, c in every():
        step = 1 if (f + half) % 2 == 0 else -1
        here, there = index(f, r, c), index(f, r + step * dr, c + step * dc)
        pairs.append((there, here) if back else (here, there))
    return pairs


def frame_pairs(step):
    return [(index(f, r, c), index(f + step, r, c)) for f, r, c in every() if 0 <= f + step < F]


def core_pairs():
    return [(index(f, r, c), index(f ^ 1, r, c)) for f, r, c in every()]


def shift_pairs(dx=0, dy=0, dz=0, opposed=False):
    pairs = []
    for f, r, c in every():
        (zhi, core), (zlo, x) = divmod(f, 2), divmod(r, 4)
        way = -1 if opposed and core else 1
        z = (2 * zhi + zlo + way * dz) % 4
        pairs.append((index(f, r, c), index((z // 2) * 2 + core, (z % 2) * 4 + (x + way * dx) % 4, c + way * dy)))
    return pairs


def send(value, pairs):
    return lax.ppermute(value, AXES, pairs)


MOVES = ((0, 0), (1, 0), (0, 1), (1, 1))


def sign_of(half, frame):
    return lax.rem(frame + half, 2)


def relay(moves, sems):
    inward = [pltpu.make_async_copy(src, held, sems.at[0, n]) for n, (src, held, _) in enumerate(moves)]
    outward = [pltpu.make_async_copy(held, dst, sems.at[1, n]) for n, (_, held, dst) in enumerate(moves)]
    for copy in inward:
        copy.start()
    for arrives, leaves in zip(inward, outward):
        arrives.wait()
        leaves.start()
    for copy in outward:
        copy.wait()


def pack_kernel(parts, meta, k_ref, v_ref, q_ref, *rest):
    outs, held, sems = rest[: len(parts)], rest[-2], rest[-1]
    moves = []
    for out, (half, piece, names) in zip(outs, parts):
        s = sign_of(half, meta[0])
        a, b = MOVES[piece]
        i = s + a * (1 - 2 * s)
        j = s + b * (1 - 2 * s)
        for n, name in enumerate(names):
            src = {"k": k_ref, "v": v_ref, "q": q_ref}[name]
            moves.append((src.at[pl.ds(2 * half, 2), i, :, j], held.at[len(moves)], out.at[n]))
    relay(moves, sems)


def pack(parts, meta, k, v, q):
    any_spec = pl.BlockSpec(memory_space=pl.ANY)
    count = sum(len(names) for _, _, names in parts)
    outs = pl.pallas_call(
        functools.partial(pack_kernel, parts),
        out_shape=[jax.ShapeDtypeStruct((len(names), 2, 8, 8, HD), jnp.bfloat16) for _, _, names in parts],
        in_specs=[pl.BlockSpec(memory_space=pltpu.SMEM)] + [any_spec] * 3,
        out_specs=[any_spec] * len(parts),
        scratch_shapes=[pltpu.VMEM((count, 2, 8, 8, HD), jnp.bfloat16), pltpu.SemaphoreType.DMA((2, count))],
        compiler_params=pltpu.CompilerParams(vmem_limit_bytes=VMEM),
        cost_estimate=pl.CostEstimate(flops=0, bytes_accessed=count * 2**20, transcendentals=0),
        name="pack",
    )(meta, k, v, q)
    return [o.reshape(-1, 128, HD) for o in outs]


def features(half, meta, kaug, qaug, alive):
    f, r, c, live_rows = (meta[n] for n in range(4))
    s = sign_of(half, f)
    stay = 2 * r + s
    moved = lax.rem(stay + 2 * s + 15, 16)
    row_split = r == s * (R - 1)
    col_split = c == s * (C - 1)
    missing = f == half * (F - 1)

    def places(count):
        token = lax.broadcasted_iota(jnp.int32, (count, HS), 0)
        lane = lax.broadcasted_iota(jnp.int32, (count, HS), 1)
        piece = (token // 128) % 4
        row = jnp.where(piece % 2 == 1, moved, stay) * 8 + (token // 8) % 8
        return token, lane, piece, row < live_rows

    token, lane, piece, live = places(1024)
    dead = (lane == 4) & jnp.logical_not(live)
    on = (lane == piece) | dead | ((lane == 5) & (token >= 512))
    kaug[:, HS:] = jnp.where(on, 1.0, 0.0).astype(jnp.bfloat16)
    token, lane, piece, live = places(512)
    rows_apart = (lane % 2 != piece % 2) & row_split
    cols_apart = (lane // 2 != piece // 2) & col_split
    off = ((lane < 4) & (rows_apart | cols_apart)) | (lane == 4) | ((lane == 5) & missing)
    qaug[:, HS:] = jnp.where(off, -BIG, 0.0).astype(jnp.bfloat16)
    alive[...] = jnp.where(live, 1.0, 0.0)


def attend_kernel(half, meta, skv, sq, x, y, d, h3, hd, o0, o1, o2, o3, kaug, vaug, qaug, alive):
    outs = (o0, o1, o2, o3)

    @pl.when(pl.program_id(0) == 0)
    def _():
        features(half, meta, kaug.at[0], qaug.at[0], alive)
        for n in range(1, STEP):
            kaug[n, :, HS:] = kaug[0, :, HS:]
            qaug[n, :, HS:] = qaug[0, :, HS:]
        vaug[:, :, HS:] = jnp.ones((STEP, 1024, HS), jnp.bfloat16)

    keys = (skv, x, y, d, h3.at[0], h3.at[1], h3.at[2], hd)
    asks = (sq.at[0], x.at[2], y.at[2], d.at[2])
    for h in range(STEP):
        lanes = pl.ds(h * HS, HS)
        for n, ref in enumerate(keys):
            kaug[h, pl.ds(n * 128, 128), :HS] = ref[0, :, lanes]
            vaug[h, pl.ds(n * 128, 128), :HS] = ref[1, :, lanes]
        for n, ref in enumerate(asks):
            qaug[h, pl.ds(n * 128, 128), :HS] = ref[:, lanes]
    scale = math.log2(math.e) / math.sqrt(HS)

    def score(at):
        h, part = divmod(at, 2)
        return lax.dot_general(
            qaug[h, pl.ds(part * 256, 256), :], kaug[h], (((1,), (1,)), ((), ())), preferred_element_type=jnp.float32
        )

    scores = score(0)
    for at in range(2 * STEP):
        later = score(at + 1) if at + 1 < 2 * STEP else None
        h, part = divmod(at, 2)
        lanes = pl.ds(h * HS, HS)
        top = jnp.max(scores, axis=1, keepdims=True)
        weights = jnp.exp2((scores - top) * scale).astype(jnp.bfloat16)
        mixed = jnp.dot(weights, vaug[h], preferred_element_type=jnp.float32)
        result = (mixed[:, :HS] / mixed[:, HS:] * alive[pl.ds(part * 256, 256), :]).astype(jnp.bfloat16)
        outs[2 * part][:, lanes] = result[:128]
        outs[2 * part + 1][:, lanes] = result[128:]
        scores = later


def attend(half, meta, *pieces):
    width = STEP * HS

    def spec(piece):
        lead = piece.shape[:-1]
        return pl.BlockSpec((*lead, width), lambda h: (0,) * len(lead) + (h,))

    return pl.pallas_call(
        functools.partial(attend_kernel, half),
        grid=(H // STEP,),
        out_shape=[jax.ShapeDtypeStruct((128, HD), jnp.bfloat16)] * 4,
        in_specs=[pl.BlockSpec(memory_space=pltpu.SMEM)] + [spec(piece) for piece in pieces],
        out_specs=[pl.BlockSpec((128, width), lambda h: (0, h))] * 4,
        scratch_shapes=[
            pltpu.VMEM((STEP, 1024, 2 * HS), jnp.bfloat16),
            pltpu.VMEM((STEP, 1024, 2 * HS), jnp.bfloat16),
            pltpu.VMEM((STEP, 512, 2 * HS), jnp.bfloat16),
            pltpu.VMEM((512, HS), jnp.float32),
        ],
        compiler_params=pltpu.CompilerParams(vmem_limit_bytes=VMEM),
        cost_estimate=pl.CostEstimate(flops=H * 4 * 512 * 1024 * 256, bytes_accessed=10 * 2**20, transcendentals=H * 2**19),
        name="attend",
    )(meta, *pieces)


def project_kernel(half, sides, meta, places, *refs):
    attended, chunks, tokens = refs[:4], refs[4 : 4 + 4 * len(sides)], refs[4 + 4 * len(sides)]
    out, lhs, held, sems = refs[-4:]
    steps = 2 * len(sides)
    step = pl.program_id(0)
    core, x = lax.rem(meta[0], 2), lax.rem(meta[1], 4)

    def fetch(n):
        which, zhi = divmod(n, 2)
        k = core if sides[which] == 0 else 1 - core
        copies = []
        for turn, src in enumerate(chunks[4 * which : 4 * which + 4]):
            at = lax.rem(x + turn * (2 * k - 1) + 4, 4)
            for zlo in range(2):
                to = pl.ds(pl.multiple_of(zlo * 384 + at * 96, 32), 96)
                copies.append(
                    pltpu.make_async_copy(
                        src.at[pl.ds((2 * zhi + zlo) * 96, 96)], held.at[n % 2, to], sems.at[n % 2, 2 * turn + zlo]
                    )
                )
        return copies

    @pl.when(step == 0)
    def _():
        for copy in fetch(0):
            copy.start()
        s = sign_of(half, meta[0])
        for piece, (a, b) in enumerate(MOVES):
            i = s + a * (1 - 2 * s)
            j = s + b * (1 - 2 * s)
            lhs[i * 2 + j] = attended[piece][...]

    for n in range(steps):

        @pl.when(step == n)
        def _():
            for copy in fetch(n):
                copy.wait()
            if n + 1 < steps:
                for copy in fetch(n + 1):
                    copy.start()

    total = lax.dot_general(
        lhs[...].reshape(512, HD), held[lax.rem(step, 2)], (((1,), (1,)), ((), ())), preferred_element_type=jnp.float32
    ).reshape(2, 2, 2, 8, 8, TILE)
    for i in range(2):
        block = jnp.concatenate([total[i, 0], total[i, 1]], axis=2)
        at = (slice(0, 2), slice(8 * i, 8 * i + 8))
        out[at] = (block + tokens[at].astype(jnp.float32)).astype(jnp.bfloat16)


def project(half, sides, attended, meta, places, chunks, tokens, partial=None):
    extra = [] if partial is None else [partial]
    first = 2 * sides[0]
    block = pl.BlockSpec((2, 16, 16, TILE), lambda t, m, p: (half, 0, 0, p[t + first]))
    grid_spec = pltpu.PrefetchScalarGridSpec(
        num_scalar_prefetch=2,
        grid=(2 * len(sides),),
        in_specs=[pl.BlockSpec((128, HD), lambda t, m, p: (0, 0))] * 4
        + [pl.BlockSpec(memory_space=pl.ANY)] * len(chunks)
        + [block]
        + [pl.BlockSpec(memory_space=pl.ANY)] * len(extra),
        out_specs=block,
        scratch_shapes=[
            pltpu.VMEM((4, 128, HD), jnp.bfloat16),
            pltpu.VMEM((2, TILE, HD), jnp.bfloat16),
            pltpu.SemaphoreType.DMA((2, 8)),
        ],
    )
    return pl.pallas_call(
        functools.partial(project_kernel, half, sides),
        grid_spec=grid_spec,
        out_shape=jax.ShapeDtypeStruct((4, 16, 16, D), jnp.bfloat16),
        input_output_aliases={} if partial is None else {7 + len(chunks): 0},
        compiler_params=pltpu.CompilerParams(vmem_limit_bytes=VMEM),
        cost_estimate=pl.CostEstimate(flops=512 * len(sides) * HD * D, bytes_accessed=9 * len(sides) * 2**20, transcendentals=0),
        name="project",
    )(meta, places, *attended, *chunks, tokens, *extra)


def ring_order(own, first, second, third, place):
    row = jnp.stack([third, second, first, own, third, second, first])
    return lax.dynamic_slice_in_dim(row, 3 - place, 4, axis=0)


def together(*values):
    return lax.optimization_barrier(values)


def local(tokens_in, queries, key_rows, value_rows, out_weight, row_valid):
    f, r, c = (lax.axis_index(a) for a in AXES)
    frame = f.astype(jnp.int32).reshape(1)
    meta = jnp.stack([f, r, c, jnp.sum(row_valid)]).astype(jnp.int32)
    core = f & 1
    places = jnp.stack([core, 2 + core, 1 - core, 3 - core]).astype(jnp.int32)
    split = lambda a: a.reshape(4, 2, 8, 2, 8, HD)
    arrays = (split(key_rows), split(value_rows), split(queries))
    shard = out_weight.T

    row, col, both = MOVES[1:]
    go = lambda value, half, move: send(value, window_pairs(half, *move))
    up = lambda value: send(value, frame_pairs(1))
    down = lambda value: send(value, frame_pairs(-1))
    swap = lambda value: send(value, core_pairs())
    turn = lambda value, step=1: send(value, shift_pairs(dx=step, opposed=True))
    back = lambda half, mixed: [mixed[0]] + [send(mixed[n], window_pairs(half, *MOVES[n], back=True)) for n in (1, 2, 3)]

    x0, y0 = pack(((0, 1, "kvq"), (0, 2, "kvq")), frame, *arrays)
    x0, y0, frame, shard = together(x0, y0, frame, shard)
    x0, y0 = go(x0, 0, row), go(y0, 0, col)
    shards = [send(shard, shift_pairs(dz=n)) for n in (1, 2, 3)]
    x1, y1 = pack(((1, 1, "kvq"), (1, 2, "kvq")), frame, *arrays)
    x1, y1, frame, *shards = together(x1, y1, frame, *shards)
    x1, y1 = go(x1, 1, row), go(y1, 1, col)
    skv0, skv1, d0, d1, sq0, sq1 = pack(
        ((0, 0, "kv"), (1, 0, "kv"), (0, 3, "kvq"), (1, 3, "kvq"), (0, 0, "q"), (1, 0, "q")), frame, *arrays
    )
    strip = ring_order(shard, *shards, (f >> 1) * 2 + (r >> 2))
    h0, h1 = jnp.stack([skv0, x0[:2], y0[:2]]), jnp.stack([skv1, x1[:2], y1[:2]])
    d0, d1, h0, h1, x0, y0, x1, y1, meta, places, strip = together(d0, d1, h0, h1, x0, y0, x1, y1, meta, places, strip)
    d0, d1, down3, up3 = go(d0, 0, both), go(d1, 1, both), down(h0), up(h1)
    strips = lax.all_gather(strip.reshape(96, HD), "col", axis=0, tiled=True)
    c0 = strips.reshape(4, 4, 24, HD).swapaxes(0, 1).reshape(384, HD)
    c0, d0, d1 = together(c0, d0, d1)
    downd, upd, c1 = down(d0[:2]), up(d1[:2]), turn(c0)
    c0, c1, downd, upd, down3, up3 = together(c0, c1, downd, upd, down3, up3)

    c2, c3, s0, s1 = turn(c1), turn(c0, -1), swap(c0), swap(c1)
    mixed1 = attend(1, meta, skv1, sq1, x1, y1, d1, down3, downd)
    s0, s1, skv0, *mixed1 = together(s0, s1, skv0, *mixed1)
    attended1 = back(1, mixed1)
    mixed0 = attend(0, meta, skv0, sq0, x0, y0, d0, up3, upd)
    c2, c3, *rest = together(c2, c3, *attended1, *mixed0)
    attended1, mixed0 = rest[:4], rest[4:]
    attended0, s2, s3 = back(0, mixed0), swap(c2), swap(c3)
    own, other = (c0, c1, c2, c3), (s0, s1, s2, s3)
    out = project(1, (0,), attended1, meta, places, own, tokens_in)
    out = project(1, (1,), attended1, meta, places, other, tokens_in, out)
    return project(0, (0, 1), attended0, meta, places, own + other, tokens_in, out)


def solution(mesh):
    return jax.shard_map(
        local,
        mesh=mesh,
        in_specs=(
            P("frame", "row", "col", None),
            P("frame", "row", "col", None),
            P("frame", "row", "col", None),
            P("frame", "row", "col", None),
            P(None, ("frame", "row", "col")),
            P(),
        ),
        out_specs=P("frame", "row", "col", None),
        check_vma=False,
    )
```

```python
import functools
import math

import jax
import jax.numpy as jnp
from jax import lax
from jax.experimental import pallas as pl
from jax.experimental.pallas import tpu as pltpu
from jax.sharding import PartitionSpec as P

D = 3072
H = 12
HS = 128
HD = 1536
F, R, C = 4, 8, 4
AXES = ("frame", "row", "col")
STEP = 4
BIG = 1e30
TILE = 768
VMEM = 56 * 1024 * 1024


def index(f, r, c):
    return ((f % F) * R + (r % R)) * C + (c % C)


def every():
    return [(f, r, c) for f in range(F) for r in range(R) for c in range(C)]


def window_pairs(half, dr, dc, back=False):
    pairs = []
    for f, r, c in every():
        step = 1 if (f + half) % 2 == 0 else -1
        here, there = index(f, r, c), index(f, r + step * dr, c + step * dc)
        pairs.append((there, here) if back else (here, there))
    return pairs


def frame_pairs(step):
    return [(index(f, r, c), index(f + step, r, c)) for f, r, c in every() if 0 <= f + step < F]


def core_pairs():
    return [(index(f, r, c), index(f ^ 1, r, c)) for f, r, c in every()]


def shift_pairs(dx=0, dy=0, dz=0, opposed=False):
    pairs = []
    for f, r, c in every():
        (zhi, core), (zlo, x) = divmod(f, 2), divmod(r, 4)
        way = -1 if opposed and core else 1
        z = (2 * zhi + zlo + way * dz) % 4
        pairs.append((index(f, r, c), index((z // 2) * 2 + core, (z % 2) * 4 + (x + way * dx) % 4, c + way * dy)))
    return pairs


def send(value, pairs):
    return lax.ppermute(value, AXES, pairs)


MOVES = ((0, 0), (1, 0), (0, 1), (1, 1))


def sign_of(half, frame):
    return lax.rem(frame + half, 2)


def relay(moves, sems):
    inward = [pltpu.make_async_copy(src, held, sems.at[0, n]) for n, (src, held, _) in enumerate(moves)]
    outward = [pltpu.make_async_copy(held, dst, sems.at[1, n]) for n, (_, held, dst) in enumerate(moves)]
    for copy in inward:
        copy.start()
    for arrives, leaves in zip(inward, outward):
        arrives.wait()
        leaves.start()
    for copy in outward:
        copy.wait()


def pack_kernel(parts, meta, k_ref, v_ref, q_ref, *rest):
    outs, held, sems = rest[: len(parts)], rest[-2], rest[-1]
    moves = []
    for out, (half, piece, names) in zip(outs, parts):
        s = sign_of(half, meta[0])
        a, b = MOVES[piece]
        i = s + a * (1 - 2 * s)
        j = s + b * (1 - 2 * s)
        for n, name in enumerate(names):
            src = {"k": k_ref, "v": v_ref, "q": q_ref}[name]
            moves.append((src.at[pl.ds(2 * half, 2), i, :, j], held.at[len(moves)], out.at[n]))
    relay(moves, sems)


def pack(parts, meta, k, v, q):
    any_spec = pl.BlockSpec(memory_space=pl.ANY)
    count = sum(len(names) for _, _, names in parts)
    outs = pl.pallas_call(
        functools.partial(pack_kernel, parts),
        out_shape=[jax.ShapeDtypeStruct((len(names), 2, 8, 8, HD), jnp.bfloat16) for _, _, names in parts],
        in_specs=[pl.BlockSpec(memory_space=pltpu.SMEM)] + [any_spec] * 3,
        out_specs=[any_spec] * len(parts),
        scratch_shapes=[pltpu.VMEM((count, 2, 8, 8, HD), jnp.bfloat16), pltpu.SemaphoreType.DMA((2, count))],
        compiler_params=pltpu.CompilerParams(vmem_limit_bytes=VMEM),
        cost_estimate=pl.CostEstimate(flops=0, bytes_accessed=count * 2**20, transcendentals=0),
        name="pack",
    )(meta, k, v, q)
    return [o.reshape(-1, 128, HD) for o in outs]


def features(half, meta, kaug, qaug, alive):
    f, r, c, live_rows = (meta[n] for n in range(4))
    s = sign_of(half, f)
    stay = 2 * r + s
    moved = lax.rem(stay + 2 * s + 15, 16)
    row_split = r == s * (R - 1)
    col_split = c == s * (C - 1)
    missing = f == half * (F - 1)

    def places(count):
        token = lax.broadcasted_iota(jnp.int32, (count, HS), 0)
        lane = lax.broadcasted_iota(jnp.int32, (count, HS), 1)
        piece = (token // 128) % 4
        row = jnp.where(piece % 2 == 1, moved, stay) * 8 + (token // 8) % 8
        return token, lane, piece, row < live_rows

    token, lane, piece, live = places(1024)
    dead = (lane == 4) & jnp.logical_not(live)
    on = (lane == piece) | dead | ((lane == 5) & (token >= 512))
    kaug[:, HS:] = jnp.where(on, 1.0, 0.0).astype(jnp.bfloat16)
    token, lane, piece, live = places(512)
    rows_apart = (lane % 2 != piece % 2) & row_split
    cols_apart = (lane // 2 != piece // 2) & col_split
    off = ((lane < 4) & (rows_apart | cols_apart)) | (lane == 4) | ((lane == 5) & missing)
    qaug[:, HS:] = jnp.where(off, -BIG, 0.0).astype(jnp.bfloat16)
    alive[...] = jnp.where(live, 1.0, 0.0)


def attend_kernel(half, meta, skv, sq, x, y, d, h3, hd, o0, o1, o2, o3, kaug, vaug, qaug, alive):
    outs = (o0, o1, o2, o3)

    @pl.when(pl.program_id(0) == 0)
    def _():
        features(half, meta, kaug.at[0], qaug.at[0], alive)
        for n in range(1, STEP):
            kaug[n, :, HS:] = kaug[0, :, HS:]
            qaug[n, :, HS:] = qaug[0, :, HS:]
        vaug[:, :, HS:] = jnp.ones((STEP, 1024, HS), jnp.bfloat16)

    keys = (skv, x, y, d, h3.at[0], h3.at[1], h3.at[2], hd)
    asks = (sq.at[0], x.at[2], y.at[2], d.at[2])
    for h in range(STEP):
        lanes = pl.ds(h * HS, HS)
        for n, ref in enumerate(keys):
            kaug[h, pl.ds(n * 128, 128), :HS] = ref[0, :, lanes]
            vaug[h, pl.ds(n * 128, 128), :HS] = ref[1, :, lanes]
        for n, ref in enumerate(asks):
            qaug[h, pl.ds(n * 128, 128), :HS] = ref[:, lanes]
    scale = math.log2(math.e) / math.sqrt(HS)

    def score(at):
        h, part = divmod(at, 2)
        return lax.dot_general(
            qaug[h, pl.ds(part * 256, 256), :], kaug[h], (((1,), (1,)), ((), ())), preferred_element_type=jnp.float32
        )

    scores = score(0)
    for at in range(2 * STEP):
        later = score(at + 1) if at + 1 < 2 * STEP else None
        h, part = divmod(at, 2)
        lanes = pl.ds(h * HS, HS)
        top = jnp.max(scores, axis=1, keepdims=True)
        weights = jnp.exp2((scores - top) * scale).astype(jnp.bfloat16)
        mixed = jnp.dot(weights, vaug[h], preferred_element_type=jnp.float32)
        result = (mixed[:, :HS] / mixed[:, HS:] * alive[pl.ds(part * 256, 256), :]).astype(jnp.bfloat16)
        outs[2 * part][:, lanes] = result[:128]
        outs[2 * part + 1][:, lanes] = result[128:]
        scores = later


def attend(half, meta, *pieces):
    width = STEP * HS

    def spec(piece):
        lead = piece.shape[:-1]
        return pl.BlockSpec((*lead, width), lambda h: (0,) * len(lead) + (h,))

    return pl.pallas_call(
        functools.partial(attend_kernel, half),
        grid=(H // STEP,),
        out_shape=[jax.ShapeDtypeStruct((128, HD), jnp.bfloat16)] * 4,
        in_specs=[pl.BlockSpec(memory_space=pltpu.SMEM)] + [spec(piece) for piece in pieces],
        out_specs=[pl.BlockSpec((128, width), lambda h: (0, h))] * 4,
        scratch_shapes=[
            pltpu.VMEM((STEP, 1024, 2 * HS), jnp.bfloat16),
            pltpu.VMEM((STEP, 1024, 2 * HS), jnp.bfloat16),
            pltpu.VMEM((STEP, 512, 2 * HS), jnp.bfloat16),
            pltpu.VMEM((512, HS), jnp.float32),
        ],
        compiler_params=pltpu.CompilerParams(vmem_limit_bytes=VMEM),
        cost_estimate=pl.CostEstimate(flops=H * 4 * 512 * 1024 * 256, bytes_accessed=10 * 2**20, transcendentals=H * 2**19),
        name="attend",
    )(meta, *pieces)


def project_kernel(half, meta, places, *refs):
    attended, own, other, tokens = refs[:4], refs[4:8], refs[8:12], refs[12]
    out, lhs, held, sems = refs[-4:]
    step = pl.program_id(0)
    core, x = lax.rem(meta[0], 2), lax.rem(meta[1], 4)

    def fetch(n):
        side, zhi = divmod(n, 2)
        k = core if side == 0 else 1 - core
        copies = []
        for turn, src in enumerate(other if side else own):
            at = lax.rem(x + turn * (2 * k - 1) + 4, 4)
            for zlo in range(2):
                to = pl.ds(pl.multiple_of(zlo * 384 + at * 96, 32), 96)
                copies.append(
                    pltpu.make_async_copy(
                        src.at[pl.ds((2 * zhi + zlo) * 96, 96)], held.at[n, to], sems.at[n, 2 * turn + zlo]
                    )
                )
        return copies

    @pl.when(step == 0)
    def _():
        for n in range(4):
            for copy in fetch(n):
                copy.start()
        s = sign_of(half, meta[0])
        for piece, (a, b) in enumerate(MOVES):
            i = s + a * (1 - 2 * s)
            j = s + b * (1 - 2 * s)
            lhs[i * 2 + j] = attended[piece][...]

    for n in range(4):

        @pl.when(step == n)
        def _():
            for copy in fetch(n):
                copy.wait()

    total = lax.dot_general(
        lhs[...].reshape(512, HD), held[step], (((1,), (1,)), ((), ())), preferred_element_type=jnp.float32
    ).reshape(2, 2, 2, 8, 8, TILE)
    for i in range(2):
        block = jnp.concatenate([total[i, 0], total[i, 1]], axis=2)
        at = (slice(0, 2), slice(8 * i, 8 * i + 8))
        out[at] = (block + tokens[at].astype(jnp.float32)).astype(jnp.bfloat16)


def project(half, attended, meta, places, chunks, tokens, partial=None):
    extra = [] if partial is None else [partial]
    block = pl.BlockSpec((2, 16, 16, TILE), lambda t, m, p: (half, 0, 0, p[t]))
    grid_spec = pltpu.PrefetchScalarGridSpec(
        num_scalar_prefetch=2,
        grid=(D // TILE,),
        in_specs=[pl.BlockSpec((128, HD), lambda t, m, p: (0, 0))] * 4
        + [pl.BlockSpec(memory_space=pl.ANY)] * 8
        + [block]
        + [pl.BlockSpec(memory_space=pl.ANY)] * len(extra),
        out_specs=block,
        scratch_shapes=[
            pltpu.VMEM((4, 128, HD), jnp.bfloat16),
            pltpu.VMEM((4, TILE, HD), jnp.bfloat16),
            pltpu.SemaphoreType.DMA((4, 8)),
        ],
    )
    return pl.pallas_call(
        functools.partial(project_kernel, half),
        grid_spec=grid_spec,
        out_shape=jax.ShapeDtypeStruct((4, 16, 16, D), jnp.bfloat16),
        input_output_aliases={} if partial is None else {15: 0},
        compiler_params=pltpu.CompilerParams(vmem_limit_bytes=VMEM),
        cost_estimate=pl.CostEstimate(flops=1024 * HD * D, bytes_accessed=17 * 2**20, transcendentals=0),
        name="project",
    )(meta, places, *attended, *chunks, tokens, *extra)


def ring_order(own, first, second, third, place):
    row = jnp.stack([third, second, first, own, third, second, first])
    return lax.dynamic_slice_in_dim(row, 3 - place, 4, axis=0)


def together(*values):
    return lax.optimization_barrier(values)


def local(tokens_in, queries, key_rows, value_rows, out_weight, row_valid):
    f, r, c = (lax.axis_index(a) for a in AXES)
    frame = f.astype(jnp.int32).reshape(1)
    meta = jnp.stack([f, r, c, jnp.sum(row_valid)]).astype(jnp.int32)
    core = f & 1
    places = jnp.stack([core, 2 + core, 1 - core, 3 - core]).astype(jnp.int32)
    split = lambda a: a.reshape(4, 2, 8, 2, 8, HD)
    arrays = (split(key_rows), split(value_rows), split(queries))
    shard = out_weight.T

    row, col, both = MOVES[1:]
    go = lambda value, half, move: send(value, window_pairs(half, *move))
    up = lambda value: send(value, frame_pairs(1))
    down = lambda value: send(value, frame_pairs(-1))
    swap = lambda value: send(value, core_pairs())
    turn = lambda value, step=1: send(value, shift_pairs(dx=step, opposed=True))
    back = lambda half, mixed: [mixed[0]] + [send(mixed[n], window_pairs(half, *MOVES[n], back=True)) for n in (1, 2, 3)]

    x0, y0 = pack(((0, 1, "kvq"), (0, 2, "kvq")), frame, *arrays)
    x0, y0, frame, shard = together(x0, y0, frame, shard)
    x0, y0 = go(x0, 0, row), go(y0, 0, col)
    shards = [send(shard, shift_pairs(dz=n)) for n in (1, 2, 3)]
    x1, y1 = pack(((1, 1, "kvq"), (1, 2, "kvq")), frame, *arrays)
    x1, y1, frame, *shards = together(x1, y1, frame, *shards)
    x1, y1 = go(x1, 1, row), go(y1, 1, col)
    skv0, skv1, d0, d1, sq0, sq1 = pack(
        ((0, 0, "kv"), (1, 0, "kv"), (0, 3, "kvq"), (1, 3, "kvq"), (0, 0, "q"), (1, 0, "q")), frame, *arrays
    )
    strip = ring_order(shard, *shards, (f >> 1) * 2 + (r >> 2))
    h0, h1 = jnp.stack([skv0, x0[:2], y0[:2]]), jnp.stack([skv1, x1[:2], y1[:2]])
    d0, d1, h0, h1, x0, y0, x1, y1, meta, places, strip = together(d0, d1, h0, h1, x0, y0, x1, y1, meta, places, strip)
    d0, d1, down3, up3 = go(d0, 0, both), go(d1, 1, both), down(h0), up(h1)
    strips = lax.all_gather(strip.reshape(96, HD), "col", axis=0, tiled=True)
    c0 = strips.reshape(4, 4, 24, HD).swapaxes(0, 1).reshape(384, HD)
    c0, d0, d1 = together(c0, d0, d1)
    downd, upd, c1 = down(d0[:2]), up(d1[:2]), turn(c0)
    c0, c1, downd, upd, down3, up3 = together(c0, c1, downd, upd, down3, up3)

    c2, c3, s0, s1 = turn(c1), turn(c0, -1), swap(c0), swap(c1)
    mixed1 = attend(1, meta, skv1, sq1, x1, y1, d1, down3, downd)
    s0, s1, skv0, *mixed1 = together(s0, s1, skv0, *mixed1)
    attended1 = back(1, mixed1)
    mixed0 = attend(0, meta, skv0, sq0, x0, y0, d0, up3, upd)
    c2, c3, *rest = together(c2, c3, *attended1, *mixed0)
    attended1, mixed0 = rest[:4], rest[4:]
    attended0, s2, s3 = back(0, mixed0), swap(c2), swap(c3)
    chunks = (c0, c1, c2, c3, s0, s1, s2, s3)
    out = project(1, attended1, meta, places, chunks, tokens_in)
    return project(0, attended0, meta, places, chunks, tokens_in, out)


def solution(mesh):
    return jax.shard_map(
        local,
        mesh=mesh,
        in_specs=(
            P("frame", "row", "col", None),
            P("frame", "row", "col", None),
            P("frame", "row", "col", None),
            P("frame", "row", "col", None),
            P(None, ("frame", "row", "col")),
            P(),
        ),
        out_specs=P("frame", "row", "col", None),
        check_vma=False,
    )
```

```python
import functools
import math

import jax
import jax.numpy as jnp
from jax import lax
from jax.experimental import pallas as pl
from jax.experimental.pallas import tpu as pltpu
from jax.sharding import PartitionSpec as P

D = 3072
H = 12
HS = 128
HD = 1536
F, R, C = 4, 8, 4
AXES = ("frame", "row", "col")
STEP = 4
BIG = 1e30
TILE = 768
VMEM = 56 * 1024 * 1024


def index(f, r, c):
    return ((f % F) * R + (r % R)) * C + (c % C)


def every():
    return [(f, r, c) for f in range(F) for r in range(R) for c in range(C)]


def window_pairs(half, dr, dc, back=False):
    pairs = []
    for f, r, c in every():
        step = 1 if (f + half) % 2 == 0 else -1
        here, there = index(f, r, c), index(f, r + step * dr, c + step * dc)
        pairs.append((there, here) if back else (here, there))
    return pairs


def frame_pairs(step):
    return [(index(f, r, c), index(f + step, r, c)) for f, r, c in every() if 0 <= f + step < F]


def core_pairs():
    return [(index(f, r, c), index(f ^ 1, r, c)) for f, r, c in every()]


def shift_pairs(dx=0, dy=0, dz=0, opposed=False):
    pairs = []
    for f, r, c in every():
        (zhi, core), (zlo, x) = divmod(f, 2), divmod(r, 4)
        way = -1 if opposed and core else 1
        z = (2 * zhi + zlo + way * dz) % 4
        pairs.append((index(f, r, c), index((z // 2) * 2 + core, (z % 2) * 4 + (x + way * dx) % 4, c + way * dy)))
    return pairs


def send(value, pairs):
    return lax.ppermute(value, AXES, pairs)


MOVES = ((0, 0), (1, 0), (0, 1), (1, 1))


def sign_of(half, frame):
    return lax.rem(frame + half, 2)


def relay(moves, sems):
    inward = [pltpu.make_async_copy(src, held, sems.at[0, n]) for n, (src, held, _) in enumerate(moves)]
    outward = [pltpu.make_async_copy(held, dst, sems.at[1, n]) for n, (_, held, dst) in enumerate(moves)]
    for copy in inward:
        copy.start()
    for arrives, leaves in zip(inward, outward):
        arrives.wait()
        leaves.start()
    for copy in outward:
        copy.wait()


def pack_kernel(parts, meta, k_ref, v_ref, q_ref, *rest):
    outs, held, sems = rest[: len(parts)], rest[-2], rest[-1]
    moves = []
    for out, (half, piece, names) in zip(outs, parts):
        s = sign_of(half, meta[0])
        a, b = MOVES[piece]
        i = s + a * (1 - 2 * s)
        j = s + b * (1 - 2 * s)
        for n, name in enumerate(names):
            src = {"k": k_ref, "v": v_ref, "q": q_ref}[name]
            moves.append((src.at[pl.ds(2 * half, 2), i, :, j], held.at[len(moves)], out.at[n]))
    relay(moves, sems)


def pack(parts, meta, k, v, q):
    any_spec = pl.BlockSpec(memory_space=pl.ANY)
    count = sum(len(names) for _, _, names in parts)
    outs = pl.pallas_call(
        functools.partial(pack_kernel, parts),
        out_shape=[jax.ShapeDtypeStruct((len(names), 2, 8, 8, HD), jnp.bfloat16) for _, _, names in parts],
        in_specs=[pl.BlockSpec(memory_space=pltpu.SMEM)] + [any_spec] * 3,
        out_specs=[any_spec] * len(parts),
        scratch_shapes=[pltpu.VMEM((count, 2, 8, 8, HD), jnp.bfloat16), pltpu.SemaphoreType.DMA((2, count))],
        compiler_params=pltpu.CompilerParams(vmem_limit_bytes=VMEM),
        cost_estimate=pl.CostEstimate(flops=0, bytes_accessed=count * 2**20, transcendentals=0),
        name="pack",
    )(meta, k, v, q)
    return [o.reshape(-1, 128, HD) for o in outs]


def features(half, meta, kaug, qaug, alive):
    f, r, c, live_rows = (meta[n] for n in range(4))
    s = sign_of(half, f)
    stay = 2 * r + s
    moved = lax.rem(stay + 2 * s + 15, 16)
    row_split = r == s * (R - 1)
    col_split = c == s * (C - 1)
    missing = f == half * (F - 1)

    def places(count):
        token = lax.broadcasted_iota(jnp.int32, (count, HS), 0)
        lane = lax.broadcasted_iota(jnp.int32, (count, HS), 1)
        piece = (token // 128) % 4
        row = jnp.where(piece % 2 == 1, moved, stay) * 8 + (token // 8) % 8
        return token, lane, piece, row < live_rows

    token, lane, piece, live = places(1024)
    dead = (lane == 4) & jnp.logical_not(live)
    on = (lane == piece) | dead | ((lane == 5) & (token >= 512))
    kaug[:, HS:] = jnp.where(on, 1.0, 0.0).astype(jnp.bfloat16)
    token, lane, piece, live = places(512)
    rows_apart = (lane % 2 != piece % 2) & row_split
    cols_apart = (lane // 2 != piece // 2) & col_split
    off = ((lane < 4) & (rows_apart | cols_apart)) | (lane == 4) | ((lane == 5) & missing)
    qaug[:, HS:] = jnp.where(off, -BIG, 0.0).astype(jnp.bfloat16)
    alive[...] = jnp.where(live, 1.0, 0.0)


def attend_kernel(half, meta, skv, sq, x, y, d, h3, hd, o0, o1, o2, o3, kaug, vaug, qaug, alive):
    outs = (o0, o1, o2, o3)

    @pl.when(pl.program_id(0) == 0)
    def _():
        features(half, meta, kaug.at[0], qaug.at[0], alive)
        for n in range(1, STEP):
            kaug[n, :, HS:] = kaug[0, :, HS:]
            qaug[n, :, HS:] = qaug[0, :, HS:]
        vaug[:, :, HS:] = jnp.ones((STEP, 1024, HS), jnp.bfloat16)

    keys = (skv, x, y, d, h3.at[0], h3.at[1], h3.at[2], hd)
    asks = (sq.at[0], x.at[2], y.at[2], d.at[2])
    for h in range(STEP):
        lanes = pl.ds(h * HS, HS)
        for n, ref in enumerate(keys):
            kaug[h, pl.ds(n * 128, 128), :HS] = ref[0, :, lanes]
            vaug[h, pl.ds(n * 128, 128), :HS] = ref[1, :, lanes]
        for n, ref in enumerate(asks):
            qaug[h, pl.ds(n * 128, 128), :HS] = ref[:, lanes]
    scale = math.log2(math.e) / math.sqrt(HS)

    def score(at):
        h, part = divmod(at, 2)
        return lax.dot_general(
            qaug[h, pl.ds(part * 256, 256), :], kaug[h], (((1,), (1,)), ((), ())), preferred_element_type=jnp.float32
        )

    scores = score(0)
    for at in range(2 * STEP):
        later = score(at + 1) if at + 1 < 2 * STEP else None
        h, part = divmod(at, 2)
        lanes = pl.ds(h * HS, HS)
        top = jnp.max(scores, axis=1, keepdims=True)
        weights = jnp.exp2((scores - top) * scale).astype(jnp.bfloat16)
        mixed = jnp.dot(weights, vaug[h], preferred_element_type=jnp.float32)
        result = (mixed[:, :HS] / mixed[:, HS:] * alive[pl.ds(part * 256, 256), :]).astype(jnp.bfloat16)
        outs[2 * part][:, lanes] = result[:128]
        outs[2 * part + 1][:, lanes] = result[128:]
        scores = later


def attend(half, meta, *pieces):
    width = STEP * HS

    def spec(piece):
        lead = piece.shape[:-1]
        return pl.BlockSpec((*lead, width), lambda h: (0,) * len(lead) + (h,))

    return pl.pallas_call(
        functools.partial(attend_kernel, half),
        grid=(H // STEP,),
        out_shape=[jax.ShapeDtypeStruct((128, HD), jnp.bfloat16)] * 4,
        in_specs=[pl.BlockSpec(memory_space=pltpu.SMEM)] + [spec(piece) for piece in pieces],
        out_specs=[pl.BlockSpec((128, width), lambda h: (0, h))] * 4,
        scratch_shapes=[
            pltpu.VMEM((STEP, 1024, 2 * HS), jnp.bfloat16),
            pltpu.VMEM((STEP, 1024, 2 * HS), jnp.bfloat16),
            pltpu.VMEM((STEP, 512, 2 * HS), jnp.bfloat16),
            pltpu.VMEM((512, HS), jnp.float32),
        ],
        compiler_params=pltpu.CompilerParams(vmem_limit_bytes=VMEM),
        cost_estimate=pl.CostEstimate(flops=H * 4 * 512 * 1024 * 256, bytes_accessed=10 * 2**20, transcendentals=H * 2**19),
        name="attend",
    )(meta, *pieces)


def project_kernel(meta, places, *refs):
    attended, own, other, (tokens, out, lhs, held, sems) = refs[:8], refs[8:12], refs[12:16], refs[16:]
    step = pl.program_id(0)
    core, x = lax.rem(meta[0], 2), lax.rem(meta[1], 4)

    def fetch(n):
        side, zhi = divmod(n, 2)
        k = core if side == 0 else 1 - core
        copies = []
        for turn, src in enumerate(other if side else own):
            at = lax.rem(x + turn * (2 * k - 1) + 4, 4)
            for zlo in range(2):
                to = pl.ds(pl.multiple_of(zlo * 384 + at * 96, 32), 96)
                copies.append(
                    pltpu.make_async_copy(
                        src.at[pl.ds((2 * zhi + zlo) * 96, 96)], held.at[n % 2, to], sems.at[n % 2, 2 * turn + zlo]
                    )
                )
        return copies

    @pl.when(step == 0)
    def _():
        for copy in fetch(0):
            copy.start()
        for half in range(2):
            s = sign_of(half, meta[0])
            for piece, (a, b) in enumerate(MOVES):
                i = s + a * (1 - 2 * s)
                j = s + b * (1 - 2 * s)
                lhs[half * 4 + i * 2 + j] = attended[half * 4 + piece][...]

    for n in range(4):

        @pl.when(step == n)
        def _():
            for copy in fetch(n):
                copy.wait()
            if n < 3:
                for copy in fetch(n + 1):
                    copy.start()

    total = lax.dot_general(
        lhs[...].reshape(1024, HD), held[lax.rem(step, 2)], (((1,), (1,)), ((), ())), preferred_element_type=jnp.float32
    ).reshape(2, 2, 2, 2, 8, 8, TILE)
    for half in range(2):
        for i in range(2):
            block = jnp.concatenate([total[half, i, 0], total[half, i, 1]], axis=2)
            at = (slice(2 * half, 2 * half + 2), slice(8 * i, 8 * i + 8))
            out[at] = (block + tokens[at].astype(jnp.float32)).astype(jnp.bfloat16)


def project(attended, meta, places, chunks, tokens):
    grid_spec = pltpu.PrefetchScalarGridSpec(
        num_scalar_prefetch=2,
        grid=(D // TILE,),
        in_specs=[pl.BlockSpec((128, HD), lambda t, m, p: (0, 0))] * 8
        + [pl.BlockSpec(memory_space=pl.ANY)] * 8
        + [pl.BlockSpec((4, 16, 16, TILE), lambda t, m, p: (0, 0, 0, p[t]))],
        out_specs=pl.BlockSpec((4, 16, 16, TILE), lambda t, m, p: (0, 0, 0, p[t])),
        scratch_shapes=[
            pltpu.VMEM((8, 128, HD), jnp.bfloat16),
            pltpu.VMEM((2, TILE, HD), jnp.bfloat16),
            pltpu.SemaphoreType.DMA((2, 8)),
        ],
    )
    return pl.pallas_call(
        project_kernel,
        grid_spec=grid_spec,
        out_shape=jax.ShapeDtypeStruct((4, 16, 16, D), jnp.bfloat16),
        compiler_params=pltpu.CompilerParams(vmem_limit_bytes=VMEM),
        cost_estimate=pl.CostEstimate(flops=2 * 1024 * HD * D, bytes_accessed=25 * 2**20, transcendentals=0),
        name="project",
    )(meta, places, *attended, *chunks, tokens)


def ring_order(own, first, second, third, place):
    row = jnp.stack([third, second, first, own, third, second, first])
    return lax.dynamic_slice_in_dim(row, 3 - place, 4, axis=0)


def together(*values):
    return lax.optimization_barrier(values)


def local(tokens_in, queries, key_rows, value_rows, out_weight, row_valid):
    f, r, c = (lax.axis_index(a) for a in AXES)
    frame = f.astype(jnp.int32).reshape(1)
    meta = jnp.stack([f, r, c, jnp.sum(row_valid)]).astype(jnp.int32)
    core = f & 1
    places = jnp.stack([core, 2 + core, 1 - core, 3 - core]).astype(jnp.int32)
    split = lambda a: a.reshape(4, 2, 8, 2, 8, HD)
    arrays = (split(key_rows), split(value_rows), split(queries))
    shard = out_weight.T

    row, col, both = MOVES[1:]
    go = lambda value, half, move: send(value, window_pairs(half, *move))
    up = lambda value: send(value, frame_pairs(1))
    down = lambda value: send(value, frame_pairs(-1))
    swap = lambda value: send(value, core_pairs())
    turn = lambda value, step=1: send(value, shift_pairs(dx=step, opposed=True))
    back = lambda half, mixed: [mixed[0]] + [send(mixed[n], window_pairs(half, *MOVES[n], back=True)) for n in (1, 2, 3)]

    x0, y0 = pack(((0, 1, "kvq"), (0, 2, "kvq")), frame, *arrays)
    x0, y0, frame, shard = together(x0, y0, frame, shard)
    x0, y0 = go(x0, 0, row), go(y0, 0, col)
    shards = [send(shard, shift_pairs(dz=n)) for n in (1, 2, 3)]
    x1, y1 = pack(((1, 1, "kvq"), (1, 2, "kvq")), frame, *arrays)
    x1, y1, frame, *shards = together(x1, y1, frame, *shards)
    x1, y1 = go(x1, 1, row), go(y1, 1, col)
    skv0, skv1, d0, d1, sq0, sq1 = pack(
        ((0, 0, "kv"), (1, 0, "kv"), (0, 3, "kvq"), (1, 3, "kvq"), (0, 0, "q"), (1, 0, "q")), frame, *arrays
    )
    strip = ring_order(shard, *shards, (f >> 1) * 2 + (r >> 2))
    h0, h1 = jnp.stack([skv0, x0[:2], y0[:2]]), jnp.stack([skv1, x1[:2], y1[:2]])
    d0, d1, h0, h1, x0, y0, x1, y1, meta, places, strip = together(d0, d1, h0, h1, x0, y0, x1, y1, meta, places, strip)
    d0, d1, down3, up3 = go(d0, 0, both), go(d1, 1, both), down(h0), up(h1)
    strips = lax.all_gather(strip.reshape(96, HD), "col", axis=0, tiled=True)
    c0 = strips.reshape(4, 4, 24, HD).swapaxes(0, 1).reshape(384, HD)
    downd, upd = down(d0[:2]), up(d1[:2])
    c0, down3, up3, downd, upd = together(c0, down3, up3, downd, upd)

    c1, s0 = turn(c0), swap(c0)
    mixed1 = attend(1, meta, skv1, sq1, x1, y1, d1, down3, downd)
    c0, c1, s0, skv0, *mixed1 = together(c0, c1, s0, skv0, *mixed1)
    c2, c3, attended1 = turn(c1), turn(c0, -1), back(1, mixed1)
    mixed0 = attend(0, meta, skv0, sq0, x0, y0, d0, up3, upd)
    rest = list(together(*attended1, *mixed0))
    attended1, mixed0 = rest[:4], rest[4:]
    attended0 = back(0, mixed0)
    c1, c2, c3, *attended0 = together(c1, c2, c3, *attended0)
    chunks = (c0, c1, c2, c3, s0, swap(c1), swap(c2), swap(c3))
    return project(attended0 + attended1, meta, places, chunks, tokens_in)


def solution(mesh):
    return jax.shard_map(
        local,
        mesh=mesh,
        in_specs=(
            P("frame", "row", "col", None),
            P("frame", "row", "col", None),
            P("frame", "row", "col", None),
            P("frame", "row", "col", None),
            P(None, ("frame", "row", "col")),
            P(),
        ),
        out_specs=P("frame", "row", "col", None),
        check_vma=False,
    )
```

```python
import functools
import math

import jax
import jax.numpy as jnp
from jax import lax
from jax.experimental import pallas as pl
from jax.experimental.pallas import tpu as pltpu
from jax.sharding import PartitionSpec as P

D = 3072
H = 12
HS = 128
HD = 1536
F, R, C = 4, 8, 4
AXES = ("frame", "row", "col")
STEP = 4
BIG = 1e30
TILE = 768
VMEM = 56 * 1024 * 1024


def index(f, r, c):
    return ((f % F) * R + (r % R)) * C + (c % C)


def every():
    return [(f, r, c) for f in range(F) for r in range(R) for c in range(C)]


def window_pairs(half, dr, dc, back=False):
    pairs = []
    for f, r, c in every():
        step = 1 if (f + half) % 2 == 0 else -1
        here, there = index(f, r, c), index(f, r + step * dr, c + step * dc)
        pairs.append((there, here) if back else (here, there))
    return pairs


def frame_pairs(step):
    return [(index(f, r, c), index(f + step, r, c)) for f, r, c in every() if 0 <= f + step < F]


def core_pairs():
    return [(index(f, r, c), index(f ^ 1, r, c)) for f, r, c in every()]


def shift_pairs(dx=0, dy=0, dz=0, opposed=False):
    pairs = []
    for f, r, c in every():
        (zhi, core), (zlo, x) = divmod(f, 2), divmod(r, 4)
        way = -1 if opposed and core else 1
        z = (2 * zhi + zlo + way * dz) % 4
        pairs.append((index(f, r, c), index((z // 2) * 2 + core, (z % 2) * 4 + (x + way * dx) % 4, c + way * dy)))
    return pairs


def send(value, pairs):
    return lax.ppermute(value, AXES, pairs)


MOVES = ((0, 0), (1, 0), (0, 1), (1, 1))


def sign_of(half, frame):
    return lax.rem(frame + half, 2)


def relay(moves, sems):
    inward = [pltpu.make_async_copy(src, held, sems.at[0, n]) for n, (src, held, _) in enumerate(moves)]
    outward = [pltpu.make_async_copy(held, dst, sems.at[1, n]) for n, (_, held, dst) in enumerate(moves)]
    for copy in inward:
        copy.start()
    for arrives, leaves in zip(inward, outward):
        arrives.wait()
        leaves.start()
    for copy in outward:
        copy.wait()


def pack_kernel(parts, meta, k_ref, v_ref, q_ref, *rest):
    outs, held, sems = rest[: len(parts)], rest[-2], rest[-1]
    moves = []
    for out, (half, piece, names) in zip(outs, parts):
        s = sign_of(half, meta[0])
        a, b = MOVES[piece]
        i = s + a * (1 - 2 * s)
        j = s + b * (1 - 2 * s)
        for n, name in enumerate(names):
            src = {"k": k_ref, "v": v_ref, "q": q_ref}[name]
            moves.append((src.at[pl.ds(2 * half, 2), i, :, j], held.at[len(moves)], out.at[n]))
    relay(moves, sems)


def pack(parts, meta, k, v, q):
    any_spec = pl.BlockSpec(memory_space=pl.ANY)
    count = sum(len(names) for _, _, names in parts)
    outs = pl.pallas_call(
        functools.partial(pack_kernel, parts),
        out_shape=[jax.ShapeDtypeStruct((len(names), 2, 8, 8, HD), jnp.bfloat16) for _, _, names in parts],
        in_specs=[pl.BlockSpec(memory_space=pltpu.SMEM)] + [any_spec] * 3,
        out_specs=[any_spec] * len(parts),
        scratch_shapes=[pltpu.VMEM((count, 2, 8, 8, HD), jnp.bfloat16), pltpu.SemaphoreType.DMA((2, count))],
        compiler_params=pltpu.CompilerParams(vmem_limit_bytes=VMEM),
        cost_estimate=pl.CostEstimate(flops=0, bytes_accessed=count * 2**20, transcendentals=0),
        name="pack",
    )(meta, k, v, q)
    return [o.reshape(-1, 128, HD) for o in outs]


def features(half, meta, kaug, qaug, alive):
    f, r, c, live_rows = (meta[n] for n in range(4))
    s = sign_of(half, f)
    stay = 2 * r + s
    moved = lax.rem(stay + 2 * s + 15, 16)
    row_split = r == s * (R - 1)
    col_split = c == s * (C - 1)
    missing = f == half * (F - 1)

    def places(count):
        token = lax.broadcasted_iota(jnp.int32, (count, HS), 0)
        lane = lax.broadcasted_iota(jnp.int32, (count, HS), 1)
        piece = (token // 128) % 4
        row = jnp.where(piece % 2 == 1, moved, stay) * 8 + (token // 8) % 8
        return token, lane, piece, row < live_rows

    token, lane, piece, live = places(1024)
    dead = (lane == 4) & jnp.logical_not(live)
    on = (lane == piece) | dead | ((lane == 5) & (token >= 512))
    kaug[:, HS:] = jnp.where(on, 1.0, 0.0).astype(jnp.bfloat16)
    token, lane, piece, live = places(512)
    rows_apart = (lane % 2 != piece % 2) & row_split
    cols_apart = (lane // 2 != piece // 2) & col_split
    off = ((lane < 4) & (rows_apart | cols_apart)) | (lane == 4) | ((lane == 5) & missing)
    qaug[:, HS:] = jnp.where(off, -BIG, 0.0).astype(jnp.bfloat16)
    alive[...] = jnp.where(live, 1.0, 0.0)


def attend_kernel(half, meta, skv, sq, x, y, d, h3, hd, o0, o1, o2, o3, kaug, vaug, qaug, alive):
    outs = (o0, o1, o2, o3)

    @pl.when(pl.program_id(0) == 0)
    def _():
        features(half, meta, kaug.at[0], qaug.at[0], alive)
        for n in range(1, STEP):
            kaug[n, :, HS:] = kaug[0, :, HS:]
            qaug[n, :, HS:] = qaug[0, :, HS:]
        vaug[:, :, HS:] = jnp.ones((STEP, 1024, HS), jnp.bfloat16)

    keys = (skv, x, y, d, h3.at[0], h3.at[1], h3.at[2], hd)
    asks = (sq.at[0], x.at[2], y.at[2], d.at[2])
    for h in range(STEP):
        lanes = pl.ds(h * HS, HS)
        for n, ref in enumerate(keys):
            kaug[h, pl.ds(n * 128, 128), :HS] = ref[0, :, lanes]
            vaug[h, pl.ds(n * 128, 128), :HS] = ref[1, :, lanes]
        for n, ref in enumerate(asks):
            qaug[h, pl.ds(n * 128, 128), :HS] = ref[:, lanes]
    scale = math.log2(math.e) / math.sqrt(HS)

    def score(at):
        h, part = divmod(at, 2)
        return lax.dot_general(
            qaug[h, pl.ds(part * 256, 256), :], kaug[h], (((1,), (1,)), ((), ())), preferred_element_type=jnp.float32
        )

    scores = score(0)
    for at in range(2 * STEP):
        later = score(at + 1) if at + 1 < 2 * STEP else None
        h, part = divmod(at, 2)
        lanes = pl.ds(h * HS, HS)
        top = jnp.max(scores, axis=1, keepdims=True)
        weights = jnp.exp2((scores - top) * scale).astype(jnp.bfloat16)
        mixed = jnp.dot(weights, vaug[h], preferred_element_type=jnp.float32)
        result = (mixed[:, :HS] / mixed[:, HS:] * alive[pl.ds(part * 256, 256), :]).astype(jnp.bfloat16)
        outs[2 * part][:, lanes] = result[:128]
        outs[2 * part + 1][:, lanes] = result[128:]
        scores = later


def attend(half, meta, *pieces):
    width = STEP * HS

    def spec(piece):
        lead = piece.shape[:-1]
        return pl.BlockSpec((*lead, width), lambda h: (0,) * len(lead) + (h,))

    return pl.pallas_call(
        functools.partial(attend_kernel, half),
        grid=(H // STEP,),
        out_shape=[jax.ShapeDtypeStruct((128, HD), jnp.bfloat16)] * 4,
        in_specs=[pl.BlockSpec(memory_space=pltpu.SMEM)] + [spec(piece) for piece in pieces],
        out_specs=[pl.BlockSpec((128, width), lambda h: (0, h))] * 4,
        scratch_shapes=[
            pltpu.VMEM((STEP, 1024, 2 * HS), jnp.bfloat16),
            pltpu.VMEM((STEP, 1024, 2 * HS), jnp.bfloat16),
            pltpu.VMEM((STEP, 512, 2 * HS), jnp.bfloat16),
            pltpu.VMEM((512, HS), jnp.float32),
        ],
        compiler_params=pltpu.CompilerParams(vmem_limit_bytes=VMEM),
        cost_estimate=pl.CostEstimate(flops=H * 4 * 512 * 1024 * 256, bytes_accessed=10 * 2**20, transcendentals=H * 2**19),
        name="attend",
    )(meta, *pieces)


def project_kernel(half, meta, places, *refs):
    attended, own, other, tokens = refs[:4], refs[4:8], refs[8:12], refs[12]
    out, lhs, held, sems = refs[-4:]
    step = pl.program_id(0)
    core, x = lax.rem(meta[0], 2), lax.rem(meta[1], 4)

    def fetch(n):
        side, zhi = divmod(n, 2)
        k = core if side == 0 else 1 - core
        copies = []
        for turn, src in enumerate(other if side else own):
            at = lax.rem(x + turn * (2 * k - 1) + 4, 4)
            for zlo in range(2):
                to = pl.ds(pl.multiple_of(zlo * 384 + at * 96, 32), 96)
                copies.append(
                    pltpu.make_async_copy(
                        src.at[pl.ds((2 * zhi + zlo) * 96, 96)], held.at[n, to], sems.at[n, 2 * turn + zlo]
                    )
                )
        return copies

    @pl.when(step == 0)
    def _():
        for n in range(4):
            for copy in fetch(n):
                copy.start()
        s = sign_of(half, meta[0])
        for piece, (a, b) in enumerate(MOVES):
            i = s + a * (1 - 2 * s)
            j = s + b * (1 - 2 * s)
            lhs[i * 2 + j] = attended[piece][...]

    for n in range(4):

        @pl.when(step == n)
        def _():
            for copy in fetch(n):
                copy.wait()

    total = lax.dot_general(
        lhs[...].reshape(512, HD), held[step], (((1,), (1,)), ((), ())), preferred_element_type=jnp.float32
    ).reshape(2, 2, 2, 8, 8, TILE)
    for i in range(2):
        block = jnp.concatenate([total[i, 0], total[i, 1]], axis=2)
        at = (slice(0, 2), slice(8 * i, 8 * i + 8))
        out[at] = (block + tokens[at].astype(jnp.float32)).astype(jnp.bfloat16)


def project(half, attended, meta, places, chunks, tokens, partial=None):
    extra = [] if partial is None else [partial]
    block = pl.BlockSpec((2, 16, 16, TILE), lambda t, m, p: (half, 0, 0, p[t]))
    grid_spec = pltpu.PrefetchScalarGridSpec(
        num_scalar_prefetch=2,
        grid=(D // TILE,),
        in_specs=[pl.BlockSpec((128, HD), lambda t, m, p: (0, 0))] * 4
        + [pl.BlockSpec(memory_space=pl.ANY)] * 8
        + [block]
        + [pl.BlockSpec(memory_space=pl.ANY)] * len(extra),
        out_specs=block,
        scratch_shapes=[
            pltpu.VMEM((4, 128, HD), jnp.bfloat16),
            pltpu.VMEM((4, TILE, HD), jnp.bfloat16),
            pltpu.SemaphoreType.DMA((4, 8)),
        ],
    )
    return pl.pallas_call(
        functools.partial(project_kernel, half),
        grid_spec=grid_spec,
        out_shape=jax.ShapeDtypeStruct((4, 16, 16, D), jnp.bfloat16),
        input_output_aliases={} if partial is None else {15: 0},
        compiler_params=pltpu.CompilerParams(vmem_limit_bytes=VMEM),
        cost_estimate=pl.CostEstimate(flops=1024 * HD * D, bytes_accessed=17 * 2**20, transcendentals=0),
        name="project",
    )(meta, places, *attended, *chunks, tokens, *extra)


def flip_pairs(frame_bit, row_bit):
    return [(index(f, r, c), index(f ^ frame_bit, r ^ row_bit, c)) for f, r, c in every()]


def side_by_side(own, other, bit):
    return jnp.where(bit == 0, jnp.stack([own, other]), jnp.stack([other, own]))


def together(*values):
    return lax.optimization_barrier(values)


def local(tokens_in, queries, key_rows, value_rows, out_weight, row_valid):
    f, r, c = (lax.axis_index(a) for a in AXES)
    frame = f.astype(jnp.int32).reshape(1)
    meta = jnp.stack([f, r, c, jnp.sum(row_valid)]).astype(jnp.int32)
    core = f & 1
    places = jnp.stack([core, 2 + core, 1 - core, 3 - core]).astype(jnp.int32)
    split = lambda a: a.reshape(4, 2, 8, 2, 8, HD)
    arrays = (split(key_rows), split(value_rows), split(queries))
    shard = out_weight.T

    row, col, both = MOVES[1:]
    go = lambda value, half, move: send(value, window_pairs(half, *move))
    up = lambda value: send(value, frame_pairs(1))
    down = lambda value: send(value, frame_pairs(-1))
    swap = lambda value: send(value, core_pairs())
    turn = lambda value, step=1: send(value, shift_pairs(dx=step, opposed=True))
    back = lambda half, mixed: [mixed[0]] + [send(mixed[n], window_pairs(half, *MOVES[n], back=True)) for n in (1, 2, 3)]

    x0, y0 = pack(((0, 1, "kvq"), (0, 2, "kvq")), frame, *arrays)
    x0, y0, frame, shard = together(x0, y0, frame, shard)
    x0, y0 = go(x0, 0, row), go(y0, 0, col)
    pair = side_by_side(shard, send(shard, flip_pairs(0, 4)), (r >> 2) & 1)
    rest_of_strip = send(pair, flip_pairs(2, 0))
    x1, y1 = pack(((1, 1, "kvq"), (1, 2, "kvq")), frame, *arrays)
    x1, y1, frame, pair = together(x1, y1, frame, pair)
    x1, y1 = go(x1, 1, row), go(y1, 1, col)
    skv0, skv1, d0, d1, sq0, sq1 = pack(
        ((0, 0, "kv"), (1, 0, "kv"), (0, 3, "kvq"), (1, 3, "kvq"), (0, 0, "q"), (1, 0, "q")), frame, *arrays
    )
    strip = side_by_side(pair, rest_of_strip, (f >> 1) & 1)
    h0, h1 = jnp.stack([skv0, x0[:2], y0[:2]]), jnp.stack([skv1, x1[:2], y1[:2]])
    d0, d1, h0, h1, x0, y0, x1, y1, meta, places, strip = together(d0, d1, h0, h1, x0, y0, x1, y1, meta, places, strip)
    d0, d1, down3, up3 = go(d0, 0, both), go(d1, 1, both), down(h0), up(h1)
    strips = lax.all_gather(strip.reshape(96, HD), "col", axis=0, tiled=True)
    c0 = strips.reshape(4, 4, 24, HD).swapaxes(0, 1).reshape(384, HD)
    c0, d0, d1 = together(c0, d0, d1)
    downd, upd, c1 = down(d0[:2]), up(d1[:2]), turn(c0)
    c0, c1, downd, upd, down3, up3 = together(c0, c1, downd, upd, down3, up3)

    c2, c3, s0, s1 = turn(c1), turn(c0, -1), swap(c0), swap(c1)
    mixed1 = attend(1, meta, skv1, sq1, x1, y1, d1, down3, downd)
    s0, s1, skv0, *mixed1 = together(s0, s1, skv0, *mixed1)
    attended1 = back(1, mixed1)
    mixed0 = attend(0, meta, skv0, sq0, x0, y0, d0, up3, upd)
    c2, c3, *rest = together(c2, c3, *attended1, *mixed0)
    attended1, mixed0 = rest[:4], rest[4:]
    attended0, s2, s3 = back(0, mixed0), swap(c2), swap(c3)
    chunks = (c0, c1, c2, c3, s0, s1, s2, s3)
    out = project(1, attended1, meta, places, chunks, tokens_in)
    return project(0, attended0, meta, places, chunks, tokens_in, out)


def solution(mesh):
    return jax.shard_map(
        local,
        mesh=mesh,
        in_specs=(
            P("frame", "row", "col", None),
            P("frame", "row", "col", None),
            P("frame", "row", "col", None),
            P("frame", "row", "col", None),
            P(None, ("frame", "row", "col")),
            P(),
        ),
        out_specs=P("frame", "row", "col", None),
        check_vma=False,
    )
```
